32 devices in a mesh: fsdp: 32 (over z, y, x, core), tp: 1.
Axes of the slice: x: 2, y: 2, z: 4, core: 2. Of those that a mesh axis runs over, the one named last changes fastest.
Arguments:
- gate_pre: bfloat16 [4096, 14336], P('fsdp', 'tp'), may hold values from -6 to 6
- up_pre: bfloat16 [4096, 14336], P('fsdp', 'tp'), may hold values from -6 to 6
- down_weight: bfloat16 [14336, 4096], P('tp', 'fsdp'), may hold values from -0.046875 to 0.046875
Outputs:
- mixed: bfloat16 [4096, 4096], P('fsdp', 'tp')
The draws below stay inside these ranges and needn't reach their ends.
All inputs are finite; a program needn't handle non-finite values.
Results may differ from the reference program's by a relative error of at most 0.0049.
Values may be sent and summed in bfloat16 or wider, within the bound.
No kernel may reach another device: no remote copies, remote signals or barrier semaphores. Data moves between devices by JAX's collectives and lax.ppermute only.
A program may use at most 192 MiB of HBM per device.

```python
import jax
import jax.numpy as jnp

D = 4096
FF = 14336
TOKENS = 4096


def shard_levels(key, dims, split, least, largest):
    factor_of, own = 1.0, jax.random.fold_in(key, 6)
    for axis_at, shards_of in split:
        steps = jnp.exp(jax.random.uniform(jax.random.fold_in(own, axis_at), (shards_of,), jnp.float32, least / len(split), largest / len(split)))
        factor_of = factor_of * jnp.repeat(steps, dims[axis_at] // shards_of).reshape([-1 if axis == axis_at else 1 for axis in range(len(dims))])
    return factor_of


def normal_values(stream_key, dims, width, reach, pieces=(), dtype=jnp.bfloat16):
    values = width * jax.random.normal(stream_key, dims, jnp.float32)
    if pieces:
        values = values * shard_levels(stream_key, dims, pieces, -0.22, 0.18)
    return jnp.clip(values, -reach, reach).astype(dtype)


def setup_inputs(seed: int = 0) -> dict:
    splits = jax.random.split(jax.random.key(seed), 4)
    gate_pre = normal_values(splits[0], (TOKENS, FF), 1.0, 6.0, ((0, 32),))
    up_pre = normal_values(splits[1], (TOKENS, FF), 1.0, 6.0, ((0, 32),))
    down_weight = normal_values(splits[2], (FF, D), FF ** -0.5, 0.046875, ((1, 32),))
    return dict(gate_pre=gate_pre, up_pre=up_pre, down_weight=down_weight)


def reference(gate_pre, up_pre, down_weight):
    hidden = (jax.nn.silu(gate_pre.astype(jnp.float32)) * up_pre.astype(jnp.float32)).astype(jnp.bfloat16)
    return jnp.dot(hidden, down_weight, preferred_element_type=jnp.float32).astype(jnp.bfloat16)
```

```python
import functools

import jax
import jax.numpy as jnp
from jax import lax
from jax.experimental import pallas as pl
from jax.experimental.pallas import tpu as pltpu
from jax.sharding import PartitionSpec as P

CORE, PLANE, PAIR = 1, 2, 8
LIMIT = 48 * 1024 * 1024


def flip(n, mask):
    return [(source, source ^ mask) for source in range(n)]


def along_z(n, pairs):
    low = PAIR
    return [(a * low + rest, b * low + rest) for a, b in pairs for rest in range(low)]


def silu_product(gate, up):
    return (jax.nn.silu(gate.astype(jnp.float32)) * up.astype(jnp.float32)).astype(jnp.bfloat16)


def product_kernel(choices, mid_ref, *refs):
    a_refs, refs = refs[:16], refs[16:]
    w_refs, refs = refs[: 4 * choices], refs[4 * choices :]
    outs, (a, w, a_sem, w_sem) = refs[:4], refs[4:]
    rows = a_refs[0].shape[0]
    columns = w_refs[0].shape[1]

    def w_copy(at, choice):
        return pltpu.make_async_copy(
            w_refs[4 * choice + at], w.at[:, pl.ds(at * columns, columns)], w_sem.at[at]
        )

    def a_copy(at):
        return pltpu.make_async_copy(a_refs[at], a.at[pl.ds(at * rows, rows)], a_sem.at[at])

    for at in range(4):
        if choices == 1:
            w_copy(at, 0).start()
        else:
            for choice in range(choices):

                @pl.when(mid_ref[0] == choice)
                def _():
                    w_copy(at, choice).start()

    for at in range(16):
        a_copy(at).start()
    for at in range(4):
        w_copy(at, 0).wait()
    order = (3, 1, 2, 0)
    for to in order:
        for half in range(2):
            at = 4 * to + 2 * half
            a_copy(at).wait()
            a_copy(at + 1).wait()
            total = jnp.dot(
                a[pl.ds(at * rows, 2 * rows)], w[...], preferred_element_type=jnp.float32
            )
            outs[to][2 * half] = total[:rows].astype(outs[to].dtype)
            outs[to][2 * half + 1] = total[rows:].astype(outs[to].dtype)


def product(mid, a_blocks, w_choices):
    rows, depth = a_blocks[0].shape
    columns = w_choices[0][0].shape[1]
    w_blocks = [block for choice in w_choices for block in choice]
    shape = (4, rows, 4 * columns)
    return pl.pallas_call(
        functools.partial(product_kernel, len(w_choices)),
        out_shape=[jax.ShapeDtypeStruct(shape, jnp.float32)]
        + [jax.ShapeDtypeStruct(shape, jnp.bfloat16)] * 3,
        in_specs=[pl.BlockSpec(memory_space=pltpu.SMEM)]
        + [pl.BlockSpec(memory_space=pl.ANY)] * (16 + len(w_blocks)),
        out_specs=[pl.BlockSpec(memory_space=pltpu.VMEM)] * 4,
        scratch_shapes=[
            pltpu.VMEM((16 * rows, depth), jnp.bfloat16),
            pltpu.VMEM((depth, 4 * columns), jnp.bfloat16),
            pltpu.SemaphoreType.DMA((16,)),
            pltpu.SemaphoreType.DMA((4,)),
        ],
        compiler_params=pltpu.CompilerParams(vmem_limit_bytes=LIMIT),
        cost_estimate=pl.CostEstimate(
            flops=2 * 16 * rows * depth * 4 * columns,
            bytes_accessed=2 * depth * (16 * rows + 4 * columns),
            transcendentals=0,
        ),
        name="product",
    )(mid, *a_blocks, *w_blocks)


def add_kernel(own, one, two, three, *outs):
    columns = own.shape[2] // 4
    for piece in range(4):
        for at in range(4):
            here = pl.ds(at * columns, columns)
            total = own[piece, :, here]
            for step, ref in ((1, one), (2, two), (3, three)):
                total += ref[piece, :, pl.ds((at ^ step) * columns, columns)].astype(jnp.float32)
            outs[piece][:, here] = total.astype(jnp.bfloat16)


def add(own, others):
    _, rows, columns = own.shape
    return pl.pallas_call(
        add_kernel,
        out_shape=[jax.ShapeDtypeStruct((rows, columns), jnp.bfloat16)] * 4,
        in_specs=[pl.BlockSpec(memory_space=pltpu.VMEM)] * 4,
        out_specs=[pl.BlockSpec(memory_space=pltpu.VMEM)] * 4,
        compiler_params=pltpu.CompilerParams(vmem_limit_bytes=LIMIT),
        cost_estimate=pl.CostEstimate(
            flops=12 * rows * columns, bytes_accessed=48 * rows * columns, transcendentals=0
        ),
        name="add",
    )(own, *others)


def assemble_kernel(place_ref, *refs):
    pieces, out = refs[:8], refs[8]
    columns = out.shape[1] // 32
    place = place_ref[0]
    for half in range(2):
        for piece in range(4):
            for at in range(4):
                index = ((piece >> 1) << 4) | (half << 3) | (at << 1) | (piece & 1)
                to = pl.multiple_of((place ^ index) * columns, columns)
                out[:, pl.ds(to, columns)] = pieces[4 * half + piece][:, pl.ds(at * columns, columns)]


def assemble(place, pieces):
    rows, columns = pieces[0].shape
    return pl.pallas_call(
        assemble_kernel,
        out_shape=jax.ShapeDtypeStruct((rows, 8 * columns), jnp.bfloat16),
        in_specs=[pl.BlockSpec(memory_space=pltpu.SMEM)]
        + [pl.BlockSpec(memory_space=pltpu.VMEM)] * 8,
        out_specs=pl.BlockSpec(memory_space=pltpu.VMEM),
        compiler_params=pltpu.CompilerParams(vmem_limit_bytes=LIMIT),
        name="assemble",
    )(place, *pieces)


def blocks(gate_pre, up_pre, down_weight):
    n = lax.axis_size("fsdp")
    me = lax.axis_index("fsdp")
    send = functools.partial(lax.ppermute, axis_name="fsdp")
    depth = gate_pre.shape[1] // 4
    plane = (me // PLANE) % 4
    z_low, z_high = (me // PAIR) % 2, me // (2 * PAIR)

    a, w = [None] * 4, [None] * 4
    for step in range(4):
        start = (plane ^ step) * depth
        hidden = silu_product(
            lax.dynamic_slice_in_dim(gate_pre, start, depth, 1),
            lax.dynamic_slice_in_dim(up_pre, start, depth, 1),
        )
        weight = lax.dynamic_slice_in_dim(down_weight, start, depth, 0)
        if step:
            hidden = send(hidden, perm=flip(n, step * PLANE))
            weight = send(weight, perm=flip(n, step * PLANE))
        a[step], w[step] = hidden, weight

    a_pair = [send(block, perm=flip(n, PAIR)) for block in a]
    w_mid = [send(block, perm=along_z(n, [(1, 2), (2, 1)])) for block in w]
    w_next = [send(block, perm=along_z(n, [(1, 0), (3, 1), (0, 2), (2, 3)])) for block in w]
    a_blocks = []
    for step in range(4):
        for block in (a[step], a_pair[step]):
            a_blocks += [block, send(block, perm=flip(n, CORE))]

    mid = (z_low ^ z_high).astype(jnp.int32).reshape(1)
    pieces = []
    for choices in ([w, w_mid], [w_next]):
        own, *others = product(mid, a_blocks, choices)
        others = [send(other, perm=flip(n, step * PLANE)) for step, other in zip((1, 2, 3), others)]
        summed = add(own, others)
        pieces += [summed[0]] + [
            send(summed[piece], perm=flip(n, (piece >> 1) * PAIR + (piece & 1) * CORE))
            for piece in (1, 2, 3)
        ]
    place = (z_low * 16 + z_high * 8 + plane * 2 + me % 2).astype(jnp.int32).reshape(1)
    return assemble(place, pieces)


def shards(gate_pre, up_pre, down_weight):
    hidden = silu_product(gate_pre, up_pre)
    terms = jnp.dot(
        hidden,
        lax.all_gather(down_weight, "fsdp", axis=1, tiled=True),
        preferred_element_type=jnp.float32,
    )
    totals = lax.psum(terms, "tp")
    share = totals.shape[1] // lax.axis_size("tp")
    result = lax.dynamic_slice_in_dim(totals, lax.axis_index("tp") * share, share, 1)
    return result.astype(jnp.bfloat16)


def solution(mesh):
    in_blocks = mesh.shape["tp"] == 1 and mesh.shape["fsdp"] == 4 * PAIR
    return jax.shard_map(
        blocks if in_blocks else shards,
        mesh=mesh,
        in_specs=(P("fsdp", "tp"), P("fsdp", "tp"), P("tp", "fsdp")),
        out_specs=P("fsdp", "tp"),
        check_vma=False,
    )
```

```python
import functools

import jax
import jax.numpy as jnp
from jax import lax
from jax.experimental import pallas as pl
from jax.experimental.pallas import tpu as pltpu
from jax.sharding import PartitionSpec as P

CORE, PLANE, PAIR = 1, 2, 8
LIMIT = 48 * 1024 * 1024
LANES = 128


def flip(n, mask):
    return [(source, source ^ mask) for source in range(n)]


def along_z(n, pairs):
    low = PAIR
    return [(a * low + rest, b * low + rest) for a, b in pairs for rest in range(low)]


def silu_product(gate, up):
    return (jax.nn.silu(gate.astype(jnp.float32)) * up.astype(jnp.float32)).astype(jnp.bfloat16)


def pack_kernel(apart, plane_ref, gate, up, weight, *refs):
    a, w = refs[-2:] if apart else (refs[-1].at[0], refs[-1].at[1])
    hidden = silu_product(gate[...], up[...])
    for tile in range(a.shape[0]):
        a[tile] = hidden[:, tile * LANES : (tile + 1) * LANES]
        w[tile] = weight[pl.ds(tile * LANES, LANES)]


def pack(plane, step, gate, up, weight, apart, after=()):
    rows, columns = gate.shape[0], weight.shape[1]
    tiles = gate.shape[1] // (4 * LANES)
    steps = 4
    share = tiles // steps
    if apart:
        shape = (tiles, rows, LANES)
        out_shape = [jax.ShapeDtypeStruct(shape, jnp.bfloat16)] * 2
        out_specs = [pl.BlockSpec((share, rows, LANES), lambda at, plane: (at, 0, 0))] * 2
    else:
        shape = (2, tiles, rows, LANES)
        out_shape = jax.ShapeDtypeStruct(shape, jnp.bfloat16)
        out_specs = pl.BlockSpec((2, share, rows, LANES), lambda at, plane: (0, at, 0, 0))

    def here(at, plane):
        return (plane[0] ^ step) * steps + at

    across = pl.BlockSpec((rows, share * LANES), lambda at, plane: (0, here(at, plane)))
    down = pl.BlockSpec((share * LANES, columns), lambda at, plane: (here(at, plane), 0))
    return pl.pallas_call(
        functools.partial(pack_kernel, apart),
        out_shape=out_shape,
        grid_spec=pltpu.PrefetchScalarGridSpec(
            num_scalar_prefetch=1,
            grid=(steps,),
            in_specs=[across, across, down] + [pl.BlockSpec(memory_space=pl.ANY)] * len(after),
            out_specs=out_specs,
        ),
        compiler_params=pltpu.CompilerParams(vmem_limit_bytes=LIMIT),
        cost_estimate=pl.CostEstimate(
            flops=0, bytes_accessed=10 * rows * tiles * LANES, transcendentals=rows * tiles * LANES
        ),
        name="pack",
    )(plane, gate, up, weight, *after)


def unpack_kernel(count, *refs):
    sources, (a, w, sem) = refs[:count], refs[-3:]
    copies = []
    for at in range(count):
        for kind, out in enumerate((a, w)):
            to = out if count == 1 else out.at[at]
            copies.append(
                pltpu.make_async_copy(sources[at].at[kind], to, sem.at[2 * at + kind])
            )
    for copy in copies:
        copy.start()
    for copy in copies:
        copy.wait()


def unpack(packed, after):
    count, shape = len(packed), packed[0].shape[1:]
    if count > 1:
        shape = (count,) + shape
    return pl.pallas_call(
        functools.partial(unpack_kernel, count),
        out_shape=[jax.ShapeDtypeStruct(shape, jnp.bfloat16)] * 2,
        in_specs=[pl.BlockSpec(memory_space=pl.ANY)] * (count + len(after)),
        out_specs=[pl.BlockSpec(memory_space=pl.ANY)] * 2,
        scratch_shapes=[pltpu.SemaphoreType.DMA((2 * count,))],
        cost_estimate=pl.CostEstimate(
            flops=0, bytes_accessed=4 * packed[0].size * count, transcendentals=0
        ),
        name="unpack",
    )(*packed, *after)


def hold_kernel(*refs):
    source, out, sem = refs[0], refs[-2], refs[-1]
    copy = pltpu.make_async_copy(source, out, sem)
    copy.start()
    copy.wait()


def hold(array, after):
    return pl.pallas_call(
        hold_kernel,
        out_shape=jax.ShapeDtypeStruct(array.shape, array.dtype),
        in_specs=[pl.BlockSpec(memory_space=pl.ANY)] * (1 + len(after)),
        out_specs=pl.BlockSpec(memory_space=pl.ANY),
        scratch_shapes=[pltpu.SemaphoreType.DMA],
        cost_estimate=pl.CostEstimate(flops=0, bytes_accessed=4 * array.size, transcendentals=0),
        name="hold",
    )(array, *after)


def product_kernel(a_at, w_at, own, mid_ref, *refs):
    groups = len(a_at) // 4
    outs, (a, w, a_sem, w_sem) = refs[-4 - groups : -4], refs[-4:]
    rows = a.shape[1] // len(a_at)
    tiles, _, columns = w.shape
    columns //= 4

    def pick(at):
        ref, index = at
        return refs[ref] if index is None else refs[ref].at[index]

    def w_copy(at, choice):
        return pltpu.make_async_copy(
            pick(w_at[choice][at]), w.at[:, :, pl.ds(at * columns, columns)], w_sem.at[at]
        )

    def a_copy(at):
        return pltpu.make_async_copy(
            pick(a_at[at]), a.at[:, pl.ds(at * rows, rows)], a_sem.at[at]
        )

    for at in range(4):
        if len(w_at) == 1:
            w_copy(at, 0).start()
        else:
            for choice in range(len(w_at)):

                @pl.when(mid_ref[0] == choice)
                def _():
                    w_copy(at, choice).start()

    for at in range(len(a_at)):
        a_copy(at).start()
    for at in range(4):
        w_copy(at, 0).wait()
    for group in range(groups):
        for at in range(4 * group, 4 * group + 4):
            a_copy(at).wait()
        left = jnp.concatenate(
            [a[tile, pl.ds(4 * group * rows, 4 * rows)] for tile in range(tiles)], axis=1
        )
        total = jnp.dot(
            left,
            w[...].reshape(tiles * LANES, 4 * columns),
            preferred_element_type=jnp.float32,
        )
        outs[group][...] = total.reshape(4, rows, 4 * columns).astype(outs[group].dtype)


def product(mid, groups, a_blocks, w_choices, own, after=()):
    arrays = []

    def at(block):
        array, index = block
        for known, other in enumerate(arrays):
            if other is array:
                return known, index
        arrays.append(array)
        return len(arrays) - 1, index

    a_at = [at(block) for group in groups for block in a_blocks[group]]
    w_at = [[at(block) for block in choice] for choice in w_choices]
    tiles, rows, _ = a_blocks[0][0][0].shape
    columns = w_choices[-1][0][0].shape[-1]
    shape = (4, rows, 4 * columns)
    count = len(arrays) + len(after)
    return pl.pallas_call(
        functools.partial(product_kernel, a_at, w_at, own),
        out_shape=[
            jax.ShapeDtypeStruct(shape, jnp.float32 if group == own else jnp.bfloat16)
            for group in groups
        ],
        in_specs=[pl.BlockSpec(memory_space=pltpu.SMEM)]
        + [pl.BlockSpec(memory_space=pl.ANY)] * count,
        out_specs=[pl.BlockSpec(memory_space=pltpu.VMEM)] * len(groups),
        scratch_shapes=[
            pltpu.VMEM((tiles, len(a_at) * rows, LANES), jnp.bfloat16),
            pltpu.VMEM((tiles, LANES, 4 * columns), jnp.bfloat16),
            pltpu.SemaphoreType.DMA((len(a_at),)),
            pltpu.SemaphoreType.DMA((4,)),
        ],
        compiler_params=pltpu.CompilerParams(vmem_limit_bytes=LIMIT),
        cost_estimate=pl.CostEstimate(
            flops=2 * len(a_at) * rows * tiles * LANES * 4 * columns,
            bytes_accessed=2 * tiles * LANES * (len(a_at) * rows + 4 * columns),
            transcendentals=0,
        ),
        name="product",
    )(mid, *arrays, *after)


def add_kernel(own, one, two, three, *outs):
    columns = own.shape[2] // 4
    for piece in range(4):
        for at in range(4):
            here = pl.ds(at * columns, columns)
            total = own[piece, :, here]
            for step, ref in ((1, one), (2, two), (3, three)):
                total += ref[piece, :, pl.ds((at ^ step) * columns, columns)].astype(jnp.float32)
            outs[piece][:, here] = total.astype(jnp.bfloat16)


def add(own, others):
    _, rows, columns = own.shape
    return pl.pallas_call(
        add_kernel,
        out_shape=[jax.ShapeDtypeStruct((rows, columns), jnp.bfloat16)] * 4,
        in_specs=[pl.BlockSpec(memory_space=pltpu.VMEM)] * 4,
        out_specs=[pl.BlockSpec(memory_space=pltpu.VMEM)] * 4,
        compiler_params=pltpu.CompilerParams(vmem_limit_bytes=LIMIT),
        cost_estimate=pl.CostEstimate(
            flops=12 * rows * columns, bytes_accessed=48 * rows * columns, transcendentals=0
        ),
        name="add",
    )(own, *others)


def assemble_kernel(place_ref, *refs):
    pieces, out = refs[:8], refs[8]
    columns = out.shape[1] // 32
    place = place_ref[0]
    for half in range(2):
        for piece in range(4):
            for at in range(4):
                index = ((piece >> 1) << 4) | (half << 3) | (at << 1) | (piece & 1)
                to = pl.multiple_of((place ^ index) * columns, columns)
                out[:, pl.ds(to, columns)] = pieces[4 * half + piece][:, pl.ds(at * columns, columns)]


def assemble(place, pieces):
    rows, columns = pieces[0].shape
    return pl.pallas_call(
        assemble_kernel,
        out_shape=jax.ShapeDtypeStruct((rows, 8 * columns), jnp.bfloat16),
        in_specs=[pl.BlockSpec(memory_space=pltpu.SMEM)]
        + [pl.BlockSpec(memory_space=pltpu.VMEM)] * 8,
        out_specs=pl.BlockSpec(memory_space=pltpu.VMEM),
        compiler_params=pltpu.CompilerParams(vmem_limit_bytes=LIMIT),
        name="assemble",
    )(place, *pieces)


def blocks(gate_pre, up_pre, down_weight):
    n = lax.axis_size("fsdp")
    me = lax.axis_index("fsdp")
    plane = (me // PLANE) % 4
    z_low, z_high = (me // PAIR) % 2, me // (2 * PAIR)
    at_plane = plane.astype(jnp.int32).reshape(1)
    inputs = (gate_pre, up_pre, down_weight)

    def send(array, perm):
        return lax.ppermute(array, "fsdp", perm=perm)

    def to_mid(array):
        return send(array, along_z(n, [(1, 2), (2, 1)]))

    def to_next(array):
        return send(array, along_z(n, [(1, 0), (3, 1), (0, 2), (2, 3)]))

    def to_core(array):
        return send(array, flip(n, CORE))

    def to_pair(array):
        return send(array, flip(n, PAIR))

    a_0, w_0 = pack(at_plane, 0, *inputs, apart=True)
    packed_1 = pack(at_plane, 1, *inputs, apart=False, after=(a_0,))
    packed_2 = pack(at_plane, 2, *inputs, apart=False, after=(packed_1,))
    pair_0, mid_0, next_0 = to_pair(a_0), to_mid(w_0), to_next(w_0)
    got_1 = send(packed_1, flip(n, PLANE))
    got_2 = send(packed_2, flip(n, 2 * PLANE))

    a_12, w_12 = unpack([got_1, got_2], after=(pair_0, mid_0, next_0))
    packed_3 = pack(at_plane, 3, *inputs, apart=False, after=(a_12,))
    pair_12, mid_12 = to_pair(a_12), to_mid(w_12)
    got_3 = send(packed_3, flip(n, 3 * PLANE))
    core_0, core_pair_0 = to_core(a_0), to_core(pair_0)

    a_3, w_3 = unpack([got_3], after=(pair_12, mid_12, core_0, core_pair_0))
    pair_3, mid_3 = to_pair(a_3), to_mid(w_3)
    next_12 = to_next(hold(w_12, after=(a_3,)))
    core_12, core_pair_12 = to_core(a_12), to_core(pair_12)
    core_3, core_pair_3 = to_core(a_3), to_core(pair_3)
    next_3 = to_next(hold(w_3, after=(pair_3,)))

    a_blocks = [
        [(a_0, None), (core_0, None), (pair_0, None), (core_pair_0, None)],
        [(a_12, 0), (core_12, 0), (pair_12, 0), (core_pair_12, 0)],
        [(a_12, 1), (core_12, 1), (pair_12, 1), (core_pair_12, 1)],
        [(a_3, None), (core_3, None), (pair_3, None), (core_pair_3, None)],
    ]
    w_first = [(w_0, None), (w_12, 0), (w_12, 1), (w_3, None)]
    w_mid = [(mid_0, None), (mid_12, 0), (mid_12, 1), (mid_3, None)]
    w_next = [(next_0, None), (next_12, 0), (next_12, 1), (next_3, None)]
    mid = (z_low ^ z_high).astype(jnp.int32).reshape(1)
    pieces = []
    for choices, calls in (([w_first, w_mid], ([3, 1, 2, 0],)), ([w_next], ([3], [1, 2], [0]))):
        totals, last = {}, ()
        for groups in calls:
            outs = product(mid, groups, a_blocks, choices, 0, last)
            totals.update(zip(groups, outs))
            last = (outs[0],)
        others = [send(totals[step], flip(n, step * PLANE)) for step in (1, 2, 3)]
        summed = add(totals[0], others)
        pieces += [summed[0]] + [
            send(summed[piece], flip(n, (piece >> 1) * PAIR + (piece & 1) * CORE))
            for piece in (1, 2, 3)
        ]
    place = (z_low * 16 + z_high * 8 + plane * 2 + me % 2).astype(jnp.int32).reshape(1)
    return assemble(place, pieces)


def shards(gate_pre, up_pre, down_weight):
    hidden = silu_product(gate_pre, up_pre)
    terms = jnp.dot(
        hidden,
        lax.all_gather(down_weight, "fsdp", axis=1, tiled=True),
        preferred_element_type=jnp.float32,
    )
    totals = lax.psum(terms, "tp")
    share = totals.shape[1] // lax.axis_size("tp")
    result = lax.dynamic_slice_in_dim(totals, lax.axis_index("tp") * share, share, 1)
    return result.astype(jnp.bfloat16)


def solution(mesh):
    in_blocks = mesh.shape["tp"] == 1 and mesh.shape["fsdp"] == 4 * PAIR
    return jax.shard_map(
        blocks if in_blocks else shards,
        mesh=mesh,
        in_specs=(P("fsdp", "tp"), P("fsdp", "tp"), P("tp", "fsdp")),
        out_specs=P("fsdp", "tp"),
        check_vma=False,
    )
```

```python
import functools

import jax
import jax.numpy as jnp
from jax import lax
from jax.experimental import pallas as pl
from jax.experimental.pallas import tpu as pltpu
from jax.sharding import PartitionSpec as P

CORE, PLANE, PAIR = 1, 2, 8
LIMIT = 60 * 1024 * 1024
LANES = 128


def flip(n, mask):
    return [(source, source ^ mask) for source in range(n)]


def along_z(n, pairs):
    low = PAIR
    return [(a * low + rest, b * low + rest) for a, b in pairs for rest in range(low)]


def silu_product(gate, up):
    return (jax.nn.silu(gate.astype(jnp.float32)) * up.astype(jnp.float32)).astype(jnp.bfloat16)


def pack_kernel(apart, count, plane_ref, *refs):
    outs = refs[len(refs) - count - apart :]
    pairs = [(outs[0], outs[1])] if apart else []
    pairs += [(out.at[0], out.at[1]) for out in outs[2 * apart :]]
    for at, (a, w) in enumerate(pairs):
        gate, up, weight = refs[3 * at : 3 * at + 3]
        hidden = silu_product(gate[...], up[...])
        for tile in range(a.shape[0]):
            a[tile] = hidden[:, tile * LANES : (tile + 1) * LANES]
            w[tile] = weight[pl.ds(tile * LANES, LANES)]


def pack(plane, steps, gate, up, weight, after=()):
    rows, columns = gate.shape[0], weight.shape[1]
    tiles = gate.shape[1] // (4 * LANES)
    grid = 4
    share = tiles // grid
    apart = int(steps[0] == 0)
    single = jax.ShapeDtypeStruct((tiles, rows, LANES), jnp.bfloat16)
    double = jax.ShapeDtypeStruct((2, tiles, rows, LANES), jnp.bfloat16)
    single_spec = pl.BlockSpec((share, rows, LANES), lambda at, plane: (at, 0, 0))
    double_spec = pl.BlockSpec((2, share, rows, LANES), lambda at, plane: (0, at, 0, 0))
    others = len(steps) - apart
    in_specs = []
    for step in steps:

        def across(at, plane, step=step):
            return 0, (plane[0] ^ step) * grid + at

        def down(at, plane, step=step):
            return (plane[0] ^ step) * grid + at, 0

        wide = pl.BlockSpec((rows, share * LANES), across)
        in_specs += [wide, wide, pl.BlockSpec((share * LANES, columns), down)]
    in_specs += [pl.BlockSpec(memory_space=pl.ANY)] * len(after)
    return pl.pallas_call(
        functools.partial(pack_kernel, apart, len(steps)),
        out_shape=[single] * (2 * apart) + [double] * others,
        grid_spec=pltpu.PrefetchScalarGridSpec(
            num_scalar_prefetch=1,
            grid=(grid,),
            in_specs=in_specs,
            out_specs=[single_spec] * (2 * apart) + [double_spec] * others,
        ),
        compiler_params=pltpu.CompilerParams(vmem_limit_bytes=LIMIT),
        cost_estimate=pl.CostEstimate(
            flops=0,
            bytes_accessed=10 * rows * tiles * LANES * len(steps),
            transcendentals=rows * tiles * LANES * len(steps),
        ),
        name="pack",
    )(plane, *[gate, up, weight] * len(steps), *after)


def unpack_pair_kernel(one, two, *refs):
    a, w, held, in_sem, out_sem = refs[-5:]
    ways = [
        (source.at[kind], out.at[at])
        for at, source in enumerate((one, two))
        for kind, out in enumerate((a, w))
    ]
    into = [
        pltpu.make_async_copy(source, held.at[at], in_sem.at[at])
        for at, (source, _) in enumerate(ways)
    ]
    out_of = [
        pltpu.make_async_copy(held.at[at], to, out_sem.at[at]) for at, (_, to) in enumerate(ways)
    ]
    for copy in into:
        copy.start()
    for copy_in, copy_out in zip(into, out_of):
        copy_in.wait()
        copy_out.start()
    for copy in out_of:
        copy.wait()


def unpack_pair(one, two, after):
    return pl.pallas_call(
        unpack_pair_kernel,
        out_shape=[jax.ShapeDtypeStruct(one.shape, one.dtype)] * 2,
        in_specs=[pl.BlockSpec(memory_space=pl.ANY)] * (2 + len(after)),
        out_specs=[pl.BlockSpec(memory_space=pl.ANY)] * 2,
        scratch_shapes=[
            pltpu.VMEM((4,) + one.shape[1:], one.dtype),
            pltpu.SemaphoreType.DMA((4,)),
            pltpu.SemaphoreType.DMA((4,)),
        ],
        compiler_params=pltpu.CompilerParams(vmem_limit_bytes=LIMIT),
        cost_estimate=pl.CostEstimate(flops=0, bytes_accessed=8 * one.size, transcendentals=0),
        name="unpack_pair",
    )(one, two, *after)


def reorder_kernel(count, order_ref, packed, w_12, *refs):
    outs, (held, in_sem, out_sem) = refs[-3 - count : -3], refs[-3:]
    into = [
        pltpu.make_async_copy(source, held.at[at], in_sem.at[at])
        for at, source in enumerate((packed.at[0], w_12.at[0], w_12.at[1], packed.at[1]))
    ]
    out_of = [
        pltpu.make_async_copy(held.at[order_ref[at]], out, out_sem.at[at])
        for at, out in enumerate(outs)
    ]
    for copy in into:
        copy.start()
    for copy in into:
        copy.wait()
    for copy in out_of:
        copy.start()
    for copy in out_of:
        copy.wait()


def reorder(order, packed, w_12, after):
    shape, count = packed.shape[1:], order.shape[0]
    return pl.pallas_call(
        functools.partial(reorder_kernel, count),
        out_shape=[jax.ShapeDtypeStruct(shape, packed.dtype)] * count,
        in_specs=[pl.BlockSpec(memory_space=pltpu.SMEM)]
        + [pl.BlockSpec(memory_space=pl.ANY)] * (2 + len(after)),
        out_specs=[pl.BlockSpec(memory_space=pl.ANY)] * count,
        scratch_shapes=[
            pltpu.VMEM((4,) + shape, packed.dtype),
            pltpu.SemaphoreType.DMA((4,)),
            pltpu.SemaphoreType.DMA((count,)),
        ],
        compiler_params=pltpu.CompilerParams(vmem_limit_bytes=LIMIT),
        cost_estimate=pl.CostEstimate(flops=0, bytes_accessed=8 * packed.size, transcendentals=0),
        name="reorder",
    )(order, packed, w_12, *after)


def product_kernel(a_at, w_at, choice_ref, *refs):
    groups = len(a_at) // 4
    outs, (a, w, a_sem, w_sem) = refs[-4 - groups : -4], refs[-4:]
    rows = a.shape[1] // len(a_at)
    wide = len(w_at[0])
    tiles, _, columns = w.shape
    columns //= wide

    def pick(at):
        ref, index = at
        return refs[ref] if index is None else refs[ref].at[index]

    def w_copy(at, choice):
        return pltpu.make_async_copy(
            pick(w_at[choice][at]), w.at[:, :, pl.ds(at * columns, columns)], w_sem.at[at]
        )

    def a_copy(at):
        return pltpu.make_async_copy(
            pick(a_at[at]), a.at[:, pl.ds(at * rows, rows)], a_sem.at[at]
        )

    for at in range(wide):
        for choice in range(len(w_at)):

            @pl.when(choice_ref[0] == choice)
            def _():
                w_copy(at, choice).start()

    for at in range(len(a_at)):
        a_copy(at).start()
    for at in range(wide):
        w_copy(at, 0).wait()
    for group in range(groups):
        for at in range(4 * group, 4 * group + 4):
            a_copy(at).wait()
        left = jnp.concatenate(
            [a[tile, pl.ds(4 * group * rows, 4 * rows)] for tile in range(tiles)], axis=1
        )
        total = jnp.dot(
            left,
            w[...].reshape(tiles * LANES, wide * columns),
            preferred_element_type=jnp.float32,
        )
        outs[group][...] = total.reshape(4, rows, wide * columns).astype(outs[group].dtype)


def product(choice, groups, a_blocks, w_choices, after=()):
    arrays = []

    def at(block):
        array, index = block
        for known, other in enumerate(arrays):
            if other is array:
                return known, index
        arrays.append(array)
        return len(arrays) - 1, index

    a_at = [at(block) for group in groups for block in a_blocks[group]]
    w_at = [[at(block) for block in choice] for choice in w_choices]
    tiles, rows, _ = a_blocks[0][0][0].shape
    columns = w_choices[-1][0][0].shape[-1]
    wide = len(w_choices[0])
    shape = (4, rows, wide * columns)
    count = len(arrays) + len(after)
    return pl.pallas_call(
        functools.partial(product_kernel, a_at, w_at),
        out_shape=[
            jax.ShapeDtypeStruct(shape, jnp.float32 if group == 0 else jnp.bfloat16)
            for group in groups
        ],
        in_specs=[pl.BlockSpec(memory_space=pltpu.SMEM)]
        + [pl.BlockSpec(memory_space=pl.ANY)] * count,
        out_specs=[pl.BlockSpec(memory_space=pltpu.VMEM)] * len(groups),
        scratch_shapes=[
            pltpu.VMEM((tiles, len(a_at) * rows, LANES), jnp.bfloat16),
            pltpu.VMEM((tiles, LANES, wide * columns), jnp.bfloat16),
            pltpu.SemaphoreType.DMA((len(a_at),)),
            pltpu.SemaphoreType.DMA((wide,)),
        ],
        compiler_params=pltpu.CompilerParams(vmem_limit_bytes=LIMIT),
        cost_estimate=pl.CostEstimate(
            flops=2 * len(a_at) * rows * tiles * LANES * wide * columns,
            bytes_accessed=2 * tiles * LANES * (len(a_at) * rows + wide * columns),
            transcendentals=0,
        ),
        name="product",
    )(choice, *arrays, *after)


def add_kernel(relative, own, one, two, three, *refs):
    blocks_wide, outs = own.shape[2] // LANES, refs[-4:]
    for piece in range(4):
        for at in range(blocks_wide):
            here = pl.ds(at * LANES, LANES)
            total = own[piece, :, here]
            for step, ref in ((1, one), (2, two), (3, three)):
                source = at ^ step if relative else at
                total += ref[piece, :, pl.ds(source * LANES, LANES)].astype(jnp.float32)
            outs[piece][:, here] = total.astype(jnp.bfloat16)


def add(own, others, relative, after=()):
    _, rows, columns = own.shape
    return pl.pallas_call(
        functools.partial(add_kernel, relative),
        out_shape=[jax.ShapeDtypeStruct((rows, columns), jnp.bfloat16)] * 4,
        in_specs=[pl.BlockSpec(memory_space=pltpu.VMEM)] * 4
        + [pl.BlockSpec(memory_space=pl.ANY)] * len(after),
        out_specs=[pl.BlockSpec(memory_space=pltpu.VMEM)] * 4,
        compiler_params=pltpu.CompilerParams(vmem_limit_bytes=LIMIT),
        cost_estimate=pl.CostEstimate(
            flops=12 * rows * columns, bytes_accessed=48 * rows * columns, transcendentals=0
        ),
        name="add",
    )(own, *others, *after)


def assemble_kernel(groups, place_ref, *refs):
    out = refs[-1]
    for ref, (fixed, first, relative) in zip(refs, groups):
        place = place_ref[0] if relative else place_ref[1]
        for at in range(ref.shape[1] // LANES):
            index = fixed | ((first + at) << 1)
            to = pl.multiple_of((place ^ index) * LANES, LANES)
            out[:, pl.ds(to, LANES)] = ref[:, pl.ds(at * LANES, LANES)]


def assemble(place, pieces):
    arrays = [piece[0] for piece in pieces]
    rows = arrays[0].shape[0]
    columns = sum(array.shape[1] for array in arrays)
    return pl.pallas_call(
        functools.partial(assemble_kernel, [piece[1:] for piece in pieces]),
        out_shape=jax.ShapeDtypeStruct((rows, columns), jnp.bfloat16),
        in_specs=[pl.BlockSpec(memory_space=pltpu.SMEM)]
        + [pl.BlockSpec(memory_space=pltpu.VMEM)] * len(arrays),
        out_specs=pl.BlockSpec(memory_space=pltpu.VMEM),
        compiler_params=pltpu.CompilerParams(vmem_limit_bytes=LIMIT),
        name="assemble",
    )(place, *arrays)


def blocks(gate_pre, up_pre, down_weight):
    n = lax.axis_size("fsdp")
    me = lax.axis_index("fsdp")
    plane = (me // PLANE) % 4
    z_low, z_high = (me // PAIR) % 2, me // (2 * PAIR)
    at_plane = plane.astype(jnp.int32).reshape(1)
    inputs = (gate_pre, up_pre, down_weight)

    def send(array, perm):
        return lax.ppermute(array, "fsdp", perm=perm)

    def to_mid(array):
        return send(array, along_z(n, [(1, 2), (2, 1)]))

    def to_next(array):
        return send(array, along_z(n, [(1, 0), (3, 1), (0, 2), (2, 3)]))

    def to_core(array):
        return send(array, flip(n, CORE))

    def to_pair(array):
        return send(array, flip(n, PAIR))

    a_0, w_0, packed_1, packed_2 = pack(at_plane, (0, 1, 2), *inputs)
    pair_0, mid_0, next_0 = to_pair(a_0), to_mid(w_0), to_next(w_0)
    got_1 = send(packed_1, flip(n, PLANE))
    got_2 = send(packed_2, flip(n, 2 * PLANE))

    (packed_3,) = pack(at_plane, (3,), *inputs, after=(pair_0,))
    got_3 = send(packed_3, flip(n, 3 * PLANE))
    a_12, w_12 = unpack_pair(got_1, got_2, after=(pair_0, mid_0, next_0))
    pair_12, mid_12 = to_pair(a_12), to_mid(w_12)
    core_0, core_pair_0 = to_core(a_0), to_core(pair_0)

    order = jnp.array([[1, 2, 3], [1, 3, 2], [2, 3, 1], [3, 2, 1]], jnp.int32)[plane]
    known = jnp.array([0, 3], jnp.int32)
    a_3, w_3, ordered_1 = reorder(
        jnp.concatenate([known, order[:1]]), got_3, w_12, after=(core_0, core_pair_0)
    )
    pair_3, mid_3 = to_pair(a_3), to_mid(w_3)
    core_12, core_pair_12 = to_core(a_12), to_core(pair_12)
    ordered_2, ordered_3 = reorder(
        order[1:], got_3, w_12, after=(pair_3, mid_3, core_12, core_pair_12)
    )
    next_1, next_2, next_3 = to_next(ordered_1), to_next(ordered_2), to_next(ordered_3)
    core_3, core_pair_3 = to_core(a_3), to_core(pair_3)

    a_blocks = [
        [(a_0, None), (core_0, None), (pair_0, None), (core_pair_0, None)],
        [(a_12, 0), (core_12, 0), (pair_12, 0), (core_pair_12, 0)],
        [(a_12, 1), (core_12, 1), (pair_12, 1), (core_pair_12, 1)],
        [(a_3, None), (core_3, None), (pair_3, None), (core_pair_3, None)],
    ]
    w_own = [(w_0, None), (w_12, 0), (w_12, 1), (w_3, None)]
    w_mid = [(mid_0, None), (mid_12, 0), (mid_12, 1), (mid_3, None)]
    first, one, two, three = [(block, None) for block in (next_0, next_1, next_2, next_3)]
    w_low = [[first, one], [one, first], [one, two], [one, two]]
    w_high = [[two, three], [two, three], [first, three], [three, first]]
    mid = (z_low ^ z_high).astype(jnp.int32).reshape(1)
    pieces, summing, last = [], [], ()
    for choice, w_choices, calls in (
        (mid, [w_own, w_mid], ([3, 1, 2, 0],)),
        (at_plane, w_low, ([3, 1, 2, 0],)),
        (at_plane, w_high, ([3, 1, 2], [0])),
    ):
        totals = {}
        for groups in calls:
            outs = product(choice, groups, a_blocks, w_choices, last)
            totals.update(zip(groups, outs))
            last = (outs[0],)
        others = [send(totals[step], flip(n, step * PLANE)) for step in (1, 2, 3)]
        summing.append((totals[0], others))
        last = tuple(others)
    for at, (half, start) in enumerate(((0, 0), (1, 0), (1, 2))):
        later = tuple(summing[at + 1][0:1]) if at < 2 else ()
        summed = add(*summing[at], half == 0, later)
        for piece in range(4):
            mask = (piece >> 1) * PAIR + (piece & 1) * CORE
            block = send(summed[piece], flip(n, mask)) if mask else summed[piece]
            fixed = ((piece >> 1) << 4) | (half << 3) | (piece & 1)
            pieces.append((block, fixed, start, half == 0))
    across = z_low * 16 + z_high * 8 + me % 2
    place = jnp.stack([across + plane * 2, across]).astype(jnp.int32)
    return assemble(place, pieces)


def shards(gate_pre, up_pre, down_weight):
    hidden = silu_product(gate_pre, up_pre)
    terms = jnp.dot(
        hidden,
        lax.all_gather(down_weight, "fsdp", axis=1, tiled=True),
        preferred_element_type=jnp.float32,
    )
    totals = lax.psum(terms, "tp")
    share = totals.shape[1] // lax.axis_size("tp")
    result = lax.dynamic_slice_in_dim(totals, lax.axis_index("tp") * share, share, 1)
    return result.astype(jnp.bfloat16)


def solution(mesh):
    in_blocks = mesh.shape["tp"] == 1 and mesh.shape["fsdp"] == 4 * PAIR
    return jax.shard_map(
        blocks if in_blocks else shards,
        mesh=mesh,
        in_specs=(P("fsdp", "tp"), P("fsdp", "tp"), P("tp", "fsdp")),
        out_specs=P("fsdp", "tp"),
        check_vma=False,
    )
```

```python
import functools

import jax
import jax.numpy as jnp
from jax import lax
from jax.experimental import pallas as pl
from jax.experimental.pallas import tpu as pltpu
from jax.sharding import PartitionSpec as P

CORE, PLANE, PAIR = 1, 2, 8
LIMIT = 24 * 1024 * 1024
LANES = 128


def flip(n, mask):
    return [(source, source ^ mask) for source in range(n)]


def along_z(n, pairs):
    low = PAIR
    return [(a * low + rest, b * low + rest) for a, b in pairs for rest in range(low)]


def silu_product(gate, up):
    return (jax.nn.silu(gate.astype(jnp.float32)) * up.astype(jnp.float32)).astype(jnp.bfloat16)


def pack_kernel(apart, count, plane_ref, *refs):
    outs = refs[len(refs) - count - apart :]
    pairs = [(outs[0], outs[1])] if apart else []
    pairs += [(out.at[0], out.at[1]) for out in outs[2 * apart :]]
    for at, (a, w) in enumerate(pairs):
        gate, up, weight = refs[3 * at : 3 * at + 3]
        hidden = silu_product(gate[...], up[...])
        for tile in range(a.shape[0]):
            a[tile] = hidden[:, tile * LANES : (tile + 1) * LANES]
            w[tile] = weight[pl.ds(tile * LANES, LANES)]


def pack(plane, steps, gate, up, weight, after=()):
    rows, columns = gate.shape[0], weight.shape[1]
    tiles = gate.shape[1] // (4 * LANES)
    grid = 4
    share = tiles // grid
    apart = int(steps[0] == 0)
    single = jax.ShapeDtypeStruct((tiles, rows, LANES), jnp.bfloat16)
    double = jax.ShapeDtypeStruct((2, tiles, rows, LANES), jnp.bfloat16)
    single_spec = pl.BlockSpec((share, rows, LANES), lambda at, plane: (at, 0, 0))
    double_spec = pl.BlockSpec((2, share, rows, LANES), lambda at, plane: (0, at, 0, 0))
    others = len(steps) - apart
    in_specs = []
    for step in steps:

        def across(at, plane, step=step):
            return 0, (plane[0] ^ step) * grid + at

        def down(at, plane, step=step):
            return (plane[0] ^ step) * grid + at, 0

        wide = pl.BlockSpec((rows, share * LANES), across)
        in_specs += [wide, wide, pl.BlockSpec((share * LANES, columns), down)]
    in_specs += [pl.BlockSpec(memory_space=pl.ANY)] * len(after)
    return pl.pallas_call(
        functools.partial(pack_kernel, apart, len(steps)),
        out_shape=[single] * (2 * apart) + [double] * others,
        grid_spec=pltpu.PrefetchScalarGridSpec(
            num_scalar_prefetch=1,
            grid=(grid,),
            in_specs=in_specs,
            out_specs=[single_spec] * (2 * apart) + [double_spec] * others,
        ),
        compiler_params=pltpu.CompilerParams(vmem_limit_bytes=LIMIT),
        cost_estimate=pl.CostEstimate(
            flops=0,
            bytes_accessed=10 * rows * tiles * LANES * len(steps),
            transcendentals=rows * tiles * LANES * len(steps),
        ),
        name="pack",
    )(plane, *[gate, up, weight] * len(steps), *after)


def unpack_pair_kernel(one, two, *refs):
    a, w, held, in_sem, out_sem = refs[-5:]
    ways = [
        (source.at[kind], out.at[at])
        for at, source in enumerate((one, two))
        for kind, out in enumerate((a, w))
    ]
    into = [
        pltpu.make_async_copy(source, held.at[at], in_sem.at[at])
        for at, (source, _) in enumerate(ways)
    ]
    out_of = [
        pltpu.make_async_copy(held.at[at], to, out_sem.at[at]) for at, (_, to) in enumerate(ways)
    ]
    for copy in into:
        copy.start()
    for copy_in, copy_out in zip(into, out_of):
        copy_in.wait()
        copy_out.start()
    for copy in out_of:
        copy.wait()


def unpack_pair(one, two, after):
    return pl.pallas_call(
        unpack_pair_kernel,
        out_shape=[jax.ShapeDtypeStruct(one.shape, one.dtype)] * 2,
        in_specs=[pl.BlockSpec(memory_space=pl.ANY)] * (2 + len(after)),
        out_specs=[pl.BlockSpec(memory_space=pl.ANY)] * 2,
        scratch_shapes=[
            pltpu.VMEM((4,) + one.shape[1:], one.dtype),
            pltpu.SemaphoreType.DMA((4,)),
            pltpu.SemaphoreType.DMA((4,)),
        ],
        compiler_params=pltpu.CompilerParams(vmem_limit_bytes=LIMIT),
        cost_estimate=pl.CostEstimate(flops=0, bytes_accessed=8 * one.size, transcendentals=0),
        name="unpack_pair",
    )(one, two, *after)


def reorder_kernel(count, order_ref, packed, w_12, *refs):
    outs, (held, in_sem, out_sem) = refs[-3 - count : -3], refs[-3:]
    into = [
        pltpu.make_async_copy(source, held.at[at], in_sem.at[at])
        for at, source in enumerate((packed.at[0], w_12.at[0], w_12.at[1], packed.at[1]))
    ]
    out_of = [
        pltpu.make_async_copy(held.at[order_ref[at]], out, out_sem.at[at])
        for at, out in enumerate(outs)
    ]
    for copy in into:
        copy.start()
    for copy in into:
        copy.wait()
    for copy in out_of:
        copy.start()
    for copy in out_of:
        copy.wait()


def reorder(order, packed, w_12, after):
    shape, count = packed.shape[1:], order.shape[0]
    return pl.pallas_call(
        functools.partial(reorder_kernel, count),
        out_shape=[jax.ShapeDtypeStruct(shape, packed.dtype)] * count,
        in_specs=[pl.BlockSpec(memory_space=pltpu.SMEM)]
        + [pl.BlockSpec(memory_space=pl.ANY)] * (2 + len(after)),
        out_specs=[pl.BlockSpec(memory_space=pl.ANY)] * count,
        scratch_shapes=[
            pltpu.VMEM((4,) + shape, packed.dtype),
            pltpu.SemaphoreType.DMA((4,)),
            pltpu.SemaphoreType.DMA((count,)),
        ],
        compiler_params=pltpu.CompilerParams(vmem_limit_bytes=LIMIT),
        cost_estimate=pl.CostEstimate(flops=0, bytes_accessed=8 * packed.size, transcendentals=0),
        name="reorder",
    )(order, packed, w_12, *after)


def stack_kernel(first, count, *refs):
    sources, stack_ref, sem = refs[-2 - count : -2], refs[-2], refs[-1]
    rows = sources[0].shape[-2]
    copies, at = [], 0
    for source in sources:
        parts = [source] if len(source.shape) == 3 else [source.at[0], source.at[1]]
        for part in parts:
            to = stack_ref.at[:, pl.ds((first + at) * rows, rows)]
            copies.append(pltpu.make_async_copy(part, to, sem.at[at]))
            at += 1
    for copy in copies:
        copy.start()
    for copy in copies:
        copy.wait()


def stack(first, blocks, before=None):
    tiles, rows, lanes = blocks[0].shape[-3:]
    shape = (tiles, 16 * rows, lanes)
    held = [] if before is None else [pltpu.with_memory_space_constraint(before, pltpu.VMEM)]
    count = sum(block.size for block in blocks) // (tiles * rows * lanes)
    return pl.pallas_call(
        functools.partial(stack_kernel, first, len(blocks)),
        out_shape=pltpu.VMEM(shape, blocks[0].dtype),
        in_specs=[pl.BlockSpec(memory_space=pltpu.VMEM)] * len(held)
        + [pl.BlockSpec(memory_space=pl.ANY)] * len(blocks),
        out_specs=pl.BlockSpec(memory_space=pltpu.VMEM),
        scratch_shapes=[pltpu.SemaphoreType.DMA((count,))],
        input_output_aliases={0: 0} if held else {},
        compiler_params=pltpu.CompilerParams(vmem_limit_bytes=LIMIT),
        cost_estimate=pl.CostEstimate(
            flops=0, bytes_accessed=4 * count * tiles * rows * lanes, transcendentals=0
        ),
        name="stack",
    )(*held, *blocks)


def product_kernel(places, w_at, choice_ref, a, *refs):
    groups, wide = len(places), len(w_at[0])
    outs, (w, w_sem) = refs[-2 - groups : -2], refs[-2:]
    tiles, _, columns = w.shape
    columns //= wide
    rows = a.shape[1] // 16

    def pick(at):
        ref, index = at
        return refs[ref] if index is None else refs[ref].at[index]

    def w_copy(at, choice):
        return pltpu.make_async_copy(
            pick(w_at[choice][at]), w.at[:, :, pl.ds(at * columns, columns)], w_sem.at[at]
        )

    for at in range(wide):
        for choice in range(len(w_at)):

            @pl.when(choice_ref[0] == choice)
            def _():
                w_copy(at, choice).start()

    for at in range(wide):
        w_copy(at, 0).wait()
    right = w[...].reshape(tiles * LANES, wide * columns)
    for place, out in zip(places, outs):
        for half in range(2):
            here = [(place[2 * half + at], at) for at in range(2)]
            left = jnp.concatenate(
                [
                    jnp.concatenate(
                        [a[tile, pl.ds(block * rows, rows)] for tile in range(tiles)], axis=1
                    )
                    for block, _ in here
                ],
                axis=0,
            )
            total = jnp.dot(left, right, preferred_element_type=jnp.float32)
            for _, at in here:
                out[2 * half + at] = total[at * rows : (at + 1) * rows].astype(out.dtype)


def product(choice, groups, places, rows_stack, w_choices, after=()):
    arrays = []

    def at(block):
        array, index = block
        for known, other in enumerate(arrays):
            if other is array:
                return known, index
        arrays.append(array)
        return len(arrays) - 1, index

    w_at = [[at(block) for block in blocks] for blocks in w_choices]
    tiles, rows, _ = rows_stack.shape
    rows //= 16
    columns = w_choices[-1][0][0].shape[-1]
    wide = len(w_choices[0])
    shape = (4, rows, wide * columns)
    count = len(arrays) + len(after)
    return pl.pallas_call(
        functools.partial(product_kernel, [places[group] for group in groups], w_at),
        out_shape=[
            jax.ShapeDtypeStruct(shape, jnp.float32 if group == 0 else jnp.bfloat16)
            for group in groups
        ],
        in_specs=[
            pl.BlockSpec(memory_space=pltpu.SMEM),
            pl.BlockSpec(memory_space=pltpu.VMEM),
        ]
        + [pl.BlockSpec(memory_space=pl.ANY)] * count,
        out_specs=[pl.BlockSpec(memory_space=pltpu.VMEM)] * len(groups),
        scratch_shapes=[
            pltpu.VMEM((tiles, LANES, wide * columns), jnp.bfloat16),
            pltpu.SemaphoreType.DMA((wide,)),
        ],
        compiler_params=pltpu.CompilerParams(vmem_limit_bytes=LIMIT),
        cost_estimate=pl.CostEstimate(
            flops=8 * len(groups) * rows * tiles * LANES * wide * columns,
            bytes_accessed=2 * tiles * LANES * (4 * len(groups) * rows + wide * columns),
            transcendentals=0,
        ),
        name="product",
    )(choice, pltpu.with_memory_space_constraint(rows_stack, pltpu.VMEM), *arrays, *after)


def add_kernel(relative, own, one, two, three, *refs):
    blocks_wide, outs = own.shape[2] // LANES, refs[-4:]
    for piece in range(4):
        for at in range(blocks_wide):
            here = pl.ds(at * LANES, LANES)
            total = own[piece, :, here]
            for step, ref in ((1, one), (2, two), (3, three)):
                source = at ^ step if relative else at
                total += ref[piece, :, pl.ds(source * LANES, LANES)].astype(jnp.float32)
            outs[piece][:, here] = total.astype(jnp.bfloat16)


def add(own, others, relative, after=()):
    _, rows, columns = own.shape
    return pl.pallas_call(
        functools.partial(add_kernel, relative),
        out_shape=[jax.ShapeDtypeStruct((rows, columns), jnp.bfloat16)] * 4,
        in_specs=[pl.BlockSpec(memory_space=pltpu.VMEM)] * 4
        + [pl.BlockSpec(memory_space=pl.ANY)] * len(after),
        out_specs=[pl.BlockSpec(memory_space=pltpu.VMEM)] * 4,
        compiler_params=pltpu.CompilerParams(vmem_limit_bytes=LIMIT),
        cost_estimate=pl.CostEstimate(
            flops=12 * rows * columns, bytes_accessed=48 * rows * columns, transcendentals=0
        ),
        name="add",
    )(own, *others, *after)


def assemble_kernel(groups, place_ref, *refs):
    out = refs[-1]
    for ref, (fixed, first, relative) in zip(refs, groups):
        place = place_ref[0] if relative else place_ref[1]
        for at in range(ref.shape[1] // LANES):
            index = fixed | ((first + at) << 1)
            to = pl.multiple_of((place ^ index) * LANES, LANES)
            out[:, pl.ds(to, LANES)] = ref[:, pl.ds(at * LANES, LANES)]


def assemble(place, pieces):
    arrays = [piece[0] for piece in pieces]
    rows = arrays[0].shape[0]
    columns = sum(array.shape[1] for array in arrays)
    return pl.pallas_call(
        functools.partial(assemble_kernel, [piece[1:] for piece in pieces]),
        out_shape=jax.ShapeDtypeStruct((rows, columns), jnp.bfloat16),
        in_specs=[pl.BlockSpec(memory_space=pltpu.SMEM)]
        + [pl.BlockSpec(memory_space=pltpu.VMEM)] * len(arrays),
        out_specs=pl.BlockSpec(memory_space=pltpu.VMEM),
        compiler_params=pltpu.CompilerParams(vmem_limit_bytes=LIMIT),
        name="assemble",
    )(place, *arrays)


def blocks(gate_pre, up_pre, down_weight):
    n = lax.axis_size("fsdp")
    me = lax.axis_index("fsdp")
    plane = (me // PLANE) % 4
    z_low, z_high = (me // PAIR) % 2, me // (2 * PAIR)
    at_plane = plane.astype(jnp.int32).reshape(1)
    inputs = [
        pltpu.with_memory_space_constraint(array, pltpu.HBM)
        for array in (gate_pre, up_pre, down_weight)
    ]

    def send(array, perm):
        return lax.ppermute(array, "fsdp", perm=perm)

    def to_mid(array):
        return send(array, along_z(n, [(1, 2), (2, 1)]))

    def to_next(array):
        return send(array, along_z(n, [(1, 0), (3, 1), (0, 2), (2, 3)]))

    def to_core(array):
        return send(array, flip(n, CORE))

    def to_pair(array):
        return send(array, flip(n, PAIR))

    a_0, w_0, packed_1, packed_2 = pack(at_plane, (0, 1, 2), *inputs)
    pair_0, mid_0, next_0 = to_pair(a_0), to_mid(w_0), to_next(w_0)
    got_1 = send(packed_1, flip(n, PLANE))
    got_2 = send(packed_2, flip(n, 2 * PLANE))

    (packed_3,) = pack(at_plane, (3,), *inputs, after=(pair_0,))
    got_3 = send(packed_3, flip(n, 3 * PLANE))
    a_12, w_12 = unpack_pair(got_1, got_2, after=(pair_0, mid_0, next_0))
    pair_12, mid_12 = to_pair(a_12), to_mid(w_12)
    core_0, core_pair_0 = to_core(a_0), to_core(pair_0)

    order = jnp.array([[1, 2, 3], [1, 3, 2], [2, 3, 1], [3, 2, 1]], jnp.int32)[plane]
    a_12, got_3 = lax.optimization_barrier((a_12, got_3))
    known = jnp.array([0, 3], jnp.int32)
    a_3, w_3, ordered_1 = reorder(
        jnp.concatenate([known, order[:1]]), got_3, w_12, after=(core_0, core_pair_0, mid_12)
    )
    pair_3, mid_3 = to_pair(a_3), to_mid(w_3)
    core_12, core_pair_12 = to_core(a_12), to_core(pair_12)
    ordered_2, ordered_3 = reorder(
        order[1:], got_3, w_12, after=(pair_3, mid_3, core_12, core_pair_12)
    )
    next_1, next_2, next_3 = to_next(ordered_1), to_next(ordered_2), to_next(ordered_3)
    core_3, core_pair_3 = to_core(a_3), to_core(pair_3)

    rows_stack = stack(0, [a_0, pair_0, core_0, core_pair_0])
    rows_stack = stack(4, [a_12, pair_12, core_12, core_pair_12], rows_stack)
    rows_stack = stack(12, [a_3, pair_3, core_3, core_pair_3], rows_stack)
    places = [(0, 2, 1, 3), (4, 8, 6, 10), (5, 9, 7, 11), (12, 14, 13, 15)]
    w_own = [(w_0, None), (w_12, 0), (w_12, 1), (w_3, None)]
    w_mid = [(mid_0, None), (mid_12, 0), (mid_12, 1), (mid_3, None)]
    mid = (z_low ^ z_high).astype(jnp.int32).reshape(1)

    def totals_of(choice, w_choices, calls, after=()):
        totals = {}
        for groups in calls:
            outs = product(choice, groups, places, rows_stack, w_choices, after)
            totals.update(zip(groups, outs))
            after = (outs[0],)
        return [totals[group] for group in range(4)]

    def across_plane(totals):
        return [send(totals[step], flip(n, step * PLANE)) for step in (1, 2, 3)]

    pieces = []

    def spread(totals, others, half, start, after=()):
        summed, received = add(totals[0], others, half == 0, after), []
        for piece in range(4):
            mask = (piece >> 1) * PAIR + (piece & 1) * CORE
            block = send(summed[piece], flip(n, mask)) if mask else summed[piece]
            fixed = ((piece >> 1) << 4) | (half << 3) | (piece & 1)
            pieces.append((block, fixed, start, half == 0))
            received.append(block)
        return received[1:]

    own = totals_of(mid, [w_own, w_mid], ([3, 1, 2, 0],))
    *own, next_1 = lax.optimization_barrier((*own, next_1))
    own_sums = across_plane(own)
    first, one, two, three = [(block, None) for block in (next_0, next_1, next_2, next_3)]
    w_low = [[first, one], [one, first], [one, two], [one, two]]
    w_high = [[two, three], [two, three], [first, three], [three, first]]
    low = totals_of(at_plane, w_low, ([3, 1, 2, 0],), tuple(own_sums))
    low_sums = across_plane(low)
    own_spread = spread(own, own_sums, 0, 0, (low[0],))
    high = totals_of(at_plane, w_high, ([3], [1, 2], [0]), (*low_sums, *own_spread))
    high_sums = across_plane(high)
    spread(low, low_sums, 1, 0, (high[0],))
    spread(high, high_sums, 1, 2)
    across = z_low * 16 + z_high * 8 + me % 2
    place = jnp.stack([across + plane * 2, across]).astype(jnp.int32)
    return assemble(place, pieces)


def shards(gate_pre, up_pre, down_weight):
    hidden = silu_product(gate_pre, up_pre)
    terms = jnp.dot(
        hidden,
        lax.all_gather(down_weight, "fsdp", axis=1, tiled=True),
        preferred_element_type=jnp.float32,
    )
    totals = lax.psum(terms, "tp")
    share = totals.shape[1] // lax.axis_size("tp")
    result = lax.dynamic_slice_in_dim(totals, lax.axis_index("tp") * share, share, 1)
    return result.astype(jnp.bfloat16)


def solution(mesh):
    in_blocks = mesh.shape["tp"] == 1 and mesh.shape["fsdp"] == 4 * PAIR
    return jax.shard_map(
        blocks if in_blocks else shards,
        mesh=mesh,
        in_specs=(P("fsdp", "tp"), P("fsdp", "tp"), P("tp", "fsdp")),
        out_specs=P("fsdp", "tp"),
        check_vma=False,
    )
```

```python
import functools

import jax
import jax.numpy as jnp
from jax import lax
from jax.experimental import pallas as pl
from jax.experimental.pallas import tpu as pltpu
from jax.sharding import PartitionSpec as P

CORE, PLANE, PAIR = 1, 2, 8
LIMIT = 24 * 1024 * 1024
LANES = 128


def flip(n, mask):
    return [(source, source ^ mask) for source in range(n)]


def along_z(n, pairs):
    low = PAIR
    return [(a * low + rest, b * low + rest) for a, b in pairs for rest in range(low)]


def silu_product(gate, up):
    return (jax.nn.silu(gate.astype(jnp.float32)) * up.astype(jnp.float32)).astype(jnp.bfloat16)


def pack_kernel(apart, count, plane_ref, *refs):
    outs = refs[len(refs) - count - apart :]
    pairs = [(outs[0], outs[1])] if apart else []
    pairs += [(out.at[0], out.at[1]) for out in outs[2 * apart :]]
    for at, (a, w) in enumerate(pairs):
        gate, up, weight = refs[3 * at : 3 * at + 3]
        hidden = silu_product(gate[...], up[...])
        for tile in range(a.shape[0]):
            a[tile] = hidden[:, tile * LANES : (tile + 1) * LANES]
            w[tile] = weight[pl.ds(tile * LANES, LANES)]


def pack(plane, steps, gate, up, weight, after=()):
    rows, columns = gate.shape[0], weight.shape[1]
    tiles = gate.shape[1] // (4 * LANES)
    grid = 4
    share = tiles // grid
    apart = int(steps[0] == 0)
    single = jax.ShapeDtypeStruct((tiles, rows, LANES), jnp.bfloat16)
    double = jax.ShapeDtypeStruct((2, tiles, rows, LANES), jnp.bfloat16)
    single_spec = pl.BlockSpec((share, rows, LANES), lambda at, plane: (at, 0, 0))
    double_spec = pl.BlockSpec((2, share, rows, LANES), lambda at, plane: (0, at, 0, 0))
    others = len(steps) - apart
    in_specs = []
    for step in steps:

        def across(at, plane, step=step):
            return 0, (plane[0] ^ step) * grid + at

        def down(at, plane, step=step):
            return (plane[0] ^ step) * grid + at, 0

        wide = pl.BlockSpec((rows, share * LANES), across)
        in_specs += [wide, wide, pl.BlockSpec((share * LANES, columns), down)]
    in_specs += [pl.BlockSpec(memory_space=pl.ANY)] * len(after)
    return pl.pallas_call(
        functools.partial(pack_kernel, apart, len(steps)),
        out_shape=[single] * (2 * apart) + [double] * others,
        grid_spec=pltpu.PrefetchScalarGridSpec(
            num_scalar_prefetch=1,
            grid=(grid,),
            in_specs=in_specs,
            out_specs=[single_spec] * (2 * apart) + [double_spec] * others,
        ),
        compiler_params=pltpu.CompilerParams(vmem_limit_bytes=LIMIT),
        cost_estimate=pl.CostEstimate(
            flops=0,
            bytes_accessed=10 * rows * tiles * LANES * len(steps),
            transcendentals=rows * tiles * LANES * len(steps),
        ),
        name="pack",
    )(plane, *[gate, up, weight] * len(steps), *after)


def unpack_pair_kernel(one, two, *refs):
    a, w, held, in_sem, out_sem = refs[-5:]
    ways = [
        (source.at[kind], out.at[at])
        for at, source in enumerate((one, two))
        for kind, out in enumerate((a, w))
    ]
    into = [
        pltpu.make_async_copy(source, held.at[at], in_sem.at[at])
        for at, (source, _) in enumerate(ways)
    ]
    out_of = [
        pltpu.make_async_copy(held.at[at], to, out_sem.at[at]) for at, (_, to) in enumerate(ways)
    ]
    for copy in into:
        copy.start()
    for copy_in, copy_out in zip(into, out_of):
        copy_in.wait()
        copy_out.start()
    for copy in out_of:
        copy.wait()


def unpack_pair(one, two, after):
    return pl.pallas_call(
        unpack_pair_kernel,
        out_shape=[jax.ShapeDtypeStruct(one.shape, one.dtype)] * 2,
        in_specs=[pl.BlockSpec(memory_space=pl.ANY)] * (2 + len(after)),
        out_specs=[pl.BlockSpec(memory_space=pl.ANY)] * 2,
        scratch_shapes=[
            pltpu.VMEM((4,) + one.shape[1:], one.dtype),
            pltpu.SemaphoreType.DMA((4,)),
            pltpu.SemaphoreType.DMA((4,)),
        ],
        compiler_params=pltpu.CompilerParams(vmem_limit_bytes=LIMIT),
        cost_estimate=pl.CostEstimate(flops=0, bytes_accessed=8 * one.size, transcendentals=0),
        name="unpack_pair",
    )(one, two, *after)


def reorder_kernel(count, order_ref, packed, w_12, *refs):
    outs, (held, in_sem, out_sem) = refs[-3 - count : -3], refs[-3:]
    into = [
        pltpu.make_async_copy(source, held.at[at], in_sem.at[at])
        for at, source in enumerate((packed.at[0], w_12.at[0], w_12.at[1], packed.at[1]))
    ]
    out_of = [
        pltpu.make_async_copy(held.at[order_ref[at]], out, out_sem.at[at])
        for at, out in enumerate(outs)
    ]
    for copy in into:
        copy.start()
    for copy in into:
        copy.wait()
    for copy in out_of:
        copy.start()
    for copy in out_of:
        copy.wait()


def reorder(order, packed, w_12, after):
    shape, count = packed.shape[1:], order.shape[0]
    return pl.pallas_call(
        functools.partial(reorder_kernel, count),
        out_shape=[jax.ShapeDtypeStruct(shape, packed.dtype)] * count,
        in_specs=[pl.BlockSpec(memory_space=pltpu.SMEM)]
        + [pl.BlockSpec(memory_space=pl.ANY)] * (2 + len(after)),
        out_specs=[pl.BlockSpec(memory_space=pl.ANY)] * count,
        scratch_shapes=[
            pltpu.VMEM((4,) + shape, packed.dtype),
            pltpu.SemaphoreType.DMA((4,)),
            pltpu.SemaphoreType.DMA((count,)),
        ],
        compiler_params=pltpu.CompilerParams(vmem_limit_bytes=LIMIT),
        cost_estimate=pl.CostEstimate(flops=0, bytes_accessed=8 * packed.size, transcendentals=0),
        name="reorder",
    )(order, packed, w_12, *after)


def stack_kernel(first, count, *refs):
    sources, stack_ref, sem = refs[-2 - count : -2], refs[-2], refs[-1]
    rows = sources[0].shape[-2]
    copies, at = [], 0
    for source in sources:
        parts = [source] if len(source.shape) == 3 else [source.at[0], source.at[1]]
        for part in parts:
            to = stack_ref.at[:, pl.ds((first + at) * rows, rows)]
            copies.append(pltpu.make_async_copy(part, to, sem.at[at]))
            at += 1
    for copy in copies:
        copy.start()
    for copy in copies:
        copy.wait()


def stack(first, blocks, before=None):
    tiles, rows, lanes = blocks[0].shape[-3:]
    shape = (tiles, 16 * rows, lanes)
    held = [] if before is None else [pltpu.with_memory_space_constraint(before, pltpu.VMEM)]
    count = sum(block.size for block in blocks) // (tiles * rows * lanes)
    return pl.pallas_call(
        functools.partial(stack_kernel, first, len(blocks)),
        out_shape=pltpu.VMEM(shape, blocks[0].dtype),
        in_specs=[pl.BlockSpec(memory_space=pltpu.VMEM)] * len(held)
        + [pl.BlockSpec(memory_space=pl.ANY)] * len(blocks),
        out_specs=pl.BlockSpec(memory_space=pltpu.VMEM),
        scratch_shapes=[pltpu.SemaphoreType.DMA((count,))],
        input_output_aliases={0: 0} if held else {},
        compiler_params=pltpu.CompilerParams(vmem_limit_bytes=LIMIT),
        cost_estimate=pl.CostEstimate(
            flops=0, bytes_accessed=4 * count * tiles * rows * lanes, transcendentals=0
        ),
        name="stack",
    )(*held, *blocks)


def product_kernel(places, w_at, choice_ref, a, *refs):
    groups, wide = len(places), len(w_at[0])
    outs, (w, w_sem) = refs[-2 - groups : -2], refs[-2:]
    tiles, _, columns = w.shape
    columns //= wide
    rows = a.shape[1] // 16

    def pick(at):
        ref, index = at
        return refs[ref] if index is None else refs[ref].at[index]

    def w_copy(at, choice):
        return pltpu.make_async_copy(
            pick(w_at[choice][at]), w.at[:, :, pl.ds(at * columns, columns)], w_sem.at[at]
        )

    for at in range(wide):
        for choice in range(len(w_at)):

            @pl.when(choice_ref[0] == choice)
            def _():
                w_copy(at, choice).start()

    for at in range(wide):
        w_copy(at, 0).wait()
    right = w[...].reshape(tiles * LANES, wide * columns)
    for place, out in zip(places, outs):
        for half in range(2):
            here = [(place[2 * half + at], at) for at in range(2)]
            left = jnp.concatenate(
                [
                    jnp.concatenate(
                        [a[tile, pl.ds(block * rows, rows)] for tile in range(tiles)], axis=1
                    )
                    for block, _ in here
                ],
                axis=0,
            )
            total = jnp.dot(left, right, preferred_element_type=jnp.float32)
            for _, at in here:
                out[2 * half + at] = total[at * rows : (at + 1) * rows].astype(out.dtype)


def product(choice, groups, places, rows_stack, w_choices, after=()):
    arrays = []

    def at(block):
        array, index = block
        for known, other in enumerate(arrays):
            if other is array:
                return known, index
        arrays.append(array)
        return len(arrays) - 1, index

    w_at = [[at(block) for block in blocks] for blocks in w_choices]
    tiles, rows, _ = rows_stack.shape
    rows //= 16
    columns = w_choices[-1][0][0].shape[-1]
    wide = len(w_choices[0])
    shape = (4, rows, wide * columns)
    count = len(arrays) + len(after)
    return pl.pallas_call(
        functools.partial(product_kernel, [places[group] for group in groups], w_at),
        out_shape=[
            jax.ShapeDtypeStruct(shape, jnp.float32 if group == 0 else jnp.bfloat16)
            for group in groups
        ],
        in_specs=[
            pl.BlockSpec(memory_space=pltpu.SMEM),
            pl.BlockSpec(memory_space=pltpu.VMEM),
        ]
        + [pl.BlockSpec(memory_space=pl.ANY)] * count,
        out_specs=[pl.BlockSpec(memory_space=pltpu.VMEM)] * len(groups),
        scratch_shapes=[
            pltpu.VMEM((tiles, LANES, wide * columns), jnp.bfloat16),
            pltpu.SemaphoreType.DMA((wide,)),
        ],
        compiler_params=pltpu.CompilerParams(vmem_limit_bytes=LIMIT),
        cost_estimate=pl.CostEstimate(
            flops=8 * len(groups) * rows * tiles * LANES * wide * columns,
            bytes_accessed=2 * tiles * LANES * (4 * len(groups) * rows + wide * columns),
            transcendentals=0,
        ),
        name="product",
    )(choice, pltpu.with_memory_space_constraint(rows_stack, pltpu.VMEM), *arrays, *after)


def add_kernel(relative, own, one, two, three, *refs):
    blocks_wide, outs = own.shape[2] // LANES, refs[-4:]
    for piece in range(4):
        for at in range(blocks_wide):
            here = pl.ds(at * LANES, LANES)
            total = own[piece, :, here]
            for step, ref in ((1, one), (2, two), (3, three)):
                source = at ^ step if relative else at
                total += ref[piece, :, pl.ds(source * LANES, LANES)].astype(jnp.float32)
            outs[piece][:, here] = total.astype(jnp.bfloat16)


def add(own, others, relative, after=()):
    _, rows, columns = own.shape
    return pl.pallas_call(
        functools.partial(add_kernel, relative),
        out_shape=[jax.ShapeDtypeStruct((rows, columns), jnp.bfloat16)] * 4,
        in_specs=[pl.BlockSpec(memory_space=pltpu.VMEM)] * 4
        + [pl.BlockSpec(memory_space=pl.ANY)] * len(after),
        out_specs=[pl.BlockSpec(memory_space=pltpu.VMEM)] * 4,
        compiler_params=pltpu.CompilerParams(vmem_limit_bytes=LIMIT),
        cost_estimate=pl.CostEstimate(
            flops=12 * rows * columns, bytes_accessed=48 * rows * columns, transcendentals=0
        ),
        name="add",
    )(own, *others, *after)


def assemble_kernel(groups, place_ref, *refs):
    out = refs[-1]
    for ref, (fixed, first, relative) in zip(refs, groups):
        place = place_ref[0] if relative else place_ref[1]
        for at in range(ref.shape[1] // LANES):
            index = fixed | ((first + at) << 1)
            to = pl.multiple_of((place ^ index) * LANES, LANES)
            out[:, pl.ds(to, LANES)] = ref[:, pl.ds(at * LANES, LANES)]


def assemble(place, pieces):
    arrays = [piece[0] for piece in pieces]
    rows = arrays[0].shape[0]
    columns = sum(array.shape[1] for array in arrays)
    return pl.pallas_call(
        functools.partial(assemble_kernel, [piece[1:] for piece in pieces]),
        out_shape=jax.ShapeDtypeStruct((rows, columns), jnp.bfloat16),
        in_specs=[pl.BlockSpec(memory_space=pltpu.SMEM)]
        + [pl.BlockSpec(memory_space=pltpu.VMEM)] * len(arrays),
        out_specs=pl.BlockSpec(memory_space=pltpu.VMEM),
        compiler_params=pltpu.CompilerParams(vmem_limit_bytes=LIMIT),
        name="assemble",
    )(place, *arrays)


def blocks(gate_pre, up_pre, down_weight):
    n = lax.axis_size("fsdp")
    me = lax.axis_index("fsdp")
    plane = (me // PLANE) % 4
    z_low, z_high = (me // PAIR) % 2, me // (2 * PAIR)
    at_plane = plane.astype(jnp.int32).reshape(1)
    inputs = [
        pltpu.with_memory_space_constraint(array, pltpu.HBM)
        for array in (gate_pre, up_pre, down_weight)
    ]

    def send(array, perm):
        return lax.ppermute(array, "fsdp", perm=perm)

    def to_mid(array):
        return send(array, along_z(n, [(1, 2), (2, 1)]))

    def to_next(array):
        return send(array, along_z(n, [(1, 0), (3, 1), (0, 2), (2, 3)]))

    def to_core(array):
        return send(array, flip(n, CORE))

    def to_pair(array):
        return send(array, flip(n, PAIR))

    a_0, w_0, packed_1, packed_2 = pack(at_plane, (0, 1, 2), *inputs)
    pair_0, mid_0, next_0 = to_pair(a_0), to_mid(w_0), to_next(w_0)
    got_1 = send(packed_1, flip(n, PLANE))
    got_2 = send(packed_2, flip(n, 2 * PLANE))

    (packed_3,) = pack(at_plane, (3,), *inputs, after=(pair_0,))
    packed_3, got_1, got_2 = lax.optimization_barrier((packed_3, got_1, got_2))
    got_3 = send(packed_3, flip(n, 3 * PLANE))
    a_12, w_12 = unpack_pair(got_1, got_2, after=(pair_0, mid_0, next_0))
    pair_12, mid_12 = to_pair(a_12), to_mid(w_12)
    core_0, core_pair_0 = to_core(a_0), to_core(pair_0)

    order = jnp.array([[1, 2, 3], [1, 3, 2], [2, 3, 1], [3, 2, 1]], jnp.int32)[plane]
    a_12, got_3 = lax.optimization_barrier((a_12, got_3))
    known = jnp.array([0, 3], jnp.int32)
    a_3, w_3, ordered_1 = reorder(
        jnp.concatenate([known, order[:1]]), got_3, w_12, after=(core_0, core_pair_0, mid_12)
    )
    pair_3, mid_3 = to_pair(a_3), to_mid(w_3)
    core_12, core_pair_12 = to_core(a_12), to_core(pair_12)
    rows_stack = stack(0, [a_0, pair_0, core_0, core_pair_0])
    rows_stack = stack(4, [a_12, pair_12, core_12, core_pair_12], rows_stack)
    pair_3, mid_3, rows_stack = lax.optimization_barrier((pair_3, mid_3, rows_stack))
    ordered_2, ordered_3 = reorder(
        order[1:], got_3, w_12, after=(pair_3, mid_3, core_12, core_pair_12)
    )
    next_1, next_2, next_3 = to_next(ordered_1), to_next(ordered_2), to_next(ordered_3)
    core_3, core_pair_3 = to_core(a_3), to_core(pair_3)

    rows_stack = stack(12, [a_3, pair_3, core_3, core_pair_3], rows_stack)
    places = [(0, 2, 1, 3), (4, 8, 6, 10), (5, 9, 7, 11), (12, 14, 13, 15)]
    w_own = [(w_0, None), (w_12, 0), (w_12, 1), (w_3, None)]
    w_mid = [(mid_0, None), (mid_12, 0), (mid_12, 1), (mid_3, None)]
    mid = (z_low ^ z_high).astype(jnp.int32).reshape(1)

    def totals_of(choice, w_choices, calls, after=()):
        totals = {}
        for groups in calls:
            outs = product(choice, groups, places, rows_stack, w_choices, after)
            totals.update(zip(groups, outs))
            after = (outs[0],)
        return [totals[group] for group in range(4)]

    def across_plane(totals):
        return [send(totals[step], flip(n, step * PLANE)) for step in (1, 2, 3)]

    pieces = []

    def spread(totals, others, half, start, after=()):
        summed = add(totals[0], others, half == 0, after)
        for piece in range(4):
            mask = (piece >> 1) * PAIR + (piece & 1) * CORE
            block = send(summed[piece], flip(n, mask)) if mask else summed[piece]
            fixed = ((piece >> 1) << 4) | (half << 3) | (piece & 1)
            pieces.append((block, fixed, start, half == 0))

    own = totals_of(mid, [w_own, w_mid], ([3, 1, 2], [0]))
    own[1], own[2], own[3], next_1 = lax.optimization_barrier((*own[1:], next_1))
    own_sums = across_plane(own)
    first, one, two, three = [(block, None) for block in (next_0, next_1, next_2, next_3)]
    w_low = [[first, one], [one, first], [one, two], [one, two]]
    w_high = [[two, three], [two, three], [first, three], [three, first]]
    low = totals_of(at_plane, w_low, ([3, 1, 2, 0],), tuple(own_sums))
    low_sums = across_plane(low)
    spread(own, own_sums, 0, 0, (low[0],))
    high = totals_of(at_plane, w_high, ([3, 1, 2], [0]), tuple(low_sums))
    high_sums = across_plane(high)
    spread(low, low_sums, 1, 0, (high[0],))
    spread(high, high_sums, 1, 2)
    across = z_low * 16 + z_high * 8 + me % 2
    place = jnp.stack([across + plane * 2, across]).astype(jnp.int32)
    return assemble(place, pieces)


def shards(gate_pre, up_pre, down_weight):
    hidden = silu_product(gate_pre, up_pre)
    terms = jnp.dot(
        hidden,
        lax.all_gather(down_weight, "fsdp", axis=1, tiled=True),
        preferred_element_type=jnp.float32,
    )
    totals = lax.psum(terms, "tp")
    share = totals.shape[1] // lax.axis_size("tp")
    result = lax.dynamic_slice_in_dim(totals, lax.axis_index("tp") * share, share, 1)
    return result.astype(jnp.bfloat16)


def solution(mesh):
    in_blocks = mesh.shape["tp"] == 1 and mesh.shape["fsdp"] == 4 * PAIR
    return jax.shard_map(
        blocks if in_blocks else shards,
        mesh=mesh,
        in_specs=(P("fsdp", "tp"), P("fsdp", "tp"), P("tp", "fsdp")),
        out_specs=P("fsdp", "tp"),
        check_vma=False,
    )
```

```python
import functools

import jax
import jax.numpy as jnp
from jax import lax
from jax.experimental import pallas as pl
from jax.experimental.pallas import tpu as pltpu
from jax.sharding import PartitionSpec as P

CORE, PLANE, PAIR = 1, 2, 8
LIMIT = 24 * 1024 * 1024
LANES = 128


def flip(n, mask):
    return [(source, source ^ mask) for source in range(n)]


def along_z(n, pairs):
    low = PAIR
    return [(a * low + rest, b * low + rest) for a, b in pairs for rest in range(low)]


def silu_product(gate, up):
    return (jax.nn.silu(gate.astype(jnp.float32)) * up.astype(jnp.float32)).astype(jnp.bfloat16)


def pack_kernel(apart, count, plane_ref, *refs):
    outs = refs[len(refs) - count - apart :]
    pairs = [(outs[0], outs[1])] if apart else []
    pairs += [(out.at[0], out.at[1]) for out in outs[2 * apart :]]
    for at, (a, w) in enumerate(pairs):
        gate, up, weight = refs[3 * at : 3 * at + 3]
        hidden = silu_product(gate[...], up[...])
        for tile in range(a.shape[0]):
            a[tile] = hidden[:, tile * LANES : (tile + 1) * LANES]
            w[tile] = weight[pl.ds(tile * LANES, LANES)]


def pack(plane, steps, gate, up, weight, apart, after=()):
    rows, columns = gate.shape[0], weight.shape[1]
    tiles = gate.shape[1] // (4 * LANES)
    grid = 4
    share = tiles // grid
    single = jax.ShapeDtypeStruct((tiles, rows, LANES), jnp.bfloat16)
    double = jax.ShapeDtypeStruct((2, tiles, rows, LANES), jnp.bfloat16)
    single_spec = pl.BlockSpec((share, rows, LANES), lambda at, plane: (at, 0, 0))
    double_spec = pl.BlockSpec((2, share, rows, LANES), lambda at, plane: (0, at, 0, 0))
    others = len(steps) - apart
    in_specs = []
    for step in steps:

        def across(at, plane, step=step):
            return 0, (plane[0] ^ step) * grid + at

        def down(at, plane, step=step):
            return (plane[0] ^ step) * grid + at, 0

        wide = pl.BlockSpec((rows, share * LANES), across)
        in_specs += [wide, wide, pl.BlockSpec((share * LANES, columns), down)]
    in_specs += [pl.BlockSpec(memory_space=pl.ANY)] * len(after)
    return pl.pallas_call(
        functools.partial(pack_kernel, apart, len(steps)),
        out_shape=[single] * (2 * apart) + [double] * others,
        grid_spec=pltpu.PrefetchScalarGridSpec(
            num_scalar_prefetch=1,
            grid=(grid,),
            in_specs=in_specs,
            out_specs=[single_spec] * (2 * apart) + [double_spec] * others,
        ),
        compiler_params=pltpu.CompilerParams(vmem_limit_bytes=LIMIT),
        cost_estimate=pl.CostEstimate(
            flops=0,
            bytes_accessed=10 * rows * tiles * LANES * len(steps),
            transcendentals=rows * tiles * LANES * len(steps),
        ),
        name="pack",
    )(plane, *[gate, up, weight] * len(steps), *after)


def unpack_pair_kernel(one, two, *refs):
    a, w, held, in_sem, out_sem = refs[-5:]
    ways = [
        (source.at[kind], out.at[at])
        for at, source in enumerate((one, two))
        for kind, out in enumerate((a, w))
    ]
    into = [
        pltpu.make_async_copy(source, held.at[at], in_sem.at[at])
        for at, (source, _) in enumerate(ways)
    ]
    out_of = [
        pltpu.make_async_copy(held.at[at], to, out_sem.at[at]) for at, (_, to) in enumerate(ways)
    ]
    for copy in into:
        copy.start()
    for copy_in, copy_out in zip(into, out_of):
        copy_in.wait()
        copy_out.start()
    for copy in out_of:
        copy.wait()


def unpack_pair(one, two, after):
    return pl.pallas_call(
        unpack_pair_kernel,
        out_shape=[jax.ShapeDtypeStruct(one.shape, one.dtype)] * 2,
        in_specs=[pl.BlockSpec(memory_space=pl.ANY)] * (2 + len(after)),
        out_specs=[pl.BlockSpec(memory_space=pl.ANY)] * 2,
        scratch_shapes=[
            pltpu.VMEM((4,) + one.shape[1:], one.dtype),
            pltpu.SemaphoreType.DMA((4,)),
            pltpu.SemaphoreType.DMA((4,)),
        ],
        compiler_params=pltpu.CompilerParams(vmem_limit_bytes=LIMIT),
        cost_estimate=pl.CostEstimate(flops=0, bytes_accessed=8 * one.size, transcendentals=0),
        name="unpack_pair",
    )(one, two, *after)


def reorder_kernel(count, order_ref, w_12, w_3, *refs):
    outs, (held, in_sem, out_sem) = refs[-3 - count : -3], refs[-3:]
    into = [
        pltpu.make_async_copy(source, held.at[at], in_sem.at[at])
        for at, source in enumerate((w_12.at[0], w_12.at[1], w_3))
    ]
    out_of = [
        pltpu.make_async_copy(held.at[order_ref[at]], out, out_sem.at[at])
        for at, out in enumerate(outs)
    ]
    for copy in into:
        copy.start()
    for copy in into:
        copy.wait()
    for copy in out_of:
        copy.start()
    for copy in out_of:
        copy.wait()


def reorder(order, w_12, w_3, after=()):
    shape, count = w_3.shape, order.shape[0]
    return pl.pallas_call(
        functools.partial(reorder_kernel, count),
        out_shape=[jax.ShapeDtypeStruct(shape, w_3.dtype)] * count,
        in_specs=[pl.BlockSpec(memory_space=pltpu.SMEM)]
        + [pl.BlockSpec(memory_space=pl.ANY)] * (2 + len(after)),
        out_specs=[pl.BlockSpec(memory_space=pl.ANY)] * count,
        scratch_shapes=[
            pltpu.VMEM((3,) + shape, w_3.dtype),
            pltpu.SemaphoreType.DMA((3,)),
            pltpu.SemaphoreType.DMA((count,)),
        ],
        compiler_params=pltpu.CompilerParams(vmem_limit_bytes=LIMIT),
        cost_estimate=pl.CostEstimate(
            flops=0, bytes_accessed=2 * (3 + count) * w_3.size, transcendentals=0
        ),
        name="reorder",
    )(order, w_12, w_3, *after)


def stack_kernel(first, count, *refs):
    sources, (stack_ref, token, sem) = refs[-3 - count : -3], refs[-3:]
    rows = sources[0].shape[-2]
    copies, at = [], 0
    for source in sources:
        parts = [source] if len(source.shape) == 3 else [source.at[0], source.at[1]]
        for part in parts:
            to = stack_ref.at[:, pl.ds((first + at) * rows, rows)]
            copies.append(pltpu.make_async_copy(part, to, sem.at[at]))
            at += 1
    for copy in copies:
        copy.start()
    token[...] = jnp.zeros_like(token)
    for copy in copies:
        copy.wait()


def stack(first, blocks, before=None):
    tiles, rows, lanes = blocks[0].shape[-3:]
    shape = (tiles, 16 * rows, lanes)
    held = [] if before is None else [pltpu.with_memory_space_constraint(before, pltpu.VMEM)]
    count = sum(block.size for block in blocks) // (tiles * rows * lanes)
    return pl.pallas_call(
        functools.partial(stack_kernel, first, len(blocks)),
        out_shape=[
            pltpu.VMEM(shape, blocks[0].dtype),
            jax.ShapeDtypeStruct((8, LANES), jnp.float32),
        ],
        in_specs=[pl.BlockSpec(memory_space=pltpu.VMEM)] * len(held)
        + [pl.BlockSpec(memory_space=pl.ANY)] * len(blocks),
        out_specs=[pl.BlockSpec(memory_space=pltpu.VMEM)] * 2,
        scratch_shapes=[pltpu.SemaphoreType.DMA((count,))],
        input_output_aliases={0: 0} if held else {},
        compiler_params=pltpu.CompilerParams(vmem_limit_bytes=LIMIT),
        cost_estimate=pl.CostEstimate(
            flops=0, bytes_accessed=4 * count * tiles * rows * lanes, transcendentals=0
        ),
        name="stack",
    )(*held, *blocks)


def product_kernel(places, w_at, choice_ref, a, *refs):
    groups, wide = len(places), len(w_at[0])
    outs, (w, w_sem) = refs[-2 - groups : -2], refs[-2:]
    tiles, _, columns = w.shape
    columns //= wide
    rows = a.shape[1] // 16

    def pick(at):
        ref, index = at
        return refs[ref] if index is None else refs[ref].at[index]

    def w_copy(at, choice):
        return pltpu.make_async_copy(
            pick(w_at[choice][at]), w.at[:, :, pl.ds(at * columns, columns)], w_sem.at[at]
        )

    for at in range(wide):
        for choice in range(len(w_at)):

            @pl.when(choice_ref[0] == choice)
            def _():
                w_copy(at, choice).start()

    for at in range(wide):
        w_copy(at, 0).wait()
    right = w[...].reshape(tiles * LANES, wide * columns)
    for place, out in zip(places, outs):
        for half in range(2):
            here = [(place[2 * half + at], at) for at in range(2)]
            left = jnp.concatenate(
                [
                    jnp.concatenate(
                        [a[tile, pl.ds(block * rows, rows)] for tile in range(tiles)], axis=1
                    )
                    for block, _ in here
                ],
                axis=0,
            )
            total = jnp.dot(left, right, preferred_element_type=jnp.float32)
            for _, at in here:
                out[2 * half + at] = total[at * rows : (at + 1) * rows].astype(out.dtype)


def product(choice, groups, places, rows_stack, w_choices, after=()):
    arrays = []

    def at(block):
        array, index = block
        for known, other in enumerate(arrays):
            if other is array:
                return known, index
        arrays.append(array)
        return len(arrays) - 1, index

    w_at = [[at(block) for block in blocks] for blocks in w_choices]
    tiles, rows, _ = rows_stack.shape
    rows //= 16
    columns = w_choices[-1][0][0].shape[-1]
    wide = len(w_choices[0])
    shape = (4, rows, wide * columns)
    count = len(arrays) + len(after)
    return pl.pallas_call(
        functools.partial(product_kernel, [places[group] for group in groups], w_at),
        out_shape=[
            jax.ShapeDtypeStruct(shape, jnp.float32 if group == 0 else jnp.bfloat16)
            for group in groups
        ],
        in_specs=[
            pl.BlockSpec(memory_space=pltpu.SMEM),
            pl.BlockSpec(memory_space=pltpu.VMEM),
        ]
        + [pl.BlockSpec(memory_space=pl.ANY)] * count,
        out_specs=[pl.BlockSpec(memory_space=pltpu.VMEM)] * len(groups),
        scratch_shapes=[
            pltpu.VMEM((tiles, LANES, wide * columns), jnp.bfloat16),
            pltpu.SemaphoreType.DMA((wide,)),
        ],
        compiler_params=pltpu.CompilerParams(vmem_limit_bytes=LIMIT),
        cost_estimate=pl.CostEstimate(
            flops=8 * len(groups) * rows * tiles * LANES * wide * columns,
            bytes_accessed=2 * tiles * LANES * (4 * len(groups) * rows + wide * columns),
            transcendentals=0,
        ),
        name="product",
    )(choice, pltpu.with_memory_space_constraint(rows_stack, pltpu.VMEM), *arrays, *after)


def add_kernel(relative, own, one, two, three, *refs):
    blocks_wide, outs = own.shape[2] // LANES, refs[-4:]
    for piece in range(4):
        for at in range(blocks_wide):
            here = pl.ds(at * LANES, LANES)
            total = own[piece, :, here]
            for step, ref in ((1, one), (2, two), (3, three)):
                source = at ^ step if relative else at
                total += ref[piece, :, pl.ds(source * LANES, LANES)].astype(jnp.float32)
            outs[piece][:, here] = total.astype(jnp.bfloat16)


def add(own, others, relative, after=()):
    _, rows, columns = own.shape
    return pl.pallas_call(
        functools.partial(add_kernel, relative),
        out_shape=[jax.ShapeDtypeStruct((rows, columns), jnp.bfloat16)] * 4,
        in_specs=[pl.BlockSpec(memory_space=pltpu.VMEM)] * 4
        + [pl.BlockSpec(memory_space=pl.ANY)] * len(after),
        out_specs=[pl.BlockSpec(memory_space=pltpu.VMEM)] * 4,
        compiler_params=pltpu.CompilerParams(vmem_limit_bytes=LIMIT),
        cost_estimate=pl.CostEstimate(
            flops=12 * rows * columns, bytes_accessed=48 * rows * columns, transcendentals=0
        ),
        name="add",
    )(own, *others, *after)


def assemble_kernel(groups, place_ref, *refs):
    out = refs[-1]
    for ref, (fixed, first, relative) in zip(refs, groups):
        place = place_ref[0] if relative else place_ref[1]
        for at in range(ref.shape[1] // LANES):
            index = fixed | ((first + at) << 1)
            to = pl.multiple_of((place ^ index) * LANES, LANES)
            out[:, pl.ds(to, LANES)] = ref[:, pl.ds(at * LANES, LANES)]


def assemble(place, pieces):
    arrays = [piece[0] for piece in pieces]
    rows = arrays[0].shape[0]
    columns = sum(array.shape[1] for array in arrays)
    return pl.pallas_call(
        functools.partial(assemble_kernel, [piece[1:] for piece in pieces]),
        out_shape=jax.ShapeDtypeStruct((rows, columns), jnp.bfloat16),
        in_specs=[pl.BlockSpec(memory_space=pltpu.SMEM)]
        + [pl.BlockSpec(memory_space=pltpu.VMEM)] * len(arrays),
        out_specs=pl.BlockSpec(memory_space=pltpu.VMEM),
        compiler_params=pltpu.CompilerParams(vmem_limit_bytes=LIMIT),
        name="assemble",
    )(place, *arrays)


def blocks(gate_pre, up_pre, down_weight):
    n = lax.axis_size("fsdp")
    me = lax.axis_index("fsdp")
    plane = (me // PLANE) % 4
    z_low, z_high = (me // PAIR) % 2, me // (2 * PAIR)
    at_plane = plane.astype(jnp.int32).reshape(1)
    inputs = [
        pltpu.with_memory_space_constraint(array, pltpu.HBM)
        for array in (gate_pre, up_pre, down_weight)
    ]

    def send(array, perm):
        return lax.ppermute(array, "fsdp", perm=perm)

    def to_mid(array):
        return send(array, along_z(n, [(1, 2), (2, 1)]))

    def to_next(array):
        return send(array, along_z(n, [(1, 0), (3, 1), (0, 2), (2, 3)]))

    def to_core(array):
        return send(array, flip(n, CORE))

    def to_pair(array):
        return send(array, flip(n, PAIR))

    a_0, w_0, packed_1, packed_2 = pack(at_plane, (0, 1, 2), *inputs, 1)
    pair_0, mid_0, next_0 = to_pair(a_0), to_mid(w_0), to_next(w_0)
    got_1 = send(packed_1, flip(n, PLANE))
    got_2 = send(packed_2, flip(n, 2 * PLANE))

    sent_a, sent_w = pack(at_plane, (3,), *inputs, 1, after=(pair_0,))
    sent_a, sent_w, got_1, got_2 = lax.optimization_barrier((sent_a, sent_w, got_1, got_2))
    a_3, w_3 = send(sent_a, flip(n, 3 * PLANE)), send(sent_w, flip(n, 3 * PLANE))
    core_0, core_pair_0 = to_core(a_0), to_core(pair_0)
    a_12, w_12 = unpack_pair(got_1, got_2, (mid_0, next_0, core_0, core_pair_0))
    pair_12, mid_12 = to_pair(a_12), to_mid(w_12)

    order = jnp.array([[0, 1, 2], [0, 2, 1], [1, 2, 0], [2, 1, 0]], jnp.int32)[plane]
    rows_stack, token = stack(0, [a_0, pair_0, core_0, core_pair_0])
    a_3, w_3, a_12, mid_12, _ = lax.optimization_barrier((a_3, w_3, a_12, mid_12, token))
    pair_3, mid_3 = to_pair(a_3), to_mid(w_3)
    core_12, core_pair_12 = to_core(a_12), to_core(pair_12)
    (ordered_1,) = reorder(order[:1], w_12, w_3)
    rows_stack, token = stack(4, [a_12, pair_12, core_12, core_pair_12], rows_stack)
    ordered_2, ordered_3 = reorder(order[1:], w_12, w_3, after=(pair_3, mid_3, token))
    next_1, next_2, next_3 = to_next(ordered_1), to_next(ordered_2), to_next(ordered_3)
    pair_3, token, _ = lax.optimization_barrier((pair_3, token, ordered_1))
    core_3, core_pair_3 = to_core(a_3), to_core(pair_3)

    rows_stack, _ = stack(12, [a_3, pair_3, core_3, core_pair_3], rows_stack)
    places = [(0, 2, 1, 3), (4, 8, 6, 10), (5, 9, 7, 11), (12, 14, 13, 15)]
    w_own = [(w_0, None), (w_12, 0), (w_12, 1), (w_3, None)]
    w_mid = [(mid_0, None), (mid_12, 0), (mid_12, 1), (mid_3, None)]
    mid = (z_low ^ z_high).astype(jnp.int32).reshape(1)

    def totals_of(choice, w_choices, calls, after=()):
        totals = {}
        for groups in calls:
            outs = product(choice, groups, places, rows_stack, w_choices, after)
            totals.update(zip(groups, outs))
            after = (outs[0],)
        return [totals[group] for group in range(4)]

    def across_plane(totals):
        return [send(totals[step], flip(n, step * PLANE)) for step in (1, 2, 3)]

    pieces = []

    def spread(totals, others, half, start, after=()):
        summed = add(totals[0], others, half == 0, after)
        for piece in range(4):
            mask = (piece >> 1) * PAIR + (piece & 1) * CORE
            block = send(summed[piece], flip(n, mask)) if mask else summed[piece]
            fixed = ((piece >> 1) << 4) | (half << 3) | (piece & 1)
            pieces.append((block, fixed, start, half == 0))
        return summed[0]

    own = totals_of(mid, [w_own, w_mid], ([3, 1, 2], [0]))
    own[1], own[2], own[3], next_1 = lax.optimization_barrier((*own[1:], next_1))
    own_sums = across_plane(own)
    first, one, two, three = [(block, None) for block in (next_0, next_1, next_2, next_3)]
    w_low = [[first, one], [one, first], [one, two], [one, two]]
    w_high = [[two, three], [two, three], [first, three], [three, first]]
    low = totals_of(at_plane, w_low, ([3, 1, 2, 0],), (*own_sums, own[0]))
    low_sums = across_plane(low)
    summed = spread(own, own_sums, 0, 0, (low[0],))
    high = totals_of(at_plane, w_high, ([3, 1, 2], [0]), (*low_sums, summed))
    high_sums = across_plane(high)
    spread(low, low_sums, 1, 0, (high[0],))
    spread(high, high_sums, 1, 2)
    across = z_low * 16 + z_high * 8 + me % 2
    place = jnp.stack([across + plane * 2, across]).astype(jnp.int32)
    return assemble(place, pieces)


def shards(gate_pre, up_pre, down_weight):
    hidden = silu_product(gate_pre, up_pre)
    terms = jnp.dot(
        hidden,
        lax.all_gather(down_weight, "fsdp", axis=1, tiled=True),
        preferred_element_type=jnp.float32,
    )
    totals = lax.psum(terms, "tp")
    share = totals.shape[1] // lax.axis_size("tp")
    result = lax.dynamic_slice_in_dim(totals, lax.axis_index("tp") * share, share, 1)
    return result.astype(jnp.bfloat16)


def solution(mesh):
    in_blocks = mesh.shape["tp"] == 1 and mesh.shape["fsdp"] == 4 * PAIR
    return jax.shard_map(
        blocks if in_blocks else shards,
        mesh=mesh,
        in_specs=(P("fsdp", "tp"), P("fsdp", "tp"), P("tp", "fsdp")),
        out_specs=P("fsdp", "tp"),
        check_vma=False,
    )
```

```python
import functools

import jax
import jax.numpy as jnp
from jax import lax
from jax.experimental import pallas as pl
from jax.experimental.pallas import tpu as pltpu
from jax.sharding import PartitionSpec as P

CORE, PLANE, PAIR = 1, 2, 8
LIMIT = 10 * 1024 * 1024
LANES = 128


def flip(n, mask):
    return [(source, source ^ mask) for source in range(n)]


def along_z(n, pairs):
    low = PAIR
    return [(a * low + rest, b * low + rest) for a, b in pairs for rest in range(low)]


def silu_product(gate, up):
    return (jax.nn.silu(gate.astype(jnp.float32)) * up.astype(jnp.float32)).astype(jnp.bfloat16)


def pack_kernel(apart, count, plane_ref, *refs):
    outs = refs[len(refs) - count - apart :]
    pairs = [(outs[0], outs[1])] if apart else []
    pairs += [(out.at[0], out.at[1]) for out in outs[2 * apart :]]
    for at, (a, w) in enumerate(pairs):
        gate, up, weight = refs[3 * at : 3 * at + 3]
        hidden = silu_product(gate[...], up[...])
        for tile in range(a.shape[0]):
            a[tile] = hidden[:, tile * LANES : (tile + 1) * LANES]
            w[tile] = weight[pl.ds(tile * LANES, LANES)]


def pack(plane, steps, gate, up, weight, after=()):
    rows, columns = gate.shape[0], weight.shape[1]
    tiles = gate.shape[1] // (4 * LANES)
    grid = 4
    share = tiles // grid
    apart = int(steps[0] == 0)
    single = jax.ShapeDtypeStruct((tiles, rows, LANES), jnp.bfloat16)
    double = jax.ShapeDtypeStruct((2, tiles, rows, LANES), jnp.bfloat16)
    single_spec = pl.BlockSpec((share, rows, LANES), lambda at, plane: (at, 0, 0))
    double_spec = pl.BlockSpec((2, share, rows, LANES), lambda at, plane: (0, at, 0, 0))
    others = len(steps) - apart
    in_specs = []
    for step in steps:

        def across(at, plane, step=step):
            return 0, (plane[0] ^ step) * grid + at

        def down(at, plane, step=step):
            return (plane[0] ^ step) * grid + at, 0

        wide = pl.BlockSpec((rows, share * LANES), across)
        in_specs += [wide, wide, pl.BlockSpec((share * LANES, columns), down)]
    in_specs += [pl.BlockSpec(memory_space=pl.ANY)] * len(after)
    return pl.pallas_call(
        functools.partial(pack_kernel, apart, len(steps)),
        out_shape=[single] * (2 * apart) + [double] * others,
        grid_spec=pltpu.PrefetchScalarGridSpec(
            num_scalar_prefetch=1,
            grid=(grid,),
            in_specs=in_specs,
            out_specs=[single_spec] * (2 * apart) + [double_spec] * others,
        ),
        compiler_params=pltpu.CompilerParams(vmem_limit_bytes=LIMIT),
        cost_estimate=pl.CostEstimate(
            flops=0,
            bytes_accessed=10 * rows * tiles * LANES * len(steps),
            transcendentals=rows * tiles * LANES * len(steps),
        ),
        name="pack",
    )(plane, *[gate, up, weight] * len(steps), *after)


def unpack_pair_kernel(one, two, *refs):
    a, w, held, in_sem, out_sem = refs[-5:]
    ways = [
        (source.at[kind], out.at[at])
        for at, source in enumerate((one, two))
        for kind, out in enumerate((a, w))
    ]
    into = [
        pltpu.make_async_copy(source, held.at[at], in_sem.at[at])
        for at, (source, _) in enumerate(ways)
    ]
    out_of = [
        pltpu.make_async_copy(held.at[at], to, out_sem.at[at]) for at, (_, to) in enumerate(ways)
    ]
    for copy in into:
        copy.start()
    for copy_in, copy_out in zip(into, out_of):
        copy_in.wait()
        copy_out.start()
    for copy in out_of:
        copy.wait()


def unpack_pair(one, two, after):
    return pl.pallas_call(
        unpack_pair_kernel,
        out_shape=[jax.ShapeDtypeStruct(one.shape, one.dtype)] * 2,
        in_specs=[pl.BlockSpec(memory_space=pl.ANY)] * (2 + len(after)),
        out_specs=[pl.BlockSpec(memory_space=pl.ANY)] * 2,
        scratch_shapes=[
            pltpu.VMEM((4,) + one.shape[1:], one.dtype),
            pltpu.SemaphoreType.DMA((4,)),
            pltpu.SemaphoreType.DMA((4,)),
        ],
        compiler_params=pltpu.CompilerParams(vmem_limit_bytes=LIMIT),
        cost_estimate=pl.CostEstimate(flops=0, bytes_accessed=8 * one.size, transcendentals=0),
        name="unpack_pair",
    )(one, two, *after)


def reorder_kernel(count, order_ref, packed, w_12, *refs):
    outs, (held, in_sem, out_sem) = refs[-3 - count : -3], refs[-3:]
    into = [
        pltpu.make_async_copy(source, held.at[at], in_sem.at[at])
        for at, source in enumerate((packed.at[0], w_12.at[0], w_12.at[1], packed.at[1]))
    ]
    out_of = [
        pltpu.make_async_copy(held.at[order_ref[at]], out, out_sem.at[at])
        for at, out in enumerate(outs)
    ]
    for copy in into:
        copy.start()
    for copy in into:
        copy.wait()
    for copy in out_of:
        copy.start()
    for copy in out_of:
        copy.wait()


def reorder(order, packed, w_12, after):
    shape, count = packed.shape[1:], order.shape[0]
    return pl.pallas_call(
        functools.partial(reorder_kernel, count),
        out_shape=[jax.ShapeDtypeStruct(shape, packed.dtype)] * count,
        in_specs=[pl.BlockSpec(memory_space=pltpu.SMEM)]
        + [pl.BlockSpec(memory_space=pl.ANY)] * (2 + len(after)),
        out_specs=[pl.BlockSpec(memory_space=pl.ANY)] * count,
        scratch_shapes=[
            pltpu.VMEM((4,) + shape, packed.dtype),
            pltpu.SemaphoreType.DMA((4,)),
            pltpu.SemaphoreType.DMA((count,)),
        ],
        compiler_params=pltpu.CompilerParams(vmem_limit_bytes=LIMIT),
        cost_estimate=pl.CostEstimate(flops=0, bytes_accessed=8 * packed.size, transcendentals=0),
        name="reorder",
    )(order, packed, w_12, *after)


def stack_kernel(first, count, *refs):
    sources, stack_ref, sem = refs[-2 - count : -2], refs[-2], refs[-1]
    rows = sources[0].shape[-2]
    copies, at = [], 0
    for source in sources:
        parts = [source] if len(source.shape) == 3 else [source.at[0], source.at[1]]
        for part in parts:
            to = stack_ref.at[:, pl.ds((first + at) * rows, rows)]
            copies.append(pltpu.make_async_copy(part, to, sem.at[at]))
            at += 1
    for copy in copies:
        copy.start()
    for copy in copies:
        copy.wait()


def stack(first, blocks, before=None):
    tiles, rows, lanes = blocks[0].shape[-3:]
    shape = (tiles, 16 * rows, lanes)
    held = [] if before is None else [pltpu.with_memory_space_constraint(before, pltpu.VMEM)]
    count = sum(block.size for block in blocks) // (tiles * rows * lanes)
    return pl.pallas_call(
        functools.partial(stack_kernel, first, len(blocks)),
        out_shape=pltpu.VMEM(shape, blocks[0].dtype),
        in_specs=[pl.BlockSpec(memory_space=pltpu.VMEM)] * len(held)
        + [pl.BlockSpec(memory_space=pl.ANY)] * len(blocks),
        out_specs=pl.BlockSpec(memory_space=pltpu.VMEM),
        scratch_shapes=[pltpu.SemaphoreType.DMA((count,))],
        input_output_aliases={0: 0} if held else {},
        compiler_params=pltpu.CompilerParams(vmem_limit_bytes=LIMIT),
        cost_estimate=pl.CostEstimate(
            flops=0, bytes_accessed=4 * count * tiles * rows * lanes, transcendentals=0
        ),
        name="stack",
    )(*held, *blocks)


def product_kernel(places, w_at, choice_ref, a, *refs):
    groups, wide = len(places), len(w_at[0])
    outs, (w, w_sem) = refs[-2 - groups : -2], refs[-2:]
    tiles, _, columns = w.shape
    columns //= wide
    rows = a.shape[1] // 16

    def pick(at):
        ref, index = at
        return refs[ref] if index is None else refs[ref].at[index]

    def w_copy(at, choice):
        return pltpu.make_async_copy(
            pick(w_at[choice][at]), w.at[:, :, pl.ds(at * columns, columns)], w_sem.at[at]
        )

    for at in range(wide):
        for choice in range(len(w_at)):

            @pl.when(choice_ref[0] == choice)
            def _():
                w_copy(at, choice).start()

    for at in range(wide):
        w_copy(at, 0).wait()
    right = w[...].reshape(tiles * LANES, wide * columns)
    for place, out in zip(places, outs):
        for half in range(2):
            here = [(place[2 * half + at], at) for at in range(2)]
            left = jnp.concatenate(
                [
                    jnp.concatenate(
                        [a[tile, pl.ds(block * rows, rows)] for tile in range(tiles)], axis=1
                    )
                    for block, _ in here
                ],
                axis=0,
            )
            total = jnp.dot(left, right, preferred_element_type=jnp.float32)
            for _, at in here:
                out[2 * half + at] = total[at * rows : (at + 1) * rows].astype(out.dtype)


def product(choice, groups, places, rows_stack, w_choices, after=()):
    arrays = []

    def at(block):
        array, index = block
        for known, other in enumerate(arrays):
            if other is array:
                return known, index
        arrays.append(array)
        return len(arrays) - 1, index

    w_at = [[at(block) for block in blocks] for blocks in w_choices]
    tiles, rows, _ = rows_stack.shape
    rows //= 16
    columns = w_choices[-1][0][0].shape[-1]
    wide = len(w_choices[0])
    shape = (4, rows, wide * columns)
    count = len(arrays) + len(after)
    return pl.pallas_call(
        functools.partial(product_kernel, [places[group] for group in groups], w_at),
        out_shape=[
            jax.ShapeDtypeStruct(shape, jnp.float32 if group == 0 else jnp.bfloat16)
            for group in groups
        ],
        in_specs=[
            pl.BlockSpec(memory_space=pltpu.SMEM),
            pl.BlockSpec(memory_space=pltpu.VMEM),
        ]
        + [pl.BlockSpec(memory_space=pl.ANY)] * count,
        out_specs=[pl.BlockSpec(memory_space=pltpu.VMEM)] * len(groups),
        scratch_shapes=[
            pltpu.VMEM((tiles, LANES, wide * columns), jnp.bfloat16),
            pltpu.SemaphoreType.DMA((wide,)),
        ],
        compiler_params=pltpu.CompilerParams(vmem_limit_bytes=LIMIT),
        cost_estimate=pl.CostEstimate(
            flops=8 * len(groups) * rows * tiles * LANES * wide * columns,
            bytes_accessed=2 * tiles * LANES * (4 * len(groups) * rows + wide * columns),
            transcendentals=0,
        ),
        name="product",
    )(choice, pltpu.with_memory_space_constraint(rows_stack, pltpu.VMEM), *arrays, *after)


def add_kernel(relative, own, one, two, three, *refs):
    blocks_wide, outs = own.shape[2] // LANES, refs[-4:]
    for piece in range(4):
        for at in range(blocks_wide):
            here = pl.ds(at * LANES, LANES)
            total = own[piece, :, here]
            for step, ref in ((1, one), (2, two), (3, three)):
                source = at ^ step if relative else at
                total += ref[piece, :, pl.ds(source * LANES, LANES)].astype(jnp.float32)
            outs[piece][:, here] = total.astype(jnp.bfloat16)


def add(own, others, relative, after=()):
    _, rows, columns = own.shape
    return pl.pallas_call(
        functools.partial(add_kernel, relative),
        out_shape=[jax.ShapeDtypeStruct((rows, columns), jnp.bfloat16)] * 4,
        in_specs=[pl.BlockSpec(memory_space=pltpu.VMEM)] * 4
        + [pl.BlockSpec(memory_space=pl.ANY)] * len(after),
        out_specs=[pl.BlockSpec(memory_space=pltpu.VMEM)] * 4,
        compiler_params=pltpu.CompilerParams(vmem_limit_bytes=LIMIT),
        cost_estimate=pl.CostEstimate(
            flops=12 * rows * columns, bytes_accessed=48 * rows * columns, transcendentals=0
        ),
        name="add",
    )(own, *others, *after)


def assemble_kernel(groups, place_ref, *refs):
    out = refs[-1]
    for ref, (fixed, first, relative) in zip(refs, groups):
        place = place_ref[0] if relative else place_ref[1]
        for at in range(ref.shape[1] // LANES):
            index = fixed | ((first + at) << 1)
            to = pl.multiple_of((place ^ index) * LANES, LANES)
            out[:, pl.ds(to, LANES)] = ref[:, pl.ds(at * LANES, LANES)]


def assemble(place, pieces):
    arrays = [piece[0] for piece in pieces]
    rows = arrays[0].shape[0]
    columns = sum(array.shape[1] for array in arrays)
    return pl.pallas_call(
        functools.partial(assemble_kernel, [piece[1:] for piece in pieces]),
        out_shape=jax.ShapeDtypeStruct((rows, columns), jnp.bfloat16),
        in_specs=[pl.BlockSpec(memory_space=pltpu.SMEM)]
        + [pl.BlockSpec(memory_space=pltpu.VMEM)] * len(arrays),
        out_specs=pl.BlockSpec(memory_space=pltpu.VMEM),
        compiler_params=pltpu.CompilerParams(vmem_limit_bytes=LIMIT),
        name="assemble",
    )(place, *arrays)


def blocks(gate_pre, up_pre, down_weight):
    n = lax.axis_size("fsdp")
    me = lax.axis_index("fsdp")
    plane = (me // PLANE) % 4
    z_low, z_high = (me // PAIR) % 2, me // (2 * PAIR)
    at_plane = plane.astype(jnp.int32).reshape(1)
    inputs = [
        pltpu.with_memory_space_constraint(array, pltpu.HBM)
        for array in (gate_pre, up_pre, down_weight)
    ]

    def send(array, perm):
        return lax.ppermute(array, "fsdp", perm=perm)

    def to_mid(array):
        return send(array, along_z(n, [(1, 2), (2, 1)]))

    def to_next(array):
        return send(array, along_z(n, [(1, 0), (3, 1), (0, 2), (2, 3)]))

    def to_core(array):
        return send(array, flip(n, CORE))

    def to_pair(array):
        return send(array, flip(n, PAIR))

    a_0, w_0, packed_1, packed_2 = pack(at_plane, (0, 1, 2), *inputs)
    pair_0, mid_0, next_0 = to_pair(a_0), to_mid(w_0), to_next(w_0)
    got_1 = send(packed_1, flip(n, PLANE))
    got_2 = send(packed_2, flip(n, 2 * PLANE))

    (packed_3,) = pack(at_plane, (3,), *inputs, after=(pair_0,))
    packed_3, got_1, got_2 = lax.optimization_barrier((packed_3, got_1, got_2))
    got_3 = send(packed_3, flip(n, 3 * PLANE))
    a_12, w_12 = unpack_pair(got_1, got_2, after=(pair_0, mid_0, next_0))
    pair_12, mid_12 = to_pair(a_12), to_mid(w_12)
    core_0, core_pair_0 = to_core(a_0), to_core(pair_0)

    order = jnp.array([[1, 2, 3], [1, 3, 2], [2, 3, 1], [3, 2, 1]], jnp.int32)[plane]
    a_12, got_3 = lax.optimization_barrier((a_12, got_3))
    known = jnp.array([0, 3], jnp.int32)
    a_3, w_3, ordered_1 = reorder(
        jnp.concatenate([known, order[:1]]), got_3, w_12, after=(core_0, core_pair_0, mid_12)
    )
    pair_3, mid_3 = to_pair(a_3), to_mid(w_3)
    core_12, core_pair_12 = to_core(a_12), to_core(pair_12)
    rows_stack = stack(0, [a_0, pair_0, core_0, core_pair_0])
    rows_stack = stack(4, [a_12, pair_12, core_12, core_pair_12], rows_stack)
    pair_3, mid_3, rows_stack = lax.optimization_barrier((pair_3, mid_3, rows_stack))
    ordered_2, ordered_3 = reorder(
        order[1:], got_3, w_12, after=(pair_3, mid_3, core_12, core_pair_12)
    )
    next_1, next_2, next_3 = to_next(ordered_1), to_next(ordered_2), to_next(ordered_3)
    core_3, core_pair_3 = to_core(a_3), to_core(pair_3)

    rows_stack = stack(12, [a_3, pair_3, core_3, core_pair_3], rows_stack)
    places = [(0, 2, 1, 3), (4, 8, 6, 10), (5, 9, 7, 11), (12, 14, 13, 15)]
    w_own = [(w_0, None), (w_12, 0), (w_12, 1), (w_3, None)]
    w_mid = [(mid_0, None), (mid_12, 0), (mid_12, 1), (mid_3, None)]
    mid = (z_low ^ z_high).astype(jnp.int32).reshape(1)

    def totals_of(choice, w_choices, calls, after=()):
        totals = {}
        for groups in calls:
            outs = product(choice, groups, places, rows_stack, w_choices, after)
            totals.update(zip(groups, outs))
            after = (outs[0],)
        return [totals[group] for group in range(4)]

    def across_plane(totals):
        return [send(totals[step], flip(n, step * PLANE)) for step in (1, 2, 3)]

    pieces = []

    def spread(totals, others, half, start, after=()):
        summed = add(totals[0], others, half == 0, after)
        for piece in range(4):
            mask = (piece >> 1) * PAIR + (piece & 1) * CORE
            block = send(summed[piece], flip(n, mask)) if mask else summed[piece]
            fixed = ((piece >> 1) << 4) | (half << 3) | (piece & 1)
            pieces.append((block, fixed, start, half == 0))
        return summed[0]

    own = totals_of(mid, [w_own, w_mid], ([3, 1, 2], [0]))
    own[1], own[2], own[3], next_1 = lax.optimization_barrier((*own[1:], next_1))
    own_sums = across_plane(own)
    first, one, two, three = [(block, None) for block in (next_0, next_1, next_2, next_3)]
    w_low = [[first, one], [one, first], [one, two], [one, two]]
    w_high = [[two, three], [two, three], [first, three], [three, first]]
    low = totals_of(at_plane, w_low, ([3, 1, 2, 0],), (*own_sums, own[0]))
    low_sums = across_plane(low)
    summed = spread(own, own_sums, 0, 0, (low[0],))
    high = totals_of(at_plane, w_high, ([3, 1, 2], [0]), (*low_sums, summed))
    high_sums = across_plane(high)
    spread(low, low_sums, 1, 0, (high[0],))
    spread(high, high_sums, 1, 2)
    across = z_low * 16 + z_high * 8 + me % 2
    place = jnp.stack([across + plane * 2, across]).astype(jnp.int32)
    return assemble(place, pieces)


def shards(gate_pre, up_pre, down_weight):
    hidden = silu_product(gate_pre, up_pre)
    terms = jnp.dot(
        hidden,
        lax.all_gather(down_weight, "fsdp", axis=1, tiled=True),
        preferred_element_type=jnp.float32,
    )
    totals = lax.psum(terms, "tp")
    share = totals.shape[1] // lax.axis_size("tp")
    result = lax.dynamic_slice_in_dim(totals, lax.axis_index("tp") * share, share, 1)
    return result.astype(jnp.bfloat16)


def solution(mesh):
    in_blocks = mesh.shape["tp"] == 1 and mesh.shape["fsdp"] == 4 * PAIR
    return jax.shard_map(
        blocks if in_blocks else shards,
        mesh=mesh,
        in_specs=(P("fsdp", "tp"), P("fsdp", "tp"), P("tp", "fsdp")),
        out_specs=P("fsdp", "tp"),
        check_vma=False,
    )
```

```python
import functools

import jax
import jax.numpy as jnp
from jax import lax
from jax.experimental import pallas as pl
from jax.experimental.pallas import tpu as pltpu
from jax.sharding import PartitionSpec as P

CORE, PLANE, PAIR = 1, 2, 8
LIMIT = 10 * 1024 * 1024
LANES = 128


def flip(n, mask):
    return [(source, source ^ mask) for source in range(n)]


def along_z(n, pairs):
    low = PAIR
    return [(a * low + rest, b * low + rest) for a, b in pairs for rest in range(low)]


def silu_product(gate, up):
    return (jax.nn.silu(gate.astype(jnp.float32)) * up.astype(jnp.float32)).astype(jnp.bfloat16)


def pack_kernel(apart, count, plane_ref, *refs):
    outs = refs[len(refs) - count - apart :]
    pairs = [(outs[0], outs[1])] if apart else []
    pairs += [(out.at[0], out.at[1]) for out in outs[2 * apart :]]
    for at, (a, w) in enumerate(pairs):
        gate, up, weight = refs[3 * at : 3 * at + 3]
        hidden = silu_product(gate[...], up[...])
        for tile in range(a.shape[0]):
            a[tile] = hidden[:, tile * LANES : (tile + 1) * LANES]
            w[tile] = weight[pl.ds(tile * LANES, LANES)]


def pack(plane, steps, gate, up, weight, after=()):
    rows, columns = gate.shape[0], weight.shape[1]
    tiles = gate.shape[1] // (4 * LANES)
    grid = 4
    share = tiles // grid
    apart = int(steps[0] == 0)
    single = pltpu.HBM((tiles, rows, LANES), jnp.bfloat16)
    double = pltpu.HBM((2, tiles, rows, LANES), jnp.bfloat16)
    single_spec = pl.BlockSpec((share, rows, LANES), lambda at, plane: (at, 0, 0))
    double_spec = pl.BlockSpec((2, share, rows, LANES), lambda at, plane: (0, at, 0, 0))
    others = len(steps) - apart
    in_specs = []
    for step in steps:

        def across(at, plane, step=step):
            return 0, (plane[0] ^ step) * grid + at

        def down(at, plane, step=step):
            return (plane[0] ^ step) * grid + at, 0

        wide = pl.BlockSpec((rows, share * LANES), across)
        in_specs += [wide, wide, pl.BlockSpec((share * LANES, columns), down)]
    in_specs += [pl.BlockSpec(memory_space=pl.ANY)] * len(after)
    return pl.pallas_call(
        functools.partial(pack_kernel, apart, len(steps)),
        out_shape=[single] * (2 * apart) + [double] * others,
        grid_spec=pltpu.PrefetchScalarGridSpec(
            num_scalar_prefetch=1,
            grid=(grid,),
            in_specs=in_specs,
            out_specs=[single_spec] * (2 * apart) + [double_spec] * others,
        ),
        compiler_params=pltpu.CompilerParams(vmem_limit_bytes=LIMIT),
        cost_estimate=pl.CostEstimate(
            flops=0,
            bytes_accessed=10 * rows * tiles * LANES * len(steps),
            transcendentals=rows * tiles * LANES * len(steps),
        ),
        name="pack",
    )(plane, *[gate, up, weight] * len(steps), *after)


def unpack_pair_kernel(one, two, *refs):
    a, w, held, in_sem, out_sem = refs[-5:]
    ways = [
        (source.at[kind], out.at[at])
        for at, source in enumerate((one, two))
        for kind, out in enumerate((a, w))
    ]
    into = [
        pltpu.make_async_copy(source, held.at[at], in_sem.at[at])
        for at, (source, _) in enumerate(ways)
    ]
    out_of = [
        pltpu.make_async_copy(held.at[at], to, out_sem.at[at]) for at, (_, to) in enumerate(ways)
    ]
    for copy in into:
        copy.start()
    for copy_in, copy_out in zip(into, out_of):
        copy_in.wait()
        copy_out.start()
    for copy in out_of:
        copy.wait()


def unpack_pair(one, two, after):
    return pl.pallas_call(
        unpack_pair_kernel,
        out_shape=[pltpu.HBM(one.shape, one.dtype)] * 2,
        in_specs=[pl.BlockSpec(memory_space=pl.ANY)] * (2 + len(after)),
        out_specs=[pl.BlockSpec(memory_space=pl.ANY)] * 2,
        scratch_shapes=[
            pltpu.VMEM((4,) + one.shape[1:], one.dtype),
            pltpu.SemaphoreType.DMA((4,)),
            pltpu.SemaphoreType.DMA((4,)),
        ],
        compiler_params=pltpu.CompilerParams(vmem_limit_bytes=LIMIT),
        cost_estimate=pl.CostEstimate(flops=0, bytes_accessed=8 * one.size, transcendentals=0),
        name="unpack_pair",
    )(one, two, *after)


def reorder_kernel(count, order_ref, packed, w_12, *refs):
    outs, (held, in_sem, out_sem) = refs[-3 - count : -3], refs[-3:]
    into = [
        pltpu.make_async_copy(source, held.at[at], in_sem.at[at])
        for at, source in enumerate((packed.at[0], w_12.at[0], w_12.at[1], packed.at[1]))
    ]
    out_of = [
        pltpu.make_async_copy(held.at[order_ref[at]], out, out_sem.at[at])
        for at, out in enumerate(outs)
    ]
    for copy in into:
        copy.start()
    for copy in into:
        copy.wait()
    for copy in out_of:
        copy.start()
    for copy in out_of:
        copy.wait()


def reorder(order, packed, w_12, after):
    shape, count = packed.shape[1:], order.shape[0]
    return pl.pallas_call(
        functools.partial(reorder_kernel, count),
        out_shape=[pltpu.HBM(shape, packed.dtype)] * count,
        in_specs=[pl.BlockSpec(memory_space=pltpu.SMEM)]
        + [pl.BlockSpec(memory_space=pl.ANY)] * (2 + len(after)),
        out_specs=[pl.BlockSpec(memory_space=pl.ANY)] * count,
        scratch_shapes=[
            pltpu.VMEM((4,) + shape, packed.dtype),
            pltpu.SemaphoreType.DMA((4,)),
            pltpu.SemaphoreType.DMA((count,)),
        ],
        compiler_params=pltpu.CompilerParams(vmem_limit_bytes=LIMIT),
        cost_estimate=pl.CostEstimate(flops=0, bytes_accessed=8 * packed.size, transcendentals=0),
        name="reorder",
    )(order, packed, w_12, *after)


def far(arrays):
    return [pltpu.with_memory_space_constraint(array, pltpu.HBM) for array in arrays]


def multiply(a, right, place, out):
    tiles, rows = a.shape[0], a.shape[1] // 16
    for half in range(2):
        left = jnp.concatenate(
            [
                jnp.concatenate([a[tile, pl.ds(block * rows, rows)] for tile in range(tiles)], axis=1)
                for block in place[2 * half : 2 * half + 2]
            ],
            axis=0,
        )
        total = jnp.dot(left, right, preferred_element_type=jnp.float32)
        for at in range(2):
            out[2 * half + at] = total[at * rows : (at + 1) * rows].astype(out.dtype)


def stack_product_kernel(places, a_at, w_at, choice_ref, *refs):
    stack_ref, *outs, w, a_sem, w_sem = refs[-7:]
    tiles, _, columns = w.shape
    columns //= len(w_at[0])
    rows = stack_ref.shape[1] // 16

    def pick(at):
        ref, index = at
        return refs[ref] if index is None else refs[ref].at[index]

    def w_copy(at, choice):
        return pltpu.make_async_copy(
            pick(w_at[choice][at]), w.at[:, :, pl.ds(at * columns, columns)], w_sem.at[at]
        )

    def a_copy(at):
        return pltpu.make_async_copy(
            pick(a_at[at]), stack_ref.at[:, pl.ds(at * rows, rows)], a_sem.at[at]
        )

    for at in range(len(w_at[0])):
        for choice in range(len(w_at)):

            @pl.when(choice_ref[0] == choice)
            def _():
                w_copy(at, choice).start()

    for group in (1, 2, 3, 0):
        for at in places[group]:
            a_copy(at).start()
    for at in range(len(w_at[0])):
        w_copy(at, 0).wait()
    right = w[...].reshape(tiles * LANES, len(w_at[0]) * columns)
    for group in (1, 2, 3):
        for at in places[group]:
            a_copy(at).wait()
        multiply(stack_ref, right, places[group], outs[group - 1])
    for at in places[0]:
        a_copy(at).wait()


def stack_product(choice, places, a_blocks, w_choices):
    arrays = []

    def at(block):
        array, index = block
        for known, other in enumerate(arrays):
            if other is array:
                return known, index
        arrays.append(array)
        return len(arrays) - 1, index

    a_at = [at(block) for block in a_blocks]
    w_at = [[at(block) for block in blocks] for blocks in w_choices]
    tiles, rows, _ = a_blocks[0][0].shape
    wide = len(w_choices[0]) * w_choices[0][0][0].shape[-1]
    return pl.pallas_call(
        functools.partial(stack_product_kernel, places, a_at, w_at),
        out_shape=[pltpu.VMEM((tiles, 16 * rows, LANES), jnp.bfloat16)]
        + [jax.ShapeDtypeStruct((4, rows, wide), jnp.bfloat16)] * 3,
        in_specs=[pl.BlockSpec(memory_space=pltpu.SMEM)]
        + [pl.BlockSpec(memory_space=pl.ANY)] * len(arrays),
        out_specs=[pl.BlockSpec(memory_space=pltpu.VMEM)] * 4,
        scratch_shapes=[
            pltpu.VMEM((tiles, LANES, wide), jnp.bfloat16),
            pltpu.SemaphoreType.DMA((16,)),
            pltpu.SemaphoreType.DMA((len(w_at[0]),)),
        ],
        compiler_params=pltpu.CompilerParams(vmem_limit_bytes=LIMIT),
        cost_estimate=pl.CostEstimate(
            flops=24 * rows * tiles * LANES * wide,
            bytes_accessed=2 * tiles * LANES * (16 * rows + wide),
            transcendentals=0,
        ),
        name="stack_product",
    )(choice, *arrays)


def product_kernel(places, w_at, choice_ref, a, *refs):
    groups, wide = len(places), len(w_at[0])
    outs, (w, w_sem) = refs[-2 - groups : -2], refs[-2:]
    tiles, _, columns = w.shape
    columns //= wide

    def pick(at):
        ref, index = at
        return refs[ref] if index is None else refs[ref].at[index]

    def w_copy(at, choice):
        return pltpu.make_async_copy(
            pick(w_at[choice][at]), w.at[:, :, pl.ds(at * columns, columns)], w_sem.at[at]
        )

    for at in range(wide):
        for choice in range(len(w_at)):

            @pl.when(choice_ref[0] == choice)
            def _():
                w_copy(at, choice).start()

    for at in range(wide):
        w_copy(at, 0).wait()
    right = w[...].reshape(tiles * LANES, wide * columns)
    for place, out in zip(places, outs):
        multiply(a, right, place, out)


def product(choice, groups, places, rows_stack, w_choices, after=()):
    arrays = []

    def at(block):
        array, index = block
        for known, other in enumerate(arrays):
            if other is array:
                return known, index
        arrays.append(array)
        return len(arrays) - 1, index

    w_at = [[at(block) for block in blocks] for blocks in w_choices]
    tiles, rows, _ = rows_stack.shape
    rows //= 16
    columns = w_choices[-1][0][0].shape[-1]
    wide = len(w_choices[0])
    shape = (4, rows, wide * columns)
    count = len(arrays) + len(after)
    return pl.pallas_call(
        functools.partial(product_kernel, [places[group] for group in groups], w_at),
        out_shape=[
            jax.ShapeDtypeStruct(shape, jnp.float32 if group == 0 else jnp.bfloat16)
            for group in groups
        ],
        in_specs=[
            pl.BlockSpec(memory_space=pltpu.SMEM),
            pl.BlockSpec(memory_space=pltpu.VMEM),
        ]
        + [pl.BlockSpec(memory_space=pl.ANY)] * count,
        out_specs=[pl.BlockSpec(memory_space=pltpu.VMEM)] * len(groups),
        scratch_shapes=[
            pltpu.VMEM((tiles, LANES, wide * columns), jnp.bfloat16),
            pltpu.SemaphoreType.DMA((wide,)),
        ],
        compiler_params=pltpu.CompilerParams(vmem_limit_bytes=LIMIT),
        cost_estimate=pl.CostEstimate(
            flops=8 * len(groups) * rows * tiles * LANES * wide * columns,
            bytes_accessed=2 * tiles * LANES * (4 * len(groups) * rows + wide * columns),
            transcendentals=0,
        ),
        name="product",
    )(choice, pltpu.with_memory_space_constraint(rows_stack, pltpu.VMEM), *arrays, *after)


def add_kernel(relative, own, one, two, three, *refs):
    blocks_wide, outs = own.shape[2] // LANES, refs[-4:]
    for piece in range(4):
        for at in range(blocks_wide):
            here = pl.ds(at * LANES, LANES)
            total = own[piece, :, here]
            for step, ref in ((1, one), (2, two), (3, three)):
                source = at ^ step if relative else at
                total += ref[piece, :, pl.ds(source * LANES, LANES)].astype(jnp.float32)
            outs[piece][:, here] = total.astype(jnp.bfloat16)


def add(own, others, relative, after=()):
    _, rows, columns = own.shape
    return pl.pallas_call(
        functools.partial(add_kernel, relative),
        out_shape=[jax.ShapeDtypeStruct((rows, columns), jnp.bfloat16)] * 4,
        in_specs=[pl.BlockSpec(memory_space=pltpu.VMEM)] * 4
        + [pl.BlockSpec(memory_space=pl.ANY)] * len(after),
        out_specs=[pl.BlockSpec(memory_space=pltpu.VMEM)] * 4,
        compiler_params=pltpu.CompilerParams(vmem_limit_bytes=LIMIT),
        cost_estimate=pl.CostEstimate(
            flops=12 * rows * columns, bytes_accessed=48 * rows * columns, transcendentals=0
        ),
        name="add",
    )(own, *others, *after)


def assemble_kernel(groups, place_ref, *refs):
    out = refs[-1]
    for ref, (fixed, first, relative) in zip(refs, groups):
        place = place_ref[0] if relative else place_ref[1]
        for at in range(ref.shape[1] // LANES):
            index = fixed | ((first + at) << 1)
            to = pl.multiple_of((place ^ index) * LANES, LANES)
            out[:, pl.ds(to, LANES)] = ref[:, pl.ds(at * LANES, LANES)]


def assemble(place, pieces):
    arrays = [piece[0] for piece in pieces]
    rows = arrays[0].shape[0]
    columns = sum(array.shape[1] for array in arrays)
    return pl.pallas_call(
        functools.partial(assemble_kernel, [piece[1:] for piece in pieces]),
        out_shape=jax.ShapeDtypeStruct((rows, columns), jnp.bfloat16),
        in_specs=[pl.BlockSpec(memory_space=pltpu.SMEM)]
        + [pl.BlockSpec(memory_space=pltpu.VMEM)] * len(arrays),
        out_specs=pl.BlockSpec(memory_space=pltpu.VMEM),
        compiler_params=pltpu.CompilerParams(vmem_limit_bytes=LIMIT),
        name="assemble",
    )(place, *arrays)


def blocks(gate_pre, up_pre, down_weight):
    n = lax.axis_size("fsdp")
    me = lax.axis_index("fsdp")
    plane = (me // PLANE) % 4
    z_low, z_high = (me // PAIR) % 2, me // (2 * PAIR)
    at_plane = plane.astype(jnp.int32).reshape(1)
    inputs = [
        pltpu.with_memory_space_constraint(array, pltpu.HBM)
        for array in (gate_pre, up_pre, down_weight)
    ]

    def send(array, perm):
        return lax.ppermute(array, "fsdp", perm=perm)

    def to_mid(array):
        return send(array, along_z(n, [(1, 2), (2, 1)]))

    def to_next(array):
        return send(array, along_z(n, [(1, 0), (3, 1), (0, 2), (2, 3)]))

    def to_core(array):
        return send(array, flip(n, CORE))

    def to_pair(array):
        return send(array, flip(n, PAIR))

    a_0, w_0, packed_1, packed_2 = pack(at_plane, (0, 1, 2), *inputs)
    pair_0, mid_0, next_0 = to_pair(a_0), to_mid(w_0), to_next(w_0)
    got_1 = send(packed_1, flip(n, PLANE))
    got_2 = send(packed_2, flip(n, 2 * PLANE))

    (packed_3,) = pack(at_plane, (3,), *inputs, after=(pair_0,))
    packed_3, got_1, got_2 = lax.optimization_barrier((packed_3, got_1, got_2))
    got_3 = send(packed_3, flip(n, 3 * PLANE))
    a_12, w_12 = unpack_pair(got_1, got_2, after=(pair_0, mid_0, next_0))
    pair_12, mid_12 = to_pair(a_12), to_mid(w_12)
    core_0, core_pair_0 = to_core(a_0), to_core(pair_0)

    order = jnp.array([[1, 2, 3], [1, 3, 2], [2, 3, 1], [3, 2, 1]], jnp.int32)[plane]
    a_12, got_3 = lax.optimization_barrier((a_12, got_3))
    known = jnp.array([0, 3], jnp.int32)
    a_3, w_3, ordered_1 = reorder(
        jnp.concatenate([known, order[:1]]), got_3, w_12, after=(core_0, core_pair_0, mid_12)
    )
    pair_3, mid_3 = to_pair(a_3), to_mid(w_3)
    core_12, core_pair_12 = to_core(a_12), to_core(pair_12)
    ordered_2, ordered_3 = reorder(
        order[1:], got_3, w_12, after=(pair_3, mid_3, core_12, core_pair_12)
    )
    next_1, next_2, next_3 = to_next(ordered_1), to_next(ordered_2), to_next(ordered_3)
    core_3, core_pair_3 = to_core(a_3), to_core(pair_3)

    a_0, w_0, a_12, w_12, a_3, w_3 = far([a_0, w_0, a_12, w_12, a_3, w_3])
    a_blocks = [(block, None) for block in (a_0, pair_0, core_0, core_pair_0)]
    for block in (a_12, pair_12, core_12, core_pair_12):
        a_blocks += [(block, 0), (block, 1)]
    a_blocks += [(block, None) for block in (a_3, pair_3, core_3, core_pair_3)]
    places = [(0, 2, 1, 3), (4, 8, 6, 10), (5, 9, 7, 11), (12, 14, 13, 15)]
    w_own = [(w_0, None), (w_12, 0), (w_12, 1), (w_3, None)]
    w_mid = [(mid_0, None), (mid_12, 0), (mid_12, 1), (mid_3, None)]
    mid = (z_low ^ z_high).astype(jnp.int32).reshape(1)

    def totals_of(choice, w_choices, calls, after=()):
        totals = {}
        for groups in calls:
            outs = product(choice, groups, places, rows_stack, w_choices, after)
            totals.update(zip(groups, outs))
            after = (outs[0],)
        return [totals[group] for group in sorted(totals)]

    def across_plane(totals):
        return [send(totals[step], flip(n, step * PLANE)) for step in (1, 2, 3)]

    pieces = []

    def spread(totals, others, half, start, after=()):
        summed = add(totals[0], others, half == 0, after)
        for piece in range(4):
            mask = (piece >> 1) * PAIR + (piece & 1) * CORE
            block = send(summed[piece], flip(n, mask)) if mask else summed[piece]
            fixed = ((piece >> 1) << 4) | (half << 3) | (piece & 1)
            pieces.append((block, fixed, start, half == 0))
        return summed[0]

    rows_stack, *own = stack_product(mid, places, a_blocks, [w_own, w_mid])
    own = totals_of(mid, [w_own, w_mid], ([0],), (own[0],)) + own
    own[1], own[2], own[3], next_1 = lax.optimization_barrier((*own[1:], next_1))
    own_sums = across_plane(own)
    first, one, two, three = [(block, None) for block in (next_0, next_1, next_2, next_3)]
    w_low = [[first, one], [one, first], [one, two], [one, two]]
    w_high = [[two, three], [two, three], [first, three], [three, first]]
    low = totals_of(at_plane, w_low, ([3, 1, 2, 0],), (own[0],))
    low[1], low[2], low[3], *own_sums = lax.optimization_barrier((*low[1:], *own_sums))
    low_sums = across_plane(low)
    summed = spread(own, own_sums, 0, 0, (low[0],))
    high = totals_of(at_plane, w_high, ([3, 1, 2], [0]), (low[0], summed))
    high[1], high[2], high[3], *low_sums = lax.optimization_barrier((*high[1:], *low_sums))
    high_sums = across_plane(high)
    spread(low, low_sums, 1, 0, (high[0],))
    spread(high, high_sums, 1, 2)
    across = z_low * 16 + z_high * 8 + me % 2
    place = jnp.stack([across + plane * 2, across]).astype(jnp.int32)
    return assemble(place, pieces)


def shards(gate_pre, up_pre, down_weight):
    hidden = silu_product(gate_pre, up_pre)
    terms = jnp.dot(
        hidden,
        lax.all_gather(down_weight, "fsdp", axis=1, tiled=True),
        preferred_element_type=jnp.float32,
    )
    totals = lax.psum(terms, "tp")
    share = totals.shape[1] // lax.axis_size("tp")
    result = lax.dynamic_slice_in_dim(totals, lax.axis_index("tp") * share, share, 1)
    return result.astype(jnp.bfloat16)


def solution(mesh):
    in_blocks = mesh.shape["tp"] == 1 and mesh.shape["fsdp"] == 4 * PAIR
    return jax.shard_map(
        blocks if in_blocks else shards,
        mesh=mesh,
        in_specs=(P("fsdp", "tp"), P("fsdp", "tp"), P("tp", "fsdp")),
        out_specs=P("fsdp", "tp"),
        check_vma=False,
    )
```

```python
import functools

import jax
import jax.numpy as jnp
from jax import lax
from jax.experimental import pallas as pl
from jax.experimental.pallas import tpu as pltpu
from jax.sharding import PartitionSpec as P

CORE, PLANE, PAIR = 1, 2, 8
LIMIT = 10 * 1024 * 1024
LANES = 128


def flip(n, mask):
    return [(source, source ^ mask) for source in range(n)]


def along_z(n, pairs):
    low = PAIR
    return [(a * low + rest, b * low + rest) for a, b in pairs for rest in range(low)]


def silu_product(gate, up):
    return (jax.nn.silu(gate.astype(jnp.float32)) * up.astype(jnp.float32)).astype(jnp.bfloat16)


def pack_kernel(apart, count, plane_ref, *refs):
    outs = refs[len(refs) - count - apart :]
    pairs = [(outs[0], outs[1])] if apart else []
    pairs += [(out.at[0], out.at[1]) for out in outs[2 * apart :]]
    for at, (a, w) in enumerate(pairs):
        gate, up, weight = refs[3 * at : 3 * at + 3]
        hidden = silu_product(gate[...], up[...])
        for tile in range(a.shape[0]):
            a[tile] = hidden[:, tile * LANES : (tile + 1) * LANES]
            w[tile] = weight[pl.ds(tile * LANES, LANES)]


def pack(plane, steps, gate, up, weight, after=()):
    rows, columns = gate.shape[0], weight.shape[1]
    tiles = gate.shape[1] // (4 * LANES)
    grid = 4
    share = tiles // grid
    apart = int(steps[0] == 0)
    single = pltpu.HBM((tiles, rows, LANES), jnp.bfloat16)
    double = pltpu.HBM((2, tiles, rows, LANES), jnp.bfloat16)
    single_spec = pl.BlockSpec((share, rows, LANES), lambda at, plane: (at, 0, 0))
    double_spec = pl.BlockSpec((2, share, rows, LANES), lambda at, plane: (0, at, 0, 0))
    others = len(steps) - apart
    in_specs = []
    for step in steps:

        def across(at, plane, step=step):
            return 0, (plane[0] ^ step) * grid + at

        def down(at, plane, step=step):
            return (plane[0] ^ step) * grid + at, 0

        wide = pl.BlockSpec((rows, share * LANES), across)
        in_specs += [wide, wide, pl.BlockSpec((share * LANES, columns), down)]
    in_specs += [pl.BlockSpec(memory_space=pl.ANY)] * len(after)
    return pl.pallas_call(
        functools.partial(pack_kernel, apart, len(steps)),
        out_shape=[single] * (2 * apart) + [double] * others,
        grid_spec=pltpu.PrefetchScalarGridSpec(
            num_scalar_prefetch=1,
            grid=(grid,),
            in_specs=in_specs,
            out_specs=[single_spec] * (2 * apart) + [double_spec] * others,
        ),
        compiler_params=pltpu.CompilerParams(vmem_limit_bytes=LIMIT),
        cost_estimate=pl.CostEstimate(
            flops=0,
            bytes_accessed=10 * rows * tiles * LANES * len(steps),
            transcendentals=rows * tiles * LANES * len(steps),
        ),
        name="pack",
    )(plane, *[gate, up, weight] * len(steps), *after)


def unpack_pair_kernel(one, two, *refs):
    a, w, held, in_sem, out_sem = refs[-5:]
    ways = [
        (source.at[kind], out.at[at])
        for at, source in enumerate((one, two))
        for kind, out in enumerate((a, w))
    ]
    into = [
        pltpu.make_async_copy(source, held.at[at], in_sem.at[at])
        for at, (source, _) in enumerate(ways)
    ]
    out_of = [
        pltpu.make_async_copy(held.at[at], to, out_sem.at[at]) for at, (_, to) in enumerate(ways)
    ]
    for copy in into:
        copy.start()
    for copy_in, copy_out in zip(into, out_of):
        copy_in.wait()
        copy_out.start()
    for copy in out_of:
        copy.wait()


def unpack_pair(one, two, after):
    return pl.pallas_call(
        unpack_pair_kernel,
        out_shape=[pltpu.HBM(one.shape, one.dtype)] * 2,
        in_specs=[pl.BlockSpec(memory_space=pl.ANY)] * (2 + len(after)),
        out_specs=[pl.BlockSpec(memory_space=pl.ANY)] * 2,
        scratch_shapes=[
            pltpu.VMEM((4,) + one.shape[1:], one.dtype),
            pltpu.SemaphoreType.DMA((4,)),
            pltpu.SemaphoreType.DMA((4,)),
        ],
        compiler_params=pltpu.CompilerParams(vmem_limit_bytes=LIMIT),
        cost_estimate=pl.CostEstimate(flops=0, bytes_accessed=8 * one.size, transcendentals=0),
        name="unpack_pair",
    )(one, two, *after)


def reorder_kernel(count, order_ref, packed, w_12, *refs):
    outs, (held, in_sem, out_sem) = refs[-3 - count : -3], refs[-3:]
    into = [
        pltpu.make_async_copy(source, held.at[at], in_sem.at[at])
        for at, source in enumerate((packed.at[0], w_12.at[0], w_12.at[1], packed.at[1]))
    ]
    out_of = [
        pltpu.make_async_copy(held.at[order_ref[at]], out, out_sem.at[at])
        for at, out in enumerate(outs)
    ]
    for copy in into:
        copy.start()
    for copy in into:
        copy.wait()
    for copy in out_of:
        copy.start()
    for copy in out_of:
        copy.wait()


def reorder(order, packed, w_12):
    shape, count = packed.shape[1:], order.shape[0]
    return pl.pallas_call(
        functools.partial(reorder_kernel, count),
        out_shape=[pltpu.HBM(shape, packed.dtype)] * count,
        in_specs=[pl.BlockSpec(memory_space=pltpu.SMEM)]
        + [pl.BlockSpec(memory_space=pl.ANY)] * 2,
        out_specs=[pl.BlockSpec(memory_space=pl.ANY)] * count,
        scratch_shapes=[
            pltpu.VMEM((4,) + shape, packed.dtype),
            pltpu.SemaphoreType.DMA((4,)),
            pltpu.SemaphoreType.DMA((count,)),
        ],
        compiler_params=pltpu.CompilerParams(vmem_limit_bytes=LIMIT),
        cost_estimate=pl.CostEstimate(flops=0, bytes_accessed=8 * packed.size, transcendentals=0),
        name="reorder",
    )(order, packed, *far([w_12]))


def far(arrays):
    return [pltpu.with_memory_space_constraint(array, pltpu.HBM) for array in arrays]


def multiply(a, right, place, out):
    tiles, rows = a.shape[0], a.shape[1] // 16
    for half in range(2):
        left = jnp.concatenate(
            [
                jnp.concatenate([a[tile, pl.ds(block * rows, rows)] for tile in range(tiles)], axis=1)
                for block in place[2 * half : 2 * half + 2]
            ],
            axis=0,
        )
        total = jnp.dot(left, right, preferred_element_type=jnp.float32)
        for at in range(2):
            out[2 * half + at] = total[at * rows : (at + 1) * rows].astype(out.dtype)


def stack_product_kernel(places, a_at, w_at, choice_ref, *refs):
    stack_ref, *outs, w, a_sem, w_sem = refs[-7:]
    tiles, _, columns = w.shape
    columns //= len(w_at[0])
    rows = stack_ref.shape[1] // 16

    def pick(at):
        ref, index = at
        return refs[ref] if index is None else refs[ref].at[index]

    def w_copy(at, choice):
        return pltpu.make_async_copy(
            pick(w_at[choice][at]), w.at[:, :, pl.ds(at * columns, columns)], w_sem.at[at]
        )

    def a_copy(at):
        return pltpu.make_async_copy(
            pick(a_at[at]), stack_ref.at[:, pl.ds(at * rows, rows)], a_sem.at[at]
        )

    for at in range(len(w_at[0])):
        for choice in range(len(w_at)):

            @pl.when(choice_ref[0] == choice)
            def _():
                w_copy(at, choice).start()

    for group in (1, 2, 3, 0):
        for at in places[group]:
            a_copy(at).start()
    for at in range(len(w_at[0])):
        w_copy(at, 0).wait()
    right = w[...].reshape(tiles * LANES, len(w_at[0]) * columns)
    for group in (1, 2, 3):
        for at in places[group]:
            a_copy(at).wait()
        multiply(stack_ref, right, places[group], outs[group - 1])
    for at in places[0]:
        a_copy(at).wait()


def stack_product(choice, places, a_blocks, w_choices):
    arrays = []

    def at(block):
        array, index = block
        for known, other in enumerate(arrays):
            if other is array:
                return known, index
        arrays.append(array)
        return len(arrays) - 1, index

    a_at = [at(block) for block in a_blocks]
    w_at = [[at(block) for block in blocks] for blocks in w_choices]
    tiles, rows, _ = a_blocks[0][0].shape
    wide = len(w_choices[0]) * w_choices[0][0][0].shape[-1]
    return pl.pallas_call(
        functools.partial(stack_product_kernel, places, a_at, w_at),
        out_shape=[pltpu.VMEM((tiles, 16 * rows, LANES), jnp.bfloat16)]
        + [jax.ShapeDtypeStruct((4, rows, wide), jnp.bfloat16)] * 3,
        in_specs=[pl.BlockSpec(memory_space=pltpu.SMEM)]
        + [pl.BlockSpec(memory_space=pl.ANY)] * len(arrays),
        out_specs=[pl.BlockSpec(memory_space=pltpu.VMEM)] * 4,
        scratch_shapes=[
            pltpu.VMEM((tiles, LANES, wide), jnp.bfloat16),
            pltpu.SemaphoreType.DMA((16,)),
            pltpu.SemaphoreType.DMA((len(w_at[0]),)),
        ],
        compiler_params=pltpu.CompilerParams(vmem_limit_bytes=LIMIT),
        cost_estimate=pl.CostEstimate(
            flops=24 * rows * tiles * LANES * wide,
            bytes_accessed=2 * tiles * LANES * (16 * rows + wide),
            transcendentals=0,
        ),
        name="stack_product",
    )(choice, *arrays)


def product_kernel(places, w_at, choice_ref, a, *refs):
    groups, wide = len(places), len(w_at[0])
    outs, (w, w_sem) = refs[-2 - groups : -2], refs[-2:]
    tiles, _, columns = w.shape
    columns //= wide

    def pick(at):
        ref, index = at
        return refs[ref] if index is None else refs[ref].at[index]

    def w_copy(at, choice):
        return pltpu.make_async_copy(
            pick(w_at[choice][at]), w.at[:, :, pl.ds(at * columns, columns)], w_sem.at[at]
        )

    for at in range(wide):
        for choice in range(len(w_at)):

            @pl.when(choice_ref[0] == choice)
            def _():
                w_copy(at, choice).start()

    for at in range(wide):
        w_copy(at, 0).wait()
    right = w[...].reshape(tiles * LANES, wide * columns)
    for place, out in zip(places, outs):
        multiply(a, right, place, out)


def product(choice, groups, places, rows_stack, w_choices, after=()):
    arrays = []

    def at(block):
        array, index = block
        for known, other in enumerate(arrays):
            if other is array:
                return known, index
        arrays.append(array)
        return len(arrays) - 1, index

    w_at = [[at(block) for block in blocks] for blocks in w_choices]
    tiles, rows, _ = rows_stack.shape
    rows //= 16
    columns = w_choices[-1][0][0].shape[-1]
    wide = len(w_choices[0])
    shape = (4, rows, wide * columns)
    count = len(arrays) + len(after)
    return pl.pallas_call(
        functools.partial(product_kernel, [places[group] for group in groups], w_at),
        out_shape=[
            jax.ShapeDtypeStruct(shape, jnp.float32 if group == 0 else jnp.bfloat16)
            for group in groups
        ],
        in_specs=[
            pl.BlockSpec(memory_space=pltpu.SMEM),
            pl.BlockSpec(memory_space=pltpu.VMEM),
        ]
        + [pl.BlockSpec(memory_space=pl.ANY)] * count,
        out_specs=[pl.BlockSpec(memory_space=pltpu.VMEM)] * len(groups),
        scratch_shapes=[
            pltpu.VMEM((tiles, LANES, wide * columns), jnp.bfloat16),
            pltpu.SemaphoreType.DMA((wide,)),
        ],
        compiler_params=pltpu.CompilerParams(vmem_limit_bytes=LIMIT),
        cost_estimate=pl.CostEstimate(
            flops=8 * len(groups) * rows * tiles * LANES * wide * columns,
            bytes_accessed=2 * tiles * LANES * (4 * len(groups) * rows + wide * columns),
            transcendentals=0,
        ),
        name="product",
    )(choice, pltpu.with_memory_space_constraint(rows_stack, pltpu.VMEM), *arrays, *after)


def add_kernel(relative, own, one, two, three, *refs):
    blocks_wide, outs = own.shape[2] // LANES, refs[-4:]
    for piece in range(4):
        for at in range(blocks_wide):
            here = pl.ds(at * LANES, LANES)
            total = own[piece, :, here]
            for step, ref in ((1, one), (2, two), (3, three)):
                source = at ^ step if relative else at
                total += ref[piece, :, pl.ds(source * LANES, LANES)].astype(jnp.float32)
            outs[piece][:, here] = total.astype(jnp.bfloat16)


def add(own, others, relative, after=()):
    _, rows, columns = own.shape
    return pl.pallas_call(
        functools.partial(add_kernel, relative),
        out_shape=[jax.ShapeDtypeStruct((rows, columns), jnp.bfloat16)] * 4,
        in_specs=[pl.BlockSpec(memory_space=pltpu.VMEM)] * 4
        + [pl.BlockSpec(memory_space=pl.ANY)] * len(after),
        out_specs=[pl.BlockSpec(memory_space=pltpu.VMEM)] * 4,
        compiler_params=pltpu.CompilerParams(vmem_limit_bytes=LIMIT),
        cost_estimate=pl.CostEstimate(
            flops=12 * rows * columns, bytes_accessed=48 * rows * columns, transcendentals=0
        ),
        name="add",
    )(own, *others, *after)


def assemble_kernel(groups, place_ref, *refs):
    out = refs[-1]
    for ref, (fixed, first, relative) in zip(refs, groups):
        place = place_ref[0] if relative else place_ref[1]
        for at in range(ref.shape[1] // LANES):
            index = fixed | ((first + at) << 1)
            to = pl.multiple_of((place ^ index) * LANES, LANES)
            out[:, pl.ds(to, LANES)] = ref[:, pl.ds(at * LANES, LANES)]


def assemble(place, pieces):
    arrays = [piece[0] for piece in pieces]
    rows = arrays[0].shape[0]
    columns = sum(array.shape[1] for array in arrays)
    return pl.pallas_call(
        functools.partial(assemble_kernel, [piece[1:] for piece in pieces]),
        out_shape=jax.ShapeDtypeStruct((rows, columns), jnp.bfloat16),
        in_specs=[pl.BlockSpec(memory_space=pltpu.SMEM)]
        + [pl.BlockSpec(memory_space=pltpu.VMEM)] * len(arrays),
        out_specs=pl.BlockSpec(memory_space=pltpu.VMEM),
        compiler_params=pltpu.CompilerParams(vmem_limit_bytes=LIMIT),
        name="assemble",
    )(place, *arrays)


def blocks(gate_pre, up_pre, down_weight):
    n = lax.axis_size("fsdp")
    me = lax.axis_index("fsdp")
    plane = (me // PLANE) % 4
    z_low, z_high = (me // PAIR) % 2, me // (2 * PAIR)
    at_plane = plane.astype(jnp.int32).reshape(1)
    inputs = [
        pltpu.with_memory_space_constraint(array, pltpu.HBM)
        for array in (gate_pre, up_pre, down_weight)
    ]

    def send(array, perm):
        return lax.ppermute(array, "fsdp", perm=perm)

    def to_mid(array):
        return send(array, along_z(n, [(1, 2), (2, 1)]))

    def to_next(array):
        return send(array, along_z(n, [(1, 0), (3, 1), (0, 2), (2, 3)]))

    def to_core(array):
        return send(array, flip(n, CORE))

    def to_pair(array):
        return send(array, flip(n, PAIR))

    a_0, w_0, packed_1, packed_2 = pack(at_plane, (0, 1, 2), *inputs)
    pair_0, mid_0, next_0 = to_pair(a_0), to_mid(w_0), to_next(w_0)
    got_1 = send(packed_1, flip(n, PLANE))
    got_2 = send(packed_2, flip(n, 2 * PLANE))

    (packed_3,) = pack(at_plane, (3,), *inputs, after=(pair_0,))
    packed_3, got_1, got_2 = lax.optimization_barrier((packed_3, got_1, got_2))
    got_3 = send(packed_3, flip(n, 3 * PLANE))
    a_12, w_12 = unpack_pair(got_1, got_2, after=(pair_0, mid_0, next_0))
    pair_12, mid_12 = to_pair(a_12), to_mid(w_12)
    core_0, core_pair_0 = to_core(a_0), to_core(pair_0)

    order = jnp.array([[1, 2, 3], [1, 3, 2], [2, 3, 1], [3, 2, 1]], jnp.int32)[plane]
    got_3, core_0, core_pair_0 = lax.optimization_barrier((got_3, core_0, core_pair_0))
    known = jnp.array([0, 3], jnp.int32)
    a_3, w_3, ordered_1 = reorder(jnp.concatenate([known, order[:1]]), got_3, w_12)
    w_3, mid_12 = lax.optimization_barrier((w_3, mid_12))
    pair_3, mid_3 = to_pair(a_3), to_mid(w_3)
    a_12, pair_12, a_3 = lax.optimization_barrier((a_12, pair_12, a_3))
    core_12, core_pair_12 = to_core(a_12), to_core(pair_12)
    got_3, pair_3, mid_3, core_12, core_pair_12 = lax.optimization_barrier(
        (got_3, pair_3, mid_3, core_12, core_pair_12)
    )
    ordered_2, ordered_3 = reorder(order[1:], got_3, w_12)
    next_1, next_2, next_3 = to_next(ordered_1), to_next(ordered_2), to_next(ordered_3)
    core_3, core_pair_3 = to_core(a_3), to_core(pair_3)

    a_0, w_0, a_12, w_12, a_3, w_3 = far([a_0, w_0, a_12, w_12, a_3, w_3])
    mid_0, mid_12, mid_3, core_12, core_pair_12 = far([mid_0, mid_12, mid_3, core_12, core_pair_12])
    a_blocks = [(block, None) for block in (a_0, pair_0, core_0, core_pair_0)]
    for block in (a_12, pair_12, core_12, core_pair_12):
        a_blocks += [(block, 0), (block, 1)]
    a_blocks += [(block, None) for block in (a_3, pair_3, core_3, core_pair_3)]
    places = [(0, 2, 1, 3), (4, 8, 6, 10), (5, 9, 7, 11), (12, 14, 13, 15)]
    w_own = [(w_0, None), (w_12, 0), (w_12, 1), (w_3, None)]
    w_mid = [(mid_0, None), (mid_12, 0), (mid_12, 1), (mid_3, None)]
    mid = (z_low ^ z_high).astype(jnp.int32).reshape(1)

    def totals_of(choice, w_choices, calls, after=()):
        totals = {}
        for groups in calls:
            outs = product(choice, groups, places, rows_stack, w_choices, after)
            totals.update(zip(groups, outs))
            after = (outs[0],)
        return [totals[group] for group in sorted(totals)]

    def across_plane(totals):
        return [send(totals[step], flip(n, step * PLANE)) for step in (1, 2, 3)]

    pieces = []

    def spread(totals, others, half, start, after=()):
        summed = add(totals[0], others, half == 0, after)
        for piece in range(4):
            mask = (piece >> 1) * PAIR + (piece & 1) * CORE
            block = send(summed[piece], flip(n, mask)) if mask else summed[piece]
            fixed = ((piece >> 1) << 4) | (half << 3) | (piece & 1)
            pieces.append((block, fixed, start, half == 0))
        return summed[0]

    rows_stack, *own = stack_product(mid, places, a_blocks, [w_own, w_mid])
    own = totals_of(mid, [w_own, w_mid], ([0],), (own[0],)) + own
    own[1], own[2], own[3], next_1 = lax.optimization_barrier((*own[1:], next_1))
    own_sums = across_plane(own)
    first, one, two, three = [(block, None) for block in (next_0, next_1, next_2, next_3)]
    w_low = [[first, one], [one, first], [one, two], [one, two]]
    w_high = [[two, three], [two, three], [first, three], [three, first]]
    low = totals_of(at_plane, w_low, ([3, 1, 2, 0],), (own[0],))
    low[1], low[2], low[3], *own_sums = lax.optimization_barrier((*low[1:], *own_sums))
    low_sums = across_plane(low)
    summed = spread(own, own_sums, 0, 0, (low[0],))
    high = totals_of(at_plane, w_high, ([3, 1, 2], [0]), (low[0], summed))
    high[1], high[2], high[3], *low_sums = lax.optimization_barrier((*high[1:], *low_sums))
    high_sums = across_plane(high)
    spread(low, low_sums, 1, 0, (high[0],))
    spread(high, high_sums, 1, 2)
    across = z_low * 16 + z_high * 8 + me % 2
    place = jnp.stack([across + plane * 2, across]).astype(jnp.int32)
    return assemble(place, pieces)


def shards(gate_pre, up_pre, down_weight):
    hidden = silu_product(gate_pre, up_pre)
    terms = jnp.dot(
        hidden,
        lax.all_gather(down_weight, "fsdp", axis=1, tiled=True),
        preferred_element_type=jnp.float32,
    )
    totals = lax.psum(terms, "tp")
    share = totals.shape[1] // lax.axis_size("tp")
    result = lax.dynamic_slice_in_dim(totals, lax.axis_index("tp") * share, share, 1)
    return result.astype(jnp.bfloat16)


def solution(mesh):
    in_blocks = mesh.shape["tp"] == 1 and mesh.shape["fsdp"] == 4 * PAIR
    return jax.shard_map(
        blocks if in_blocks else shards,
        mesh=mesh,
        in_specs=(P("fsdp", "tp"), P("fsdp", "tp"), P("tp", "fsdp")),
        out_specs=P("fsdp", "tp"),
        check_vma=False,
    )
```

```python
import functools

import jax
import jax.numpy as jnp
from jax import lax
from jax.experimental import pallas as pl
from jax.experimental.pallas import tpu as pltpu
from jax.sharding import PartitionSpec as P

CORE, PLANE, PAIR = 1, 2, 8
LIMIT = 10 * 1024 * 1024
LANES = 128


def flip(n, mask):
    return [(source, source ^ mask) for source in range(n)]


def along_z(n, pairs):
    low = PAIR
    return [(a * low + rest, b * low + rest) for a, b in pairs for rest in range(low)]


def silu_product(gate, up):
    return (jax.nn.silu(gate.astype(jnp.float32)) * up.astype(jnp.float32)).astype(jnp.bfloat16)


def pack_kernel(apart, count, plane_ref, *refs):
    outs = refs[len(refs) - count - apart :]
    pairs = [(outs[0], outs[1])] if apart else []
    pairs += [(out.at[0], out.at[1]) for out in outs[2 * apart :]]
    for at, (a, w) in enumerate(pairs):
        gate, up, weight = refs[3 * at : 3 * at + 3]
        hidden = silu_product(gate[...], up[...])
        for tile in range(a.shape[0]):
            a[tile] = hidden[:, tile * LANES : (tile + 1) * LANES]
            w[tile] = weight[pl.ds(tile * LANES, LANES)]


def pack(plane, steps, gate, up, weight, after=()):
    rows, columns = gate.shape[0], weight.shape[1]
    tiles = gate.shape[1] // (4 * LANES)
    grid = 4
    share = tiles // grid
    apart = int(steps[0] == 0)
    single = pltpu.HBM((tiles, rows, LANES), jnp.bfloat16)
    double = pltpu.HBM((2, tiles, rows, LANES), jnp.bfloat16)
    single_spec = pl.BlockSpec((share, rows, LANES), lambda at, plane: (at, 0, 0))
    double_spec = pl.BlockSpec((2, share, rows, LANES), lambda at, plane: (0, at, 0, 0))
    others = len(steps) - apart
    in_specs = []
    for step in steps:

        def across(at, plane, step=step):
            return 0, (plane[0] ^ step) * grid + at

        def down(at, plane, step=step):
            return (plane[0] ^ step) * grid + at, 0

        wide = pl.BlockSpec((rows, share * LANES), across)
        in_specs += [wide, wide, pl.BlockSpec((share * LANES, columns), down)]
    in_specs += [pl.BlockSpec(memory_space=pl.ANY)] * len(after)
    return pl.pallas_call(
        functools.partial(pack_kernel, apart, len(steps)),
        out_shape=[single] * (2 * apart) + [double] * others,
        grid_spec=pltpu.PrefetchScalarGridSpec(
            num_scalar_prefetch=1,
            grid=(grid,),
            in_specs=in_specs,
            out_specs=[single_spec] * (2 * apart) + [double_spec] * others,
        ),
        compiler_params=pltpu.CompilerParams(vmem_limit_bytes=LIMIT),
        cost_estimate=pl.CostEstimate(
            flops=0,
            bytes_accessed=10 * rows * tiles * LANES * len(steps),
            transcendentals=rows * tiles * LANES * len(steps),
        ),
        name="pack",
    )(plane, *[gate, up, weight] * len(steps), *after)


def unpack_pair_kernel(one, two, *refs):
    a, w, held, in_sem, out_sem = refs[-5:]
    ways = [
        (source.at[kind], out.at[at])
        for at, source in enumerate((one, two))
        for kind, out in enumerate((a, w))
    ]
    into = [
        pltpu.make_async_copy(source, held.at[at], in_sem.at[at])
        for at, (source, _) in enumerate(ways)
    ]
    out_of = [
        pltpu.make_async_copy(held.at[at], to, out_sem.at[at]) for at, (_, to) in enumerate(ways)
    ]
    for copy in into:
        copy.start()
    for copy_in, copy_out in zip(into, out_of):
        copy_in.wait()
        copy_out.start()
    for copy in out_of:
        copy.wait()


def unpack_pair(one, two, after):
    return pl.pallas_call(
        unpack_pair_kernel,
        out_shape=[pltpu.HBM(one.shape, one.dtype)] * 2,
        in_specs=[pl.BlockSpec(memory_space=pl.ANY)] * (2 + len(after)),
        out_specs=[pl.BlockSpec(memory_space=pl.ANY)] * 2,
        scratch_shapes=[
            pltpu.VMEM((4,) + one.shape[1:], one.dtype),
            pltpu.SemaphoreType.DMA((4,)),
            pltpu.SemaphoreType.DMA((4,)),
        ],
        compiler_params=pltpu.CompilerParams(vmem_limit_bytes=LIMIT),
        cost_estimate=pl.CostEstimate(flops=0, bytes_accessed=8 * one.size, transcendentals=0),
        name="unpack_pair",
    )(one, two, *after)


def reorder_kernel(count, order_ref, packed, w_12, *refs):
    outs, (held, in_sem, out_sem) = refs[-3 - count : -3], refs[-3:]
    into = [
        pltpu.make_async_copy(source, held.at[at], in_sem.at[at])
        for at, source in enumerate((packed.at[0], w_12.at[0], w_12.at[1], packed.at[1]))
    ]
    out_of = [
        pltpu.make_async_copy(held.at[order_ref[at]], out, out_sem.at[at])
        for at, out in enumerate(outs)
    ]
    for copy in into:
        copy.start()
    for copy in into:
        copy.wait()
    for copy in out_of:
        copy.start()
    for copy in out_of:
        copy.wait()


def reorder(order, packed, w_12):
    shape, count = packed.shape[1:], order.shape[0]
    return pl.pallas_call(
        functools.partial(reorder_kernel, count),
        out_shape=[pltpu.HBM(shape, packed.dtype)] * count,
        in_specs=[pl.BlockSpec(memory_space=pltpu.SMEM)]
        + [pl.BlockSpec(memory_space=pl.ANY)] * 2,
        out_specs=[pl.BlockSpec(memory_space=pl.ANY)] * count,
        scratch_shapes=[
            pltpu.VMEM((4,) + shape, packed.dtype),
            pltpu.SemaphoreType.DMA((4,)),
            pltpu.SemaphoreType.DMA((count,)),
        ],
        compiler_params=pltpu.CompilerParams(vmem_limit_bytes=LIMIT),
        cost_estimate=pl.CostEstimate(flops=0, bytes_accessed=8 * packed.size, transcendentals=0),
        name="reorder",
    )(order, packed, *far([w_12]))


def far(arrays):
    return [pltpu.with_memory_space_constraint(array, pltpu.HBM) for array in arrays]


def multiply(a, right, place, out):
    tiles, rows = a.shape[0], a.shape[1] // 16
    for half in range(2):
        left = jnp.concatenate(
            [
                jnp.concatenate([a[tile, pl.ds(block * rows, rows)] for tile in range(tiles)], axis=1)
                for block in place[2 * half : 2 * half + 2]
            ],
            axis=0,
        )
        total = jnp.dot(left, right, preferred_element_type=jnp.float32)
        for at in range(2):
            out[2 * half + at] = total[at * rows : (at + 1) * rows].astype(out.dtype)


def stack_product_kernel(places, a_at, w_at, choice_ref, *refs):
    stack_ref, *outs, w, a_sem, w_sem = refs[-7:]
    tiles, _, columns = w.shape
    columns //= len(w_at[0])
    rows = stack_ref.shape[1] // 16

    def pick(at):
        ref, index = at
        return refs[ref] if index is None else refs[ref].at[index]

    def w_copy(at, choice):
        return pltpu.make_async_copy(
            pick(w_at[choice][at]), w.at[:, :, pl.ds(at * columns, columns)], w_sem.at[at]
        )

    def a_copy(at):
        return pltpu.make_async_copy(
            pick(a_at[at]), stack_ref.at[:, pl.ds(at * rows, rows)], a_sem.at[at]
        )

    for at in range(len(w_at[0])):
        for choice in range(len(w_at)):

            @pl.when(choice_ref[0] == choice)
            def _():
                w_copy(at, choice).start()

    for group in (1, 2, 3, 0):
        for at in places[group]:
            a_copy(at).start()
    for at in range(len(w_at[0])):
        w_copy(at, 0).wait()
    right = w[...].reshape(tiles * LANES, len(w_at[0]) * columns)
    for group in (1, 2, 3):
        for at in places[group]:
            a_copy(at).wait()
        multiply(stack_ref, right, places[group], outs[group - 1])
    for at in places[0]:
        a_copy(at).wait()


def stack_product(choice, places, a_blocks, w_choices):
    arrays = []

    def at(block):
        array, index = block
        for known, other in enumerate(arrays):
            if other is array:
                return known, index
        arrays.append(array)
        return len(arrays) - 1, index

    a_at = [at(block) for block in a_blocks]
    w_at = [[at(block) for block in blocks] for blocks in w_choices]
    tiles, rows, _ = a_blocks[0][0].shape
    wide = len(w_choices[0]) * w_choices[0][0][0].shape[-1]
    return pl.pallas_call(
        functools.partial(stack_product_kernel, places, a_at, w_at),
        out_shape=[pltpu.VMEM((tiles, 16 * rows, LANES), jnp.bfloat16)]
        + [jax.ShapeDtypeStruct((4, rows, wide), jnp.bfloat16)] * 3,
        in_specs=[pl.BlockSpec(memory_space=pltpu.SMEM)]
        + [pl.BlockSpec(memory_space=pl.ANY)] * len(arrays),
        out_specs=[pl.BlockSpec(memory_space=pltpu.VMEM)] * 4,
        scratch_shapes=[
            pltpu.VMEM((tiles, LANES, wide), jnp.bfloat16),
            pltpu.SemaphoreType.DMA((16,)),
            pltpu.SemaphoreType.DMA((len(w_at[0]),)),
        ],
        compiler_params=pltpu.CompilerParams(vmem_limit_bytes=LIMIT),
        cost_estimate=pl.CostEstimate(
            flops=24 * rows * tiles * LANES * wide,
            bytes_accessed=2 * tiles * LANES * (16 * rows + wide),
            transcendentals=0,
        ),
        name="stack_product",
    )(choice, *arrays)


def product_kernel(places, w_at, choice_ref, a, *refs):
    groups, wide = len(places), len(w_at[0])
    outs, (w, w_sem) = refs[-2 - groups : -2], refs[-2:]
    tiles, _, columns = w.shape
    columns //= wide

    def pick(at):
        ref, index = at
        return refs[ref] if index is None else refs[ref].at[index]

    def w_copy(at, choice):
        return pltpu.make_async_copy(
            pick(w_at[choice][at]), w.at[:, :, pl.ds(at * columns, columns)], w_sem.at[at]
        )

    for at in range(wide):
        for choice in range(len(w_at)):

            @pl.when(choice_ref[0] == choice)
            def _():
                w_copy(at, choice).start()

    for at in range(wide):
        w_copy(at, 0).wait()
    right = w[...].reshape(tiles * LANES, wide * columns)
    for place, out in zip(places, outs):
        multiply(a, right, place, out)


def product(choice, groups, places, rows_stack, w_choices, after=()):
    arrays = []

    def at(block):
        array, index = block
        for known, other in enumerate(arrays):
            if other is array:
                return known, index
        arrays.append(array)
        return len(arrays) - 1, index

    w_at = [[at(block) for block in blocks] for blocks in w_choices]
    tiles, rows, _ = rows_stack.shape
    rows //= 16
    columns = w_choices[-1][0][0].shape[-1]
    wide = len(w_choices[0])
    shape = (4, rows, wide * columns)
    count = len(arrays) + len(after)
    return pl.pallas_call(
        functools.partial(product_kernel, [places[group] for group in groups], w_at),
        out_shape=[
            jax.ShapeDtypeStruct(shape, jnp.float32 if group == 0 else jnp.bfloat16)
            for group in groups
        ],
        in_specs=[
            pl.BlockSpec(memory_space=pltpu.SMEM),
            pl.BlockSpec(memory_space=pltpu.VMEM),
        ]
        + [pl.BlockSpec(memory_space=pl.ANY)] * count,
        out_specs=[pl.BlockSpec(memory_space=pltpu.VMEM)] * len(groups),
        scratch_shapes=[
            pltpu.VMEM((tiles, LANES, wide * columns), jnp.bfloat16),
            pltpu.SemaphoreType.DMA((wide,)),
        ],
        compiler_params=pltpu.CompilerParams(vmem_limit_bytes=LIMIT),
        cost_estimate=pl.CostEstimate(
            flops=8 * len(groups) * rows * tiles * LANES * wide * columns,
            bytes_accessed=2 * tiles * LANES * (4 * len(groups) * rows + wide * columns),
            transcendentals=0,
        ),
        name="product",
    )(choice, pltpu.with_memory_space_constraint(rows_stack, pltpu.VMEM), *arrays, *after)


def add_kernel(kinds, *refs):
    outs, first = refs[-4:], 0
    for kind, relative in enumerate(kinds):
        own, *others = refs[4 * kind : 4 * kind + 4]
        blocks_wide = own.shape[2] // LANES
        for piece in range(4):
            for at in range(blocks_wide):
                total = own[piece, :, pl.ds(at * LANES, LANES)]
                for step, ref in zip((1, 2, 3), others):
                    source = at ^ step if relative else at
                    total += ref[piece, :, pl.ds(source * LANES, LANES)].astype(jnp.float32)
                outs[piece][:, pl.ds((first + at) * LANES, LANES)] = total.astype(jnp.bfloat16)
        first += blocks_wide


def add(terms, kinds, after=()):
    rows = terms[0][0].shape[1]
    columns = sum(own.shape[2] for own, *_ in terms)
    arrays = [array for group in terms for array in group]
    return pl.pallas_call(
        functools.partial(add_kernel, kinds),
        out_shape=[jax.ShapeDtypeStruct((rows, columns), jnp.bfloat16)] * 4,
        in_specs=[pl.BlockSpec(memory_space=pltpu.VMEM)] * len(arrays)
        + [pl.BlockSpec(memory_space=pl.ANY)] * len(after),
        out_specs=[pl.BlockSpec(memory_space=pltpu.VMEM)] * 4,
        compiler_params=pltpu.CompilerParams(vmem_limit_bytes=LIMIT),
        cost_estimate=pl.CostEstimate(
            flops=12 * rows * columns, bytes_accessed=48 * rows * columns, transcendentals=0
        ),
        name="add",
    )(*arrays, *after)


def assemble_kernel(groups, place_ref, *refs):
    out = refs[-1]
    for ref, (fixed, parts) in zip(refs, groups):
        for at, (half, block) in enumerate(parts):
            index = fixed | (half << 3) | (block << 1)
            to = pl.multiple_of((place_ref[half] ^ index) * LANES, LANES)
            out[:, pl.ds(to, LANES)] = ref[:, pl.ds(at * LANES, LANES)]


def assemble(place, pieces):
    arrays = [piece[0] for piece in pieces]
    rows = arrays[0].shape[0]
    columns = sum(array.shape[1] for array in arrays)
    return pl.pallas_call(
        functools.partial(assemble_kernel, [piece[1:] for piece in pieces]),
        out_shape=jax.ShapeDtypeStruct((rows, columns), jnp.bfloat16),
        in_specs=[pl.BlockSpec(memory_space=pltpu.SMEM)]
        + [pl.BlockSpec(memory_space=pltpu.VMEM)] * len(arrays),
        out_specs=pl.BlockSpec(memory_space=pltpu.VMEM),
        compiler_params=pltpu.CompilerParams(vmem_limit_bytes=LIMIT),
        name="assemble",
    )(place, *arrays)


def blocks(gate_pre, up_pre, down_weight):
    n = lax.axis_size("fsdp")
    me = lax.axis_index("fsdp")
    plane = (me // PLANE) % 4
    z_low, z_high = (me // PAIR) % 2, me // (2 * PAIR)
    at_plane = plane.astype(jnp.int32).reshape(1)
    inputs = [
        pltpu.with_memory_space_constraint(array, pltpu.HBM)
        for array in (gate_pre, up_pre, down_weight)
    ]

    def send(array, perm):
        return lax.ppermute(array, "fsdp", perm=perm)

    def to_mid(array):
        return send(array, along_z(n, [(1, 2), (2, 1)]))

    def to_next(array):
        return send(array, along_z(n, [(1, 0), (3, 1), (0, 2), (2, 3)]))

    def to_core(array):
        return send(array, flip(n, CORE))

    def to_pair(array):
        return send(array, flip(n, PAIR))

    a_0, w_0, packed_1, packed_2 = pack(at_plane, (0, 1, 2), *inputs)
    pair_0, mid_0, next_0 = to_pair(a_0), to_mid(w_0), to_next(w_0)
    got_1 = send(packed_1, flip(n, PLANE))
    got_2 = send(packed_2, flip(n, 2 * PLANE))

    (packed_3,) = pack(at_plane, (3,), *inputs, after=(pair_0,))
    packed_3, got_1, got_2 = lax.optimization_barrier((packed_3, got_1, got_2))
    got_3 = send(packed_3, flip(n, 3 * PLANE))
    a_12, w_12 = unpack_pair(got_1, got_2, after=(pair_0, mid_0, next_0))
    pair_12, mid_12 = to_pair(a_12), to_mid(w_12)
    core_0, core_pair_0 = to_core(a_0), to_core(pair_0)

    order = jnp.array([[1, 2, 3], [1, 3, 2], [2, 3, 1], [3, 2, 1]], jnp.int32)[plane]
    got_3, core_0, core_pair_0 = lax.optimization_barrier((got_3, core_0, core_pair_0))
    known = jnp.array([0, 3], jnp.int32)
    a_3, w_3, ordered_1, ordered_2 = reorder(jnp.concatenate([known, order[:2]]), got_3, w_12)
    pair_3 = to_pair(a_3)
    a_12, pair_12, a_3 = lax.optimization_barrier((a_12, pair_12, a_3))
    core_12, core_pair_12 = to_core(a_12), to_core(pair_12)
    w_3, mid_12, core_12 = lax.optimization_barrier((w_3, mid_12, core_12))
    mid_3 = to_mid(w_3)
    ordered_1, pair_3 = lax.optimization_barrier((ordered_1, pair_3))
    ordered_2, mid_3 = lax.optimization_barrier((ordered_2, mid_3))
    next_1, next_2 = to_next(ordered_1), to_next(ordered_2)
    core_3, core_pair_3 = to_core(a_3), to_core(pair_3)

    a_0, w_0, a_12, w_12, a_3, w_3 = far([a_0, w_0, a_12, w_12, a_3, w_3])
    mid_0, mid_12, mid_3, core_12, core_pair_12 = far([mid_0, mid_12, mid_3, core_12, core_pair_12])
    a_blocks = [(block, None) for block in (a_0, pair_0, core_0, core_pair_0)]
    for block in (a_12, pair_12, core_12, core_pair_12):
        a_blocks += [(block, 0), (block, 1)]
    a_blocks += [(block, None) for block in (a_3, pair_3, core_3, core_pair_3)]
    places = [(0, 2, 1, 3), (4, 8, 6, 10), (5, 9, 7, 11), (12, 14, 13, 15)]
    w_own = [(w_0, None), (w_12, 0), (w_12, 1), (w_3, None)]
    w_mid = [(mid_0, None), (mid_12, 0), (mid_12, 1), (mid_3, None)]
    mid = (z_low ^ z_high).astype(jnp.int32).reshape(1)

    def totals_of(choice, w_choices, calls, after=()):
        totals = {}
        for groups in calls:
            outs = product(choice, groups, places, rows_stack, w_choices, after)
            totals.update(zip(groups, outs))
            after = (outs[0],)
        return [totals[group] for group in sorted(totals)]

    def across_plane(totals):
        return [send(totals[step], flip(n, step * PLANE)) for step in (1, 2, 3)]

    pieces = []

    def spread(terms, kinds, parts, after=()):
        summed = add(terms, kinds, after)
        for piece in range(4):
            mask = (piece >> 1) * PAIR + (piece & 1) * CORE
            block = send(summed[piece], flip(n, mask)) if mask else summed[piece]
            pieces.append((block, ((piece >> 1) << 4) | (piece & 1), parts))

    rows_stack, *own = stack_product(mid, places, a_blocks, [w_own, w_mid])
    own = totals_of(mid, [w_own, w_mid], ([0],), (own[0],)) + own
    own[1], got_3 = lax.optimization_barrier((own[1], got_3))
    (ordered_3,) = reorder(order[2:], got_3, w_12)
    next_3 = to_next(ordered_3)
    own_sums = across_plane(own)
    first, one, two, three = [(block, None) for block in (next_0, next_1, next_2, next_3)]
    w_low = [[first, one], [one, first], [one, two], [one, two]]
    w_high = [[two, three], [two, three], [first, three], [three, first]]
    low = totals_of(at_plane, w_low, ([3, 1, 2, 0],), (own[0],))
    low[1], low[2], low[3], *own_sums = lax.optimization_barrier((*low[1:], *own_sums))
    low_sums = across_plane(low)
    high = totals_of(at_plane, w_high, ([3, 1, 2], [0]), (low[0],))
    high[1], high[2], high[3], *low_sums = lax.optimization_barrier((*high[1:], *low_sums))
    high_sums = across_plane(high)
    spread(
        [(own[0], *own_sums), (low[0], *low_sums)],
        (True, False),
        [(0, 0), (0, 1), (0, 2), (0, 3), (1, 0), (1, 1)],
        (high[0],),
    )
    spread([(high[0], *high_sums)], (False,), [(1, 2), (1, 3)])
    across = z_low * 16 + z_high * 8 + me % 2
    place = jnp.stack([across + plane * 2, across]).astype(jnp.int32)
    return assemble(place, pieces)


def shards(gate_pre, up_pre, down_weight):
    hidden = silu_product(gate_pre, up_pre)
    terms = jnp.dot(
        hidden,
        lax.all_gather(down_weight, "fsdp", axis=1, tiled=True),
        preferred_element_type=jnp.float32,
    )
    totals = lax.psum(terms, "tp")
    share = totals.shape[1] // lax.axis_size("tp")
    result = lax.dynamic_slice_in_dim(totals, lax.axis_index("tp") * share, share, 1)
    return result.astype(jnp.bfloat16)


def solution(mesh):
    in_blocks = mesh.shape["tp"] == 1 and mesh.shape["fsdp"] == 4 * PAIR
    return jax.shard_map(
        blocks if in_blocks else shards,
        mesh=mesh,
        in_specs=(P("fsdp", "tp"), P("fsdp", "tp"), P("tp", "fsdp")),
        out_specs=P("fsdp", "tp"),
        check_vma=False,
    )
```

```python
import functools

import jax
import jax.numpy as jnp
from jax import lax
from jax.experimental import pallas as pl
from jax.experimental.pallas import tpu as pltpu
from jax.sharding import PartitionSpec as P

CORE, PLANE, PAIR = 1, 2, 8
LIMIT = 10 * 1024 * 1024
LANES = 128


def flip(n, mask):
    return [(source, source ^ mask) for source in range(n)]


def along_z(n, pairs):
    low = PAIR
    return [(a * low + rest, b * low + rest) for a, b in pairs for rest in range(low)]


def silu_product(gate, up):
    return (jax.nn.silu(gate.astype(jnp.float32)) * up.astype(jnp.float32)).astype(jnp.bfloat16)


def pack_kernel(apart, count, plane_ref, *refs):
    outs = refs[len(refs) - count - apart :]
    pairs = [(outs[0], outs[1])] if apart else []
    pairs += [(out.at[0], out.at[1]) for out in outs[2 * apart :]]
    for at, (a, w) in enumerate(pairs):
        gate, up, weight = refs[3 * at : 3 * at + 3]
        hidden = silu_product(gate[...], up[...])
        for tile in range(a.shape[0]):
            a[tile] = hidden[:, tile * LANES : (tile + 1) * LANES]
            w[tile] = weight[pl.ds(tile * LANES, LANES)]


def pack(plane, steps, gate, up, weight, after=()):
    rows, columns = gate.shape[0], weight.shape[1]
    tiles = gate.shape[1] // (4 * LANES)
    grid = 4
    share = tiles // grid
    apart = int(steps[0] == 0)
    single = pltpu.HBM((tiles, rows, LANES), jnp.bfloat16)
    double = pltpu.HBM((2, tiles, rows, LANES), jnp.bfloat16)
    single_spec = pl.BlockSpec((share, rows, LANES), lambda at, plane: (at, 0, 0))
    double_spec = pl.BlockSpec((2, share, rows, LANES), lambda at, plane: (0, at, 0, 0))
    others = len(steps) - apart
    in_specs = []
    for step in steps:

        def across(at, plane, step=step):
            return 0, (plane[0] ^ step) * grid + at

        def down(at, plane, step=step):
            return (plane[0] ^ step) * grid + at, 0

        wide = pl.BlockSpec((rows, share * LANES), across)
        in_specs += [wide, wide, pl.BlockSpec((share * LANES, columns), down)]
    in_specs += [pl.BlockSpec(memory_space=pl.ANY)] * len(after)
    return pl.pallas_call(
        functools.partial(pack_kernel, apart, len(steps)),
        out_shape=[single] * (2 * apart) + [double] * others,
        grid_spec=pltpu.PrefetchScalarGridSpec(
            num_scalar_prefetch=1,
            grid=(grid,),
            in_specs=in_specs,
            out_specs=[single_spec] * (2 * apart) + [double_spec] * others,
        ),
        compiler_params=pltpu.CompilerParams(vmem_limit_bytes=LIMIT),
        cost_estimate=pl.CostEstimate(
            flops=0,
            bytes_accessed=10 * rows * tiles * LANES * len(steps),
            transcendentals=rows * tiles * LANES * len(steps),
        ),
        name="pack",
    )(plane, *[gate, up, weight] * len(steps), *after)


def unpack_pair_kernel(one, two, *refs):
    a, w, held, in_sem, out_sem = refs[-5:]
    ways = [
        (source.at[kind], out.at[at])
        for at, source in enumerate((one, two))
        for kind, out in enumerate((a, w))
    ]
    into = [
        pltpu.make_async_copy(source, held.at[at], in_sem.at[at])
        for at, (source, _) in enumerate(ways)
    ]
    out_of = [
        pltpu.make_async_copy(held.at[at], to, out_sem.at[at]) for at, (_, to) in enumerate(ways)
    ]
    for copy in into:
        copy.start()
    for copy_in, copy_out in zip(into, out_of):
        copy_in.wait()
        copy_out.start()
    for copy in out_of:
        copy.wait()


def unpack_pair(one, two, after):
    return pl.pallas_call(
        unpack_pair_kernel,
        out_shape=[pltpu.HBM(one.shape, one.dtype)] * 2,
        in_specs=[pl.BlockSpec(memory_space=pl.ANY)] * (2 + len(after)),
        out_specs=[pl.BlockSpec(memory_space=pl.ANY)] * 2,
        scratch_shapes=[
            pltpu.VMEM((4,) + one.shape[1:], one.dtype),
            pltpu.SemaphoreType.DMA((4,)),
            pltpu.SemaphoreType.DMA((4,)),
        ],
        compiler_params=pltpu.CompilerParams(vmem_limit_bytes=LIMIT),
        cost_estimate=pl.CostEstimate(flops=0, bytes_accessed=8 * one.size, transcendentals=0),
        name="unpack_pair",
    )(one, two, *after)


def reorder_kernel(count, order_ref, packed, w_12, *refs):
    outs, (held, in_sem, out_sem) = refs[-3 - count : -3], refs[-3:]
    into = [
        pltpu.make_async_copy(source, held.at[at], in_sem.at[at])
        for at, source in enumerate((packed.at[0], w_12.at[0], w_12.at[1], packed.at[1]))
    ]
    out_of = [
        pltpu.make_async_copy(held.at[order_ref[at]], out, out_sem.at[at])
        for at, out in enumerate(outs)
    ]
    for copy in into:
        copy.start()
    for copy in into:
        copy.wait()
    for copy in out_of:
        copy.start()
    for copy in out_of:
        copy.wait()


def reorder(order, packed, w_12):
    shape, count = packed.shape[1:], order.shape[0]
    return pl.pallas_call(
        functools.partial(reorder_kernel, count),
        out_shape=[pltpu.HBM(shape, packed.dtype)] * count,
        in_specs=[pl.BlockSpec(memory_space=pltpu.SMEM)]
        + [pl.BlockSpec(memory_space=pl.ANY)] * 2,
        out_specs=[pl.BlockSpec(memory_space=pl.ANY)] * count,
        scratch_shapes=[
            pltpu.VMEM((4,) + shape, packed.dtype),
            pltpu.SemaphoreType.DMA((4,)),
            pltpu.SemaphoreType.DMA((count,)),
        ],
        compiler_params=pltpu.CompilerParams(vmem_limit_bytes=LIMIT),
        cost_estimate=pl.CostEstimate(flops=0, bytes_accessed=8 * packed.size, transcendentals=0),
        name="reorder",
    )(order, packed, *far([w_12]))


def far(arrays):
    return [pltpu.with_memory_space_constraint(array, pltpu.HBM) for array in arrays]


def multiply(a, right, place, out):
    tiles, rows = a.shape[0], a.shape[1] // 16
    for half in range(2):
        left = jnp.concatenate(
            [
                jnp.concatenate([a[tile, pl.ds(block * rows, rows)] for tile in range(tiles)], axis=1)
                for block in place[2 * half : 2 * half + 2]
            ],
            axis=0,
        )
        total = jnp.dot(left, right, preferred_element_type=jnp.float32)
        for at in range(2):
            out[2 * half + at] = total[at * rows : (at + 1) * rows].astype(out.dtype)


def stack_product_kernel(places, a_at, w_at, choice_ref, *refs):
    stack_ref, *outs, w, a_sem, w_sem = refs[-7:]
    tiles, _, columns = w.shape
    columns //= len(w_at[0])
    rows = stack_ref.shape[1] // 16

    def pick(at):
        ref, index = at
        return refs[ref] if index is None else refs[ref].at[index]

    def w_copy(at, choice):
        return pltpu.make_async_copy(
            pick(w_at[choice][at]), w.at[:, :, pl.ds(at * columns, columns)], w_sem.at[at]
        )

    def a_copy(at):
        return pltpu.make_async_copy(
            pick(a_at[at]), stack_ref.at[:, pl.ds(at * rows, rows)], a_sem.at[at]
        )

    for at in range(len(w_at[0])):
        for choice in range(len(w_at)):

            @pl.when(choice_ref[0] == choice)
            def _():
                w_copy(at, choice).start()

    for group in (1, 2, 3, 0):
        for at in places[group]:
            a_copy(at).start()
    for at in range(len(w_at[0])):
        w_copy(at, 0).wait()
    right = w[...].reshape(tiles * LANES, len(w_at[0]) * columns)
    for group in (1, 2, 3):
        for at in places[group]:
            a_copy(at).wait()
        multiply(stack_ref, right, places[group], outs[group - 1])
    for at in places[0]:
        a_copy(at).wait()


def stack_product(choice, places, a_blocks, w_choices):
    arrays = []

    def at(block):
        array, index = block
        for known, other in enumerate(arrays):
            if other is array:
                return known, index
        arrays.append(array)
        return len(arrays) - 1, index

    a_at = [at(block) for block in a_blocks]
    w_at = [[at(block) for block in blocks] for blocks in w_choices]
    tiles, rows, _ = a_blocks[0][0].shape
    wide = len(w_choices[0]) * w_choices[0][0][0].shape[-1]
    return pl.pallas_call(
        functools.partial(stack_product_kernel, places, a_at, w_at),
        out_shape=[pltpu.VMEM((tiles, 16 * rows, LANES), jnp.bfloat16)]
        + [jax.ShapeDtypeStruct((4, rows, wide), jnp.bfloat16)] * 3,
        in_specs=[pl.BlockSpec(memory_space=pltpu.SMEM)]
        + [pl.BlockSpec(memory_space=pl.ANY)] * len(arrays),
        out_specs=[pl.BlockSpec(memory_space=pltpu.VMEM)] * 4,
        scratch_shapes=[
            pltpu.VMEM((tiles, LANES, wide), jnp.bfloat16),
            pltpu.SemaphoreType.DMA((16,)),
            pltpu.SemaphoreType.DMA((len(w_at[0]),)),
        ],
        compiler_params=pltpu.CompilerParams(vmem_limit_bytes=LIMIT),
        cost_estimate=pl.CostEstimate(
            flops=24 * rows * tiles * LANES * wide,
            bytes_accessed=2 * tiles * LANES * (16 * rows + wide),
            transcendentals=0,
        ),
        name="stack_product",
    )(choice, *arrays)


def product_kernel(places, w_at, choice_ref, a, *refs):
    groups, wide = len(places), len(w_at[0])
    outs, (w, w_sem) = refs[-2 - groups : -2], refs[-2:]
    tiles, _, columns = w.shape
    columns //= wide

    def pick(at):
        ref, index = at
        return refs[ref] if index is None else refs[ref].at[index]

    def w_copy(at, choice):
        return pltpu.make_async_copy(
            pick(w_at[choice][at]), w.at[:, :, pl.ds(at * columns, columns)], w_sem.at[at]
        )

    for at in range(wide):
        for choice in range(len(w_at)):

            @pl.when(choice_ref[0] == choice)
            def _():
                w_copy(at, choice).start()

    for at in range(wide):
        w_copy(at, 0).wait()
    right = w[...].reshape(tiles * LANES, wide * columns)
    for place, out in zip(places, outs):
        multiply(a, right, place, out)


def product(choice, groups, places, rows_stack, w_choices, after=()):
    arrays = []

    def at(block):
        array, index = block
        for known, other in enumerate(arrays):
            if other is array:
                return known, index
        arrays.append(array)
        return len(arrays) - 1, index

    w_at = [[at(block) for block in blocks] for blocks in w_choices]
    tiles, rows, _ = rows_stack.shape
    rows //= 16
    columns = w_choices[-1][0][0].shape[-1]
    wide = len(w_choices[0])
    shape = (4, rows, wide * columns)
    count = len(arrays) + len(after)
    return pl.pallas_call(
        functools.partial(product_kernel, [places[group] for group in groups], w_at),
        out_shape=[
            jax.ShapeDtypeStruct(shape, jnp.float32 if group == 0 else jnp.bfloat16)
            for group in groups
        ],
        in_specs=[
            pl.BlockSpec(memory_space=pltpu.SMEM),
            pl.BlockSpec(memory_space=pltpu.VMEM),
        ]
        + [pl.BlockSpec(memory_space=pl.ANY)] * count,
        out_specs=[pl.BlockSpec(memory_space=pltpu.VMEM)] * len(groups),
        scratch_shapes=[
            pltpu.VMEM((tiles, LANES, wide * columns), jnp.bfloat16),
            pltpu.SemaphoreType.DMA((wide,)),
        ],
        compiler_params=pltpu.CompilerParams(vmem_limit_bytes=LIMIT),
        cost_estimate=pl.CostEstimate(
            flops=8 * len(groups) * rows * tiles * LANES * wide * columns,
            bytes_accessed=2 * tiles * LANES * (4 * len(groups) * rows + wide * columns),
            transcendentals=0,
        ),
        name="product",
    )(choice, pltpu.with_memory_space_constraint(rows_stack, pltpu.VMEM), *arrays, *after)


def add_kernel(kinds, *refs):
    outs, first = refs[-4:], 0
    for kind, relative in enumerate(kinds):
        own, *others = refs[4 * kind : 4 * kind + 4]
        blocks_wide = own.shape[2] // LANES
        for piece in range(4):
            for at in range(blocks_wide):
                total = own[piece, :, pl.ds(at * LANES, LANES)]
                for step, ref in zip((1, 2, 3), others):
                    source = at ^ step if relative else at
                    total += ref[piece, :, pl.ds(source * LANES, LANES)].astype(jnp.float32)
                outs[piece][:, pl.ds((first + at) * LANES, LANES)] = total.astype(jnp.bfloat16)
        first += blocks_wide


def add(terms, kinds, after=()):
    rows = terms[0][0].shape[1]
    columns = sum(own.shape[2] for own, *_ in terms)
    arrays = [array for group in terms for array in group]
    return pl.pallas_call(
        functools.partial(add_kernel, kinds),
        out_shape=[jax.ShapeDtypeStruct((rows, columns), jnp.bfloat16)] * 4,
        in_specs=[pl.BlockSpec(memory_space=pltpu.VMEM)] * len(arrays)
        + [pl.BlockSpec(memory_space=pl.ANY)] * len(after),
        out_specs=[pl.BlockSpec(memory_space=pltpu.VMEM)] * 4,
        compiler_params=pltpu.CompilerParams(vmem_limit_bytes=LIMIT),
        cost_estimate=pl.CostEstimate(
            flops=12 * rows * columns, bytes_accessed=48 * rows * columns, transcendentals=0
        ),
        name="add",
    )(*arrays, *after)


def assemble_kernel(groups, place_ref, *refs):
    out = refs[-1]
    for ref, (fixed, parts) in zip(refs, groups):
        for at, (half, block) in enumerate(parts):
            index = fixed | (half << 3) | (block << 1)
            to = pl.multiple_of((place_ref[half] ^ index) * LANES, LANES)
            out[:, pl.ds(to, LANES)] = ref[:, pl.ds(at * LANES, LANES)]


def assemble(place, pieces):
    arrays = [piece[0] for piece in pieces]
    rows = arrays[0].shape[0]
    columns = sum(array.shape[1] for array in arrays)
    return pl.pallas_call(
        functools.partial(assemble_kernel, [piece[1:] for piece in pieces]),
        out_shape=jax.ShapeDtypeStruct((rows, columns), jnp.bfloat16),
        in_specs=[pl.BlockSpec(memory_space=pltpu.SMEM)]
        + [pl.BlockSpec(memory_space=pltpu.VMEM)] * len(arrays),
        out_specs=pl.BlockSpec(memory_space=pltpu.VMEM),
        compiler_params=pltpu.CompilerParams(vmem_limit_bytes=LIMIT),
        name="assemble",
    )(place, *arrays)


def blocks(gate_pre, up_pre, down_weight):
    n = lax.axis_size("fsdp")
    me = lax.axis_index("fsdp")
    plane = (me // PLANE) % 4
    z_low, z_high = (me // PAIR) % 2, me // (2 * PAIR)
    at_plane = plane.astype(jnp.int32).reshape(1)
    inputs = [
        pltpu.with_memory_space_constraint(array, pltpu.HBM)
        for array in (gate_pre, up_pre, down_weight)
    ]

    def send(array, perm):
        return lax.ppermute(array, "fsdp", perm=perm)

    def to_mid(array):
        return send(array, along_z(n, [(1, 2), (2, 1)]))

    def to_next(array):
        return send(array, along_z(n, [(1, 0), (3, 1), (0, 2), (2, 3)]))

    def to_core(array):
        return send(array, flip(n, CORE))

    def to_pair(array):
        return send(array, flip(n, PAIR))

    a_0, w_0, packed_1, packed_2 = pack(at_plane, (0, 1, 2), *inputs)
    pair_0, mid_0, next_0 = to_pair(a_0), to_mid(w_0), to_next(w_0)
    got_1 = send(packed_1, flip(n, PLANE))
    got_2 = send(packed_2, flip(n, 2 * PLANE))

    (packed_3,) = pack(at_plane, (3,), *inputs, after=(pair_0,))
    packed_3, got_1, got_2 = lax.optimization_barrier((packed_3, got_1, got_2))
    got_3 = send(packed_3, flip(n, 3 * PLANE))
    a_12, w_12 = unpack_pair(got_1, got_2, after=(pair_0, mid_0, next_0))
    pair_12, mid_12 = to_pair(a_12), to_mid(w_12)
    core_0, core_pair_0 = to_core(a_0), to_core(pair_0)

    order = jnp.array([[1, 2, 3], [1, 3, 2], [2, 3, 1], [3, 2, 1]], jnp.int32)[plane]
    got_3, core_0, core_pair_0 = lax.optimization_barrier((got_3, core_0, core_pair_0))
    known = jnp.array([0, 3], jnp.int32)
    a_3, w_3, ordered_1, ordered_2 = reorder(jnp.concatenate([known, order[:2]]), got_3, w_12)
    pair_3 = to_pair(a_3)
    a_12, pair_12, a_3 = lax.optimization_barrier((a_12, pair_12, a_3))
    core_12, core_pair_12 = to_core(a_12), to_core(pair_12)
    mid_3 = to_mid(w_3)
    ordered_1, ordered_2, pair_3, mid_3, mid_12 = lax.optimization_barrier(
        (ordered_1, ordered_2, pair_3, mid_3, mid_12)
    )
    next_1, next_2 = to_next(ordered_1), to_next(ordered_2)
    core_3, core_pair_3 = to_core(a_3), to_core(pair_3)

    a_0, w_0, a_12, w_12, a_3, w_3 = far([a_0, w_0, a_12, w_12, a_3, w_3])
    mid_0, mid_12, mid_3, core_12, core_pair_12 = far([mid_0, mid_12, mid_3, core_12, core_pair_12])
    a_blocks = [(block, None) for block in (a_0, pair_0, core_0, core_pair_0)]
    for block in (a_12, pair_12, core_12, core_pair_12):
        a_blocks += [(block, 0), (block, 1)]
    a_blocks += [(block, None) for block in (a_3, pair_3, core_3, core_pair_3)]
    places = [(0, 2, 1, 3), (4, 8, 6, 10), (5, 9, 7, 11), (12, 14, 13, 15)]
    w_own = [(w_0, None), (w_12, 0), (w_12, 1), (w_3, None)]
    w_mid = [(mid_0, None), (mid_12, 0), (mid_12, 1), (mid_3, None)]
    mid = (z_low ^ z_high).astype(jnp.int32).reshape(1)

    def totals_of(choice, w_choices, calls, after=()):
        totals = {}
        for groups in calls:
            outs = product(choice, groups, places, rows_stack, w_choices, after)
            totals.update(zip(groups, outs))
            after = (outs[0],)
        return [totals[group] for group in sorted(totals)]

    def across_plane(totals):
        return [send(totals[step], flip(n, step * PLANE)) for step in (1, 2, 3)]

    pieces = []

    def spread(terms, kinds, parts, after=()):
        summed = add(terms, kinds, after)
        for piece in range(4):
            mask = (piece >> 1) * PAIR + (piece & 1) * CORE
            block = send(summed[piece], flip(n, mask)) if mask else summed[piece]
            pieces.append((block, ((piece >> 1) << 4) | (piece & 1), parts))

    rows_stack, *own = stack_product(mid, places, a_blocks, [w_own, w_mid])
    own = totals_of(mid, [w_own, w_mid], ([0],), (own[0],)) + own
    own[0], got_3 = lax.optimization_barrier((own[0], got_3))
    (ordered_3,) = reorder(order[2:], got_3, w_12)
    next_3 = to_next(ordered_3)
    own_sums = across_plane(own)
    first, one, two, three = [(block, None) for block in (next_0, next_1, next_2, next_3)]
    w_low = [[first, one], [one, first], [one, two], [one, two]]
    w_high = [[two, three], [two, three], [first, three], [three, first]]
    low = totals_of(at_plane, w_low, ([3, 1, 2, 0],), (own[0],))
    low[1], low[2], low[3], *own_sums = lax.optimization_barrier((*low[1:], *own_sums))
    low_sums = across_plane(low)
    high = totals_of(at_plane, w_high, ([3, 1, 2], [0]), (low[0],))
    high[1], high[2], high[3], *low_sums = lax.optimization_barrier((*high[1:], *low_sums))
    high_sums = across_plane(high)
    spread(
        [(own[0], *own_sums), (low[0], *low_sums)],
        (True, False),
        [(0, 0), (0, 1), (0, 2), (0, 3), (1, 0), (1, 1)],
        (high[0],),
    )
    spread([(high[0], *high_sums)], (False,), [(1, 2), (1, 3)])
    across = z_low * 16 + z_high * 8 + me % 2
    place = jnp.stack([across + plane * 2, across]).astype(jnp.int32)
    return assemble(place, pieces)


def shards(gate_pre, up_pre, down_weight):
    hidden = silu_product(gate_pre, up_pre)
    terms = jnp.dot(
        hidden,
        lax.all_gather(down_weight, "fsdp", axis=1, tiled=True),
        preferred_element_type=jnp.float32,
    )
    totals = lax.psum(terms, "tp")
    share = totals.shape[1] // lax.axis_size("tp")
    result = lax.dynamic_slice_in_dim(totals, lax.axis_index("tp") * share, share, 1)
    return result.astype(jnp.bfloat16)


def solution(mesh):
    in_blocks = mesh.shape["tp"] == 1 and mesh.shape["fsdp"] == 4 * PAIR
    return jax.shard_map(
        blocks if in_blocks else shards,
        mesh=mesh,
        in_specs=(P("fsdp", "tp"), P("fsdp", "tp"), P("tp", "fsdp")),
        out_specs=P("fsdp", "tp"),
        check_vma=False,
    )
```

```python
import functools

import jax
import jax.numpy as jnp
from jax import lax
from jax.experimental import pallas as pl
from jax.experimental.pallas import tpu as pltpu
from jax.sharding import PartitionSpec as P

CORE, PLANE, PAIR = 1, 2, 8
LIMIT = 10 * 1024 * 1024
LANES = 128


def flip(n, mask):
    return [(source, source ^ mask) for source in range(n)]


def along_z(n, pairs):
    low = PAIR
    return [(a * low + rest, b * low + rest) for a, b in pairs for rest in range(low)]


def silu_product(gate, up):
    return (jax.nn.silu(gate.astype(jnp.float32)) * up.astype(jnp.float32)).astype(jnp.bfloat16)


def pack_kernel(apart, count, plane_ref, *refs):
    outs = refs[len(refs) - count - apart :]
    pairs = [(outs[0], outs[1])] if apart else []
    pairs += [(out.at[0], out.at[1]) for out in outs[2 * apart :]]
    for at, (a, w) in enumerate(pairs):
        gate, up, weight = refs[3 * at : 3 * at + 3]
        hidden = silu_product(gate[...], up[...])
        for tile in range(a.shape[0]):
            a[tile] = hidden[:, tile * LANES : (tile + 1) * LANES]
            w[tile] = weight[pl.ds(tile * LANES, LANES)]


def pack(plane, steps, gate, up, weight, after=()):
    rows, columns = gate.shape[0], weight.shape[1]
    tiles = gate.shape[1] // (4 * LANES)
    grid = 4
    share = tiles // grid
    apart = int(steps[0] == 0)
    single = pltpu.HBM((tiles, rows, LANES), jnp.bfloat16)
    double = jax.ShapeDtypeStruct((2, tiles, rows, LANES), jnp.bfloat16)
    single_spec = pl.BlockSpec((share, rows, LANES), lambda at, plane: (at, 0, 0))
    double_spec = pl.BlockSpec((2, share, rows, LANES), lambda at, plane: (0, at, 0, 0))
    others = len(steps) - apart
    in_specs = []
    for step in steps:

        def across(at, plane, step=step):
            return 0, (plane[0] ^ step) * grid + at

        def down(at, plane, step=step):
            return (plane[0] ^ step) * grid + at, 0

        wide = pl.BlockSpec((rows, share * LANES), across)
        in_specs += [wide, wide, pl.BlockSpec((share * LANES, columns), down)]
    in_specs += [pl.BlockSpec(memory_space=pl.ANY)] * len(after)
    return pl.pallas_call(
        functools.partial(pack_kernel, apart, len(steps)),
        out_shape=[single] * (2 * apart) + [double] * others,
        grid_spec=pltpu.PrefetchScalarGridSpec(
            num_scalar_prefetch=1,
            grid=(grid,),
            in_specs=in_specs,
            out_specs=[single_spec] * (2 * apart) + [double_spec] * others,
        ),
        compiler_params=pltpu.CompilerParams(vmem_limit_bytes=LIMIT),
        cost_estimate=pl.CostEstimate(
            flops=0,
            bytes_accessed=10 * rows * tiles * LANES * len(steps),
            transcendentals=rows * tiles * LANES * len(steps),
        ),
        name="pack",
    )(plane, *[gate, up, weight] * len(steps), *after)


def unpack_pair_kernel(one, two, *refs):
    a, w, held, in_sem, out_sem = refs[-5:]
    ways = [
        (source.at[kind], out.at[at])
        for at, source in enumerate((one, two))
        for kind, out in enumerate((a, w))
    ]
    into = [
        pltpu.make_async_copy(source, held.at[at], in_sem.at[at])
        for at, (source, _) in enumerate(ways)
    ]
    out_of = [
        pltpu.make_async_copy(held.at[at], to, out_sem.at[at]) for at, (_, to) in enumerate(ways)
    ]
    for copy in into:
        copy.start()
    for copy_in, copy_out in zip(into, out_of):
        copy_in.wait()
        copy_out.start()
    for copy in out_of:
        copy.wait()


def unpack_pair(one, two, after):
    return pl.pallas_call(
        unpack_pair_kernel,
        out_shape=[pltpu.HBM(one.shape, one.dtype)] * 2,
        in_specs=[pl.BlockSpec(memory_space=pl.ANY)] * (2 + len(after)),
        out_specs=[pl.BlockSpec(memory_space=pl.ANY)] * 2,
        scratch_shapes=[
            pltpu.VMEM((4,) + one.shape[1:], one.dtype),
            pltpu.SemaphoreType.DMA((4,)),
            pltpu.SemaphoreType.DMA((4,)),
        ],
        compiler_params=pltpu.CompilerParams(vmem_limit_bytes=LIMIT),
        cost_estimate=pl.CostEstimate(flops=0, bytes_accessed=8 * one.size, transcendentals=0),
        name="unpack_pair",
    )(one, two, *after)


def reorder_kernel(count, order_ref, packed, w_12, *refs):
    outs, (held, in_sem, out_sem) = refs[-3 - count : -3], refs[-3:]
    into = [
        pltpu.make_async_copy(source, held.at[at], in_sem.at[at])
        for at, source in enumerate((packed.at[0], w_12.at[0], w_12.at[1], packed.at[1]))
    ]
    out_of = [
        pltpu.make_async_copy(held.at[order_ref[at]], out, out_sem.at[at])
        for at, out in enumerate(outs)
    ]
    for copy in into:
        copy.start()
    for copy in into:
        copy.wait()
    for copy in out_of:
        copy.start()
    for copy in out_of:
        copy.wait()


def reorder(order, packed, w_12):
    shape, count = packed.shape[1:], order.shape[0]
    return pl.pallas_call(
        functools.partial(reorder_kernel, count),
        out_shape=[pltpu.HBM(shape, packed.dtype)] * count,
        in_specs=[pl.BlockSpec(memory_space=pltpu.SMEM)]
        + [pl.BlockSpec(memory_space=pl.ANY)] * 2,
        out_specs=[pl.BlockSpec(memory_space=pl.ANY)] * count,
        scratch_shapes=[
            pltpu.VMEM((4,) + shape, packed.dtype),
            pltpu.SemaphoreType.DMA((4,)),
            pltpu.SemaphoreType.DMA((count,)),
        ],
        compiler_params=pltpu.CompilerParams(vmem_limit_bytes=LIMIT),
        cost_estimate=pl.CostEstimate(flops=0, bytes_accessed=8 * packed.size, transcendentals=0),
        name="reorder",
    )(order, packed, *far([w_12]))


def far(arrays):
    return [pltpu.with_memory_space_constraint(array, pltpu.HBM) for array in arrays]


def multiply(a, right, place, out):
    tiles, rows = a.shape[0], a.shape[1] // 16
    for half in range(2):
        left = jnp.concatenate(
            [
                jnp.concatenate([a[tile, pl.ds(block * rows, rows)] for tile in range(tiles)], axis=1)
                for block in place[2 * half : 2 * half + 2]
            ],
            axis=0,
        )
        total = jnp.dot(left, right, preferred_element_type=jnp.float32)
        for at in range(2):
            out[2 * half + at] = total[at * rows : (at + 1) * rows].astype(out.dtype)


def stack_product_kernel(places, a_at, w_at, choice_ref, *refs):
    stack_ref, *outs, w, a_sem, w_sem = refs[-7:]
    tiles, _, columns = w.shape
    columns //= len(w_at[0])
    rows = stack_ref.shape[1] // 16

    def pick(at):
        ref, index = at
        return refs[ref] if index is None else refs[ref].at[index]

    def w_copy(at, choice):
        return pltpu.make_async_copy(
            pick(w_at[choice][at]), w.at[:, :, pl.ds(at * columns, columns)], w_sem.at[at]
        )

    def a_copy(at):
        return pltpu.make_async_copy(
            pick(a_at[at]), stack_ref.at[:, pl.ds(at * rows, rows)], a_sem.at[at]
        )

    for at in range(len(w_at[0])):
        for choice in range(len(w_at)):

            @pl.when(choice_ref[0] == choice)
            def _():
                w_copy(at, choice).start()

    for group in (1, 2, 3, 0):
        for at in places[group]:
            a_copy(at).start()
    for at in range(len(w_at[0])):
        w_copy(at, 0).wait()
    right = w[...].reshape(tiles * LANES, len(w_at[0]) * columns)
    for group in (1, 2, 3):
        for at in places[group]:
            a_copy(at).wait()
        multiply(stack_ref, right, places[group], outs[group - 1])
    for at in places[0]:
        a_copy(at).wait()


def stack_product(choice, places, a_blocks, w_choices):
    arrays = []

    def at(block):
        array, index = block
        for known, other in enumerate(arrays):
            if other is array:
                return known, index
        arrays.append(array)
        return len(arrays) - 1, index

    a_at = [at(block) for block in a_blocks]
    w_at = [[at(block) for block in blocks] for blocks in w_choices]
    tiles, rows, _ = a_blocks[0][0].shape
    wide = len(w_choices[0]) * w_choices[0][0][0].shape[-1]
    return pl.pallas_call(
        functools.partial(stack_product_kernel, places, a_at, w_at),
        out_shape=[pltpu.VMEM((tiles, 16 * rows, LANES), jnp.bfloat16)]
        + [jax.ShapeDtypeStruct((4, rows, wide), jnp.bfloat16)] * 3,
        in_specs=[pl.BlockSpec(memory_space=pltpu.SMEM)]
        + [pl.BlockSpec(memory_space=pl.ANY)] * len(arrays),
        out_specs=[pl.BlockSpec(memory_space=pltpu.VMEM)] * 4,
        scratch_shapes=[
            pltpu.VMEM((tiles, LANES, wide), jnp.bfloat16),
            pltpu.SemaphoreType.DMA((16,)),
            pltpu.SemaphoreType.DMA((len(w_at[0]),)),
        ],
        compiler_params=pltpu.CompilerParams(vmem_limit_bytes=LIMIT),
        cost_estimate=pl.CostEstimate(
            flops=24 * rows * tiles * LANES * wide,
            bytes_accessed=2 * tiles * LANES * (16 * rows + wide),
            transcendentals=0,
        ),
        name="stack_product",
    )(choice, *arrays)


def product_kernel(places, w_at, choice_ref, a, *refs):
    groups, wide = len(places), len(w_at[0])
    outs, (w, w_sem) = refs[-2 - groups : -2], refs[-2:]
    tiles, _, columns = w.shape
    columns //= wide

    def pick(at):
        ref, index = at
        return refs[ref] if index is None else refs[ref].at[index]

    def w_copy(at, choice):
        return pltpu.make_async_copy(
            pick(w_at[choice][at]), w.at[:, :, pl.ds(at * columns, columns)], w_sem.at[at]
        )

    for at in range(wide):
        for choice in range(len(w_at)):

            @pl.when(choice_ref[0] == choice)
            def _():
                w_copy(at, choice).start()

    for at in range(wide):
        w_copy(at, 0).wait()
    right = w[...].reshape(tiles * LANES, wide * columns)
    for place, out in zip(places, outs):
        multiply(a, right, place, out)


def product(choice, groups, places, rows_stack, w_choices, after=()):
    arrays = []

    def at(block):
        array, index = block
        for known, other in enumerate(arrays):
            if other is array:
                return known, index
        arrays.append(array)
        return len(arrays) - 1, index

    w_at = [[at(block) for block in blocks] for blocks in w_choices]
    tiles, rows, _ = rows_stack.shape
    rows //= 16
    columns = w_choices[-1][0][0].shape[-1]
    wide = len(w_choices[0])
    shape = (4, rows, wide * columns)
    count = len(arrays) + len(after)
    return pl.pallas_call(
        functools.partial(product_kernel, [places[group] for group in groups], w_at),
        out_shape=[
            jax.ShapeDtypeStruct(shape, jnp.float32 if group == 0 else jnp.bfloat16)
            for group in groups
        ],
        in_specs=[
            pl.BlockSpec(memory_space=pltpu.SMEM),
            pl.BlockSpec(memory_space=pltpu.VMEM),
        ]
        + [pl.BlockSpec(memory_space=pl.ANY)] * count,
        out_specs=[pl.BlockSpec(memory_space=pltpu.VMEM)] * len(groups),
        scratch_shapes=[
            pltpu.VMEM((tiles, LANES, wide * columns), jnp.bfloat16),
            pltpu.SemaphoreType.DMA((wide,)),
        ],
        compiler_params=pltpu.CompilerParams(vmem_limit_bytes=LIMIT),
        cost_estimate=pl.CostEstimate(
            flops=8 * len(groups) * rows * tiles * LANES * wide * columns,
            bytes_accessed=2 * tiles * LANES * (4 * len(groups) * rows + wide * columns),
            transcendentals=0,
        ),
        name="product",
    )(choice, pltpu.with_memory_space_constraint(rows_stack, pltpu.VMEM), *arrays, *after)


def add_kernel(kinds, *refs):
    outs, first = refs[-4:], 0
    for kind, relative in enumerate(kinds):
        own, *others = refs[4 * kind : 4 * kind + 4]
        blocks_wide = own.shape[2] // LANES
        for piece in range(4):
            for at in range(blocks_wide):
                total = own[piece, :, pl.ds(at * LANES, LANES)]
                for step, ref in zip((1, 2, 3), others):
                    source = at ^ step if relative else at
                    total += ref[piece, :, pl.ds(source * LANES, LANES)].astype(jnp.float32)
                outs[piece][:, pl.ds((first + at) * LANES, LANES)] = total.astype(jnp.bfloat16)
        first += blocks_wide


def add(terms, kinds, after=()):
    rows = terms[0][0].shape[1]
    columns = sum(own.shape[2] for own, *_ in terms)
    arrays = [array for group in terms for array in group]
    return pl.pallas_call(
        functools.partial(add_kernel, kinds),
        out_shape=[jax.ShapeDtypeStruct((rows, columns), jnp.bfloat16)] * 4,
        in_specs=[pl.BlockSpec(memory_space=pltpu.VMEM)] * len(arrays)
        + [pl.BlockSpec(memory_space=pl.ANY)] * len(after),
        out_specs=[pl.BlockSpec(memory_space=pltpu.VMEM)] * 4,
        compiler_params=pltpu.CompilerParams(vmem_limit_bytes=LIMIT),
        cost_estimate=pl.CostEstimate(
            flops=12 * rows * columns, bytes_accessed=48 * rows * columns, transcendentals=0
        ),
        name="add",
    )(*arrays, *after)


def assemble_kernel(groups, place_ref, *refs):
    out = refs[-1]
    for ref, (fixed, parts) in zip(refs, groups):
        for at, (half, block) in enumerate(parts):
            index = fixed | (half << 3) | (block << 1)
            to = pl.multiple_of((place_ref[half] ^ index) * LANES, LANES)
            out[:, pl.ds(to, LANES)] = ref[:, pl.ds(at * LANES, LANES)]


def assemble(place, pieces):
    arrays = [piece[0] for piece in pieces]
    rows = arrays[0].shape[0]
    columns = sum(array.shape[1] for array in arrays)
    return pl.pallas_call(
        functools.partial(assemble_kernel, [piece[1:] for piece in pieces]),
        out_shape=jax.ShapeDtypeStruct((rows, columns), jnp.bfloat16),
        in_specs=[pl.BlockSpec(memory_space=pltpu.SMEM)]
        + [pl.BlockSpec(memory_space=pltpu.VMEM)] * len(arrays),
        out_specs=pl.BlockSpec(memory_space=pltpu.VMEM),
        compiler_params=pltpu.CompilerParams(vmem_limit_bytes=LIMIT),
        name="assemble",
    )(place, *arrays)


def blocks(gate_pre, up_pre, down_weight):
    n = lax.axis_size("fsdp")
    me = lax.axis_index("fsdp")
    plane = (me // PLANE) % 4
    z_low, z_high = (me // PAIR) % 2, me // (2 * PAIR)
    at_plane = plane.astype(jnp.int32).reshape(1)
    inputs = [
        pltpu.with_memory_space_constraint(array, pltpu.HBM)
        for array in (gate_pre, up_pre, down_weight)
    ]

    def send(array, perm):
        return lax.ppermute(array, "fsdp", perm=perm)

    def to_mid(array):
        return send(array, along_z(n, [(1, 2), (2, 1)]))

    def to_next(array):
        return send(array, along_z(n, [(1, 0), (3, 1), (0, 2), (2, 3)]))

    def to_core(array):
        return send(array, flip(n, CORE))

    def to_pair(array):
        return send(array, flip(n, PAIR))

    a_0, w_0, packed_1, packed_2 = pack(at_plane, (0, 1, 2), *inputs)
    pair_0, mid_0, next_0 = to_pair(a_0), to_mid(w_0), to_next(w_0)
    got_1 = send(packed_1, flip(n, PLANE))
    got_2 = send(packed_2, flip(n, 2 * PLANE))

    (packed_3,) = pack(at_plane, (3,), *inputs, after=(pair_0,))
    packed_3, got_1, got_2 = lax.optimization_barrier((packed_3, got_1, got_2))
    got_3 = send(packed_3, flip(n, 3 * PLANE))
    a_12, w_12 = unpack_pair(got_1, got_2, after=(pair_0,))
    pair_12, mid_12 = to_pair(a_12), to_mid(w_12)
    pair_0, mid_0, next_0 = lax.optimization_barrier((pair_0, mid_0, next_0))
    core_0, core_pair_0 = to_core(a_0), to_core(pair_0)

    order = jnp.array([[1, 2, 3], [1, 3, 2], [2, 3, 1], [3, 2, 1]], jnp.int32)[plane]
    got_3, core_0, core_pair_0 = lax.optimization_barrier((got_3, core_0, core_pair_0))
    known = jnp.array([0, 3], jnp.int32)
    a_3, w_3, ordered_1, ordered_2 = reorder(jnp.concatenate([known, order[:2]]), got_3, w_12)
    pair_3 = to_pair(a_3)
    a_12, pair_12, a_3 = lax.optimization_barrier((a_12, pair_12, a_3))
    core_12, core_pair_12 = to_core(a_12), to_core(pair_12)
    mid_3 = to_mid(w_3)
    ordered_1, ordered_2, pair_3, mid_3, mid_12 = lax.optimization_barrier(
        (ordered_1, ordered_2, pair_3, mid_3, mid_12)
    )
    next_1, next_2 = to_next(ordered_1), to_next(ordered_2)
    core_3, core_pair_3 = to_core(a_3), to_core(pair_3)

    a_0, w_0, a_12, w_12, a_3, w_3 = far([a_0, w_0, a_12, w_12, a_3, w_3])
    mid_0, mid_12, mid_3, core_12, core_pair_12 = far([mid_0, mid_12, mid_3, core_12, core_pair_12])
    a_blocks = [(block, None) for block in (a_0, pair_0, core_0, core_pair_0)]
    for block in (a_12, pair_12, core_12, core_pair_12):
        a_blocks += [(block, 0), (block, 1)]
    a_blocks += [(block, None) for block in (a_3, pair_3, core_3, core_pair_3)]
    places = [(0, 2, 1, 3), (4, 8, 6, 10), (5, 9, 7, 11), (12, 14, 13, 15)]
    w_own = [(w_0, None), (w_12, 0), (w_12, 1), (w_3, None)]
    w_mid = [(mid_0, None), (mid_12, 0), (mid_12, 1), (mid_3, None)]
    mid = (z_low ^ z_high).astype(jnp.int32).reshape(1)

    def totals_of(choice, w_choices, calls, after=()):
        totals = {}
        for groups in calls:
            outs = product(choice, groups, places, rows_stack, w_choices, after)
            totals.update(zip(groups, outs))
            after = (outs[0],)
        return [totals[group] for group in sorted(totals)]

    def across_plane(totals):
        return [send(totals[step], flip(n, step * PLANE)) for step in (1, 2, 3)]

    pieces = []

    def spread(terms, kinds, parts, after=()):
        summed = add(terms, kinds, after)
        for piece in range(4):
            mask = (piece >> 1) * PAIR + (piece & 1) * CORE
            block = send(summed[piece], flip(n, mask)) if mask else summed[piece]
            pieces.append((block, ((piece >> 1) << 4) | (piece & 1), parts))

    rows_stack, *own = stack_product(mid, places, a_blocks, [w_own, w_mid])
    own = totals_of(mid, [w_own, w_mid], ([0],), (own[0],)) + own
    own[1], got_3 = lax.optimization_barrier((own[1], got_3))
    (ordered_3,) = reorder(order[2:], got_3, w_12)
    next_3 = to_next(ordered_3)
    own_sums = across_plane(own)
    first, one, two, three = [(block, None) for block in (next_0, next_1, next_2, next_3)]
    w_low = [[first, one], [one, first], [one, two], [one, two]]
    w_high = [[two, three], [two, three], [first, three], [three, first]]
    low = totals_of(at_plane, w_low, ([3, 1, 2, 0],), (own[0],))
    low[1], low[2], low[3], *own_sums = lax.optimization_barrier((*low[1:], *own_sums))
    low_sums = across_plane(low)
    high = totals_of(at_plane, w_high, ([3, 1, 2], [0]), (low[0],))
    high[1], high[2], high[3], *low_sums = lax.optimization_barrier((*high[1:], *low_sums))
    high_sums = across_plane(high)
    spread(
        [(own[0], *own_sums), (low[0], *low_sums)],
        (True, False),
        [(0, 0), (0, 1), (0, 2), (0, 3), (1, 0), (1, 1)],
        (high[0],),
    )
    spread([(high[0], *high_sums)], (False,), [(1, 2), (1, 3)])
    across = z_low * 16 + z_high * 8 + me % 2
    place = jnp.stack([across + plane * 2, across]).astype(jnp.int32)
    return assemble(place, pieces)


def shards(gate_pre, up_pre, down_weight):
    hidden = silu_product(gate_pre, up_pre)
    terms = jnp.dot(
        hidden,
        lax.all_gather(down_weight, "fsdp", axis=1, tiled=True),
        preferred_element_type=jnp.float32,
    )
    totals = lax.psum(terms, "tp")
    share = totals.shape[1] // lax.axis_size("tp")
    result = lax.dynamic_slice_in_dim(totals, lax.axis_index("tp") * share, share, 1)
    return result.astype(jnp.bfloat16)


def solution(mesh):
    in_blocks = mesh.shape["tp"] == 1 and mesh.shape["fsdp"] == 4 * PAIR
    return jax.shard_map(
        blocks if in_blocks else shards,
        mesh=mesh,
        in_specs=(P("fsdp", "tp"), P("fsdp", "tp"), P("tp", "fsdp")),
        out_specs=P("fsdp", "tp"),
        check_vma=False,
    )
```

```python
import functools

import jax
import jax.numpy as jnp
from jax import lax
from jax.experimental import pallas as pl
from jax.experimental.pallas import tpu as pltpu
from jax.sharding import PartitionSpec as P

CORE, PLANE, PAIR = 1, 2, 8
LIMIT = 10 * 1024 * 1024
LANES = 128


def flip(n, mask):
    return [(source, source ^ mask) for source in range(n)]


def along_z(n, pairs):
    low = PAIR
    return [(a * low + rest, b * low + rest) for a, b in pairs for rest in range(low)]


def silu_product(gate, up):
    return (jax.nn.silu(gate.astype(jnp.float32)) * up.astype(jnp.float32)).astype(jnp.bfloat16)


def pack_kernel(apart, count, plane_ref, *refs):
    outs = refs[len(refs) - count - apart :]
    pairs = [(outs[0], outs[1])] if apart else []
    pairs += [(out.at[0], out.at[1]) for out in outs[2 * apart :]]
    for at, (a, w) in enumerate(pairs):
        gate, up, weight = refs[3 * at : 3 * at + 3]
        hidden = silu_product(gate[...], up[...])
        for tile in range(a.shape[0]):
            a[tile] = hidden[:, tile * LANES : (tile + 1) * LANES]
            w[tile] = weight[pl.ds(tile * LANES, LANES)]


def pack(plane, steps, gate, up, weight, after=()):
    rows, columns = gate.shape[0], weight.shape[1]
    tiles = gate.shape[1] // (4 * LANES)
    grid = 4
    share = tiles // grid
    apart = int(steps[0] == 0)
    single = pltpu.HBM((tiles, rows, LANES), jnp.bfloat16)
    double = jax.ShapeDtypeStruct((2, tiles, rows, LANES), jnp.bfloat16)
    single_spec = pl.BlockSpec((share, rows, LANES), lambda at, plane: (at, 0, 0))
    double_spec = pl.BlockSpec((2, share, rows, LANES), lambda at, plane: (0, at, 0, 0))
    others = len(steps) - apart
    in_specs = []
    for step in steps:

        def across(at, plane, step=step):
            return 0, (plane[0] ^ step) * grid + at

        def down(at, plane, step=step):
            return (plane[0] ^ step) * grid + at, 0

        wide = pl.BlockSpec((rows, share * LANES), across)
        in_specs += [wide, wide, pl.BlockSpec((share * LANES, columns), down)]
    in_specs += [pl.BlockSpec(memory_space=pl.ANY)] * len(after)
    return pl.pallas_call(
        functools.partial(pack_kernel, apart, len(steps)),
        out_shape=[single] * (2 * apart) + [double] * others,
        grid_spec=pltpu.PrefetchScalarGridSpec(
            num_scalar_prefetch=1,
            grid=(grid,),
            in_specs=in_specs,
            out_specs=[single_spec] * (2 * apart) + [double_spec] * others,
        ),
        compiler_params=pltpu.CompilerParams(vmem_limit_bytes=LIMIT),
        cost_estimate=pl.CostEstimate(
            flops=0,
            bytes_accessed=10 * rows * tiles * LANES * len(steps),
            transcendentals=rows * tiles * LANES * len(steps),
        ),
        name="pack",
    )(plane, *[gate, up, weight] * len(steps), *after)


def unpack_pair_kernel(one, two, *refs):
    a, w, held, in_sem, out_sem = refs[-5:]
    ways = [
        (source.at[kind], out.at[at])
        for at, source in enumerate((one, two))
        for kind, out in enumerate((a, w))
    ]
    into = [
        pltpu.make_async_copy(source, held.at[at], in_sem.at[at])
        for at, (source, _) in enumerate(ways)
    ]
    out_of = [
        pltpu.make_async_copy(held.at[at], to, out_sem.at[at]) for at, (_, to) in enumerate(ways)
    ]
    for copy in into:
        copy.start()
    for copy_in, copy_out in zip(into, out_of):
        copy_in.wait()
        copy_out.start()
    for copy in out_of:
        copy.wait()


def unpack_pair(one, two, after):
    return pl.pallas_call(
        unpack_pair_kernel,
        out_shape=[pltpu.HBM(one.shape, one.dtype)] * 2,
        in_specs=[pl.BlockSpec(memory_space=pl.ANY)] * (2 + len(after)),
        out_specs=[pl.BlockSpec(memory_space=pl.ANY)] * 2,
        scratch_shapes=[
            pltpu.VMEM((4,) + one.shape[1:], one.dtype),
            pltpu.SemaphoreType.DMA((4,)),
            pltpu.SemaphoreType.DMA((4,)),
        ],
        compiler_params=pltpu.CompilerParams(vmem_limit_bytes=LIMIT),
        cost_estimate=pl.CostEstimate(flops=0, bytes_accessed=8 * one.size, transcendentals=0),
        name="unpack_pair",
    )(one, two, *after)


def unpack_kernel(packed, a, w, held, in_sem, out_sem):
    into = [pltpu.make_async_copy(packed.at[at], held.at[at], in_sem.at[at]) for at in range(2)]
    out_of = [
        pltpu.make_async_copy(held.at[at], out, out_sem.at[at]) for at, out in enumerate((a, w))
    ]
    for copy in into:
        copy.start()
    for copy_in, copy_out in zip(into, out_of):
        copy_in.wait()
        copy_out.start()
    for copy in out_of:
        copy.wait()


def unpack(packed):
    return pl.pallas_call(
        unpack_kernel,
        out_shape=[pltpu.HBM(packed.shape[1:], packed.dtype)] * 2,
        in_specs=[pl.BlockSpec(memory_space=pl.ANY)],
        out_specs=[pl.BlockSpec(memory_space=pl.ANY)] * 2,
        scratch_shapes=[
            pltpu.VMEM(packed.shape, packed.dtype),
            pltpu.SemaphoreType.DMA((2,)),
            pltpu.SemaphoreType.DMA((2,)),
        ],
        compiler_params=pltpu.CompilerParams(vmem_limit_bytes=LIMIT),
        cost_estimate=pl.CostEstimate(flops=0, bytes_accessed=4 * packed.size, transcendentals=0),
        name="unpack",
    )(packed)


def reorder_kernel(count, order_ref, packed, w_12, *refs):
    outs, (held, in_sem, out_sem) = refs[-3 - count : -3], refs[-3:]
    into = [
        pltpu.make_async_copy(source, held.at[at], in_sem.at[at])
        for at, source in enumerate((packed.at[0], w_12.at[0], w_12.at[1], packed.at[1]))
    ]
    out_of = [
        pltpu.make_async_copy(held.at[order_ref[at]], out, out_sem.at[at])
        for at, out in enumerate(outs)
    ]
    for copy in into:
        copy.start()
    for copy in into:
        copy.wait()
    for copy in out_of:
        copy.start()
    for copy in out_of:
        copy.wait()


def reorder(order, packed, w_12):
    shape, count = packed.shape[1:], order.shape[0]
    return pl.pallas_call(
        functools.partial(reorder_kernel, count),
        out_shape=[pltpu.HBM(shape, packed.dtype)] * count,
        in_specs=[pl.BlockSpec(memory_space=pltpu.SMEM)]
        + [pl.BlockSpec(memory_space=pl.ANY)] * 2,
        out_specs=[pl.BlockSpec(memory_space=pl.ANY)] * count,
        scratch_shapes=[
            pltpu.VMEM((4,) + shape, packed.dtype),
            pltpu.SemaphoreType.DMA((4,)),
            pltpu.SemaphoreType.DMA((count,)),
        ],
        compiler_params=pltpu.CompilerParams(vmem_limit_bytes=LIMIT),
        cost_estimate=pl.CostEstimate(flops=0, bytes_accessed=8 * packed.size, transcendentals=0),
        name="reorder",
    )(order, packed, *far([w_12]))


def far(arrays):
    return [pltpu.with_memory_space_constraint(array, pltpu.HBM) for array in arrays]


def multiply(a, right, place, out):
    tiles, rows = a.shape[0], a.shape[1] // 16
    for half in range(2):
        left = jnp.concatenate(
            [
                jnp.concatenate([a[tile, pl.ds(block * rows, rows)] for tile in range(tiles)], axis=1)
                for block in place[2 * half : 2 * half + 2]
            ],
            axis=0,
        )
        total = jnp.dot(left, right, preferred_element_type=jnp.float32)
        for at in range(2):
            out[2 * half + at] = total[at * rows : (at + 1) * rows].astype(out.dtype)


def stack_product_kernel(places, a_at, w_at, choice_ref, *refs):
    stack_ref, *outs, w, a_sem, w_sem = refs[-7:]
    tiles, _, columns = w.shape
    columns //= len(w_at[0])
    rows = stack_ref.shape[1] // 16

    def pick(at):
        ref, index = at
        return refs[ref] if index is None else refs[ref].at[index]

    def w_copy(at, choice):
        return pltpu.make_async_copy(
            pick(w_at[choice][at]), w.at[:, :, pl.ds(at * columns, columns)], w_sem.at[at]
        )

    def a_copy(at):
        return pltpu.make_async_copy(
            pick(a_at[at]), stack_ref.at[:, pl.ds(at * rows, rows)], a_sem.at[at]
        )

    for at in range(len(w_at[0])):
        for choice in range(len(w_at)):

            @pl.when(choice_ref[0] == choice)
            def _():
                w_copy(at, choice).start()

    for group in (1, 2, 3, 0):
        for at in places[group]:
            a_copy(at).start()
    for at in range(len(w_at[0])):
        w_copy(at, 0).wait()
    right = w[...].reshape(tiles * LANES, len(w_at[0]) * columns)
    for group in (1, 2, 3):
        for at in places[group]:
            a_copy(at).wait()
        multiply(stack_ref, right, places[group], outs[group - 1])
    for at in places[0]:
        a_copy(at).wait()


def stack_product(choice, places, a_blocks, w_choices):
    arrays = []

    def at(block):
        array, index = block
        for known, other in enumerate(arrays):
            if other is array:
                return known, index
        arrays.append(array)
        return len(arrays) - 1, index

    a_at = [at(block) for block in a_blocks]
    w_at = [[at(block) for block in blocks] for blocks in w_choices]
    tiles, rows, _ = a_blocks[0][0].shape
    wide = len(w_choices[0]) * w_choices[0][0][0].shape[-1]
    return pl.pallas_call(
        functools.partial(stack_product_kernel, places, a_at, w_at),
        out_shape=[pltpu.VMEM((tiles, 16 * rows, LANES), jnp.bfloat16)]
        + [jax.ShapeDtypeStruct((4, rows, wide), jnp.bfloat16)] * 3,
        in_specs=[pl.BlockSpec(memory_space=pltpu.SMEM)]
        + [pl.BlockSpec(memory_space=pl.ANY)] * len(arrays),
        out_specs=[pl.BlockSpec(memory_space=pltpu.VMEM)] * 4,
        scratch_shapes=[
            pltpu.VMEM((tiles, LANES, wide), jnp.bfloat16),
            pltpu.SemaphoreType.DMA((16,)),
            pltpu.SemaphoreType.DMA((len(w_at[0]),)),
        ],
        compiler_params=pltpu.CompilerParams(vmem_limit_bytes=LIMIT),
        cost_estimate=pl.CostEstimate(
            flops=24 * rows * tiles * LANES * wide,
            bytes_accessed=2 * tiles * LANES * (16 * rows + wide),
            transcendentals=0,
        ),
        name="stack_product",
    )(choice, *arrays)


def product_kernel(places, w_at, choice_ref, a, *refs):
    groups, wide = len(places), len(w_at[0])
    outs, (w, w_sem) = refs[-2 - groups : -2], refs[-2:]
    tiles, _, columns = w.shape
    columns //= wide

    def pick(at):
        ref, index = at
        return refs[ref] if index is None else refs[ref].at[index]

    def w_copy(at, choice):
        return pltpu.make_async_copy(
            pick(w_at[choice][at]), w.at[:, :, pl.ds(at * columns, columns)], w_sem.at[at]
        )

    for at in range(wide):
        for choice in range(len(w_at)):

            @pl.when(choice_ref[0] == choice)
            def _():
                w_copy(at, choice).start()

    for at in range(wide):
        w_copy(at, 0).wait()
    right = w[...].reshape(tiles * LANES, wide * columns)
    for place, out in zip(places, outs):
        multiply(a, right, place, out)


def product(choice, groups, places, rows_stack, w_choices, after=()):
    arrays = []

    def at(block):
        array, index = block
        for known, other in enumerate(arrays):
            if other is array:
                return known, index
        arrays.append(array)
        return len(arrays) - 1, index

    w_at = [[at(block) for block in blocks] for blocks in w_choices]
    tiles, rows, _ = rows_stack.shape
    rows //= 16
    columns = w_choices[-1][0][0].shape[-1]
    wide = len(w_choices[0])
    shape = (4, rows, wide * columns)
    count = len(arrays) + len(after)
    return pl.pallas_call(
        functools.partial(product_kernel, [places[group] for group in groups], w_at),
        out_shape=[
            jax.ShapeDtypeStruct(shape, jnp.float32 if group == 0 else jnp.bfloat16)
            for group in groups
        ],
        in_specs=[
            pl.BlockSpec(memory_space=pltpu.SMEM),
            pl.BlockSpec(memory_space=pltpu.VMEM),
        ]
        + [pl.BlockSpec(memory_space=pl.ANY)] * count,
        out_specs=[pl.BlockSpec(memory_space=pltpu.VMEM)] * len(groups),
        scratch_shapes=[
            pltpu.VMEM((tiles, LANES, wide * columns), jnp.bfloat16),
            pltpu.SemaphoreType.DMA((wide,)),
        ],
        compiler_params=pltpu.CompilerParams(vmem_limit_bytes=LIMIT),
        cost_estimate=pl.CostEstimate(
            flops=8 * len(groups) * rows * tiles * LANES * wide * columns,
            bytes_accessed=2 * tiles * LANES * (4 * len(groups) * rows + wide * columns),
            transcendentals=0,
        ),
        name="product",
    )(choice, pltpu.with_memory_space_constraint(rows_stack, pltpu.VMEM), *arrays, *after)


def add_kernel(kinds, *refs):
    outs, first = refs[-4:], 0
    for kind, relative in enumerate(kinds):
        own, *others = refs[4 * kind : 4 * kind + 4]
        blocks_wide = own.shape[2] // LANES
        for piece in range(4):
            for at in range(blocks_wide):
                total = own[piece, :, pl.ds(at * LANES, LANES)]
                for step, ref in zip((1, 2, 3), others):
                    source = at ^ step if relative else at
                    total += ref[piece, :, pl.ds(source * LANES, LANES)].astype(jnp.float32)
                outs[piece][:, pl.ds((first + at) * LANES, LANES)] = total.astype(jnp.bfloat16)
        first += blocks_wide


def add(terms, kinds, after=()):
    rows = terms[0][0].shape[1]
    columns = sum(own.shape[2] for own, *_ in terms)
    arrays = [array for group in terms for array in group]
    return pl.pallas_call(
        functools.partial(add_kernel, kinds),
        out_shape=[jax.ShapeDtypeStruct((rows, columns), jnp.bfloat16)] * 4,
        in_specs=[pl.BlockSpec(memory_space=pltpu.VMEM)] * len(arrays)
        + [pl.BlockSpec(memory_space=pl.ANY)] * len(after),
        out_specs=[pl.BlockSpec(memory_space=pltpu.VMEM)] * 4,
        compiler_params=pltpu.CompilerParams(vmem_limit_bytes=LIMIT),
        cost_estimate=pl.CostEstimate(
            flops=12 * rows * columns, bytes_accessed=48 * rows * columns, transcendentals=0
        ),
        name="add",
    )(*arrays, *after)


def assemble_kernel(groups, place_ref, *refs):
    out = refs[-1]
    for ref, (fixed, parts) in zip(refs, groups):
        for at, (half, block) in enumerate(parts):
            index = fixed | (half << 3) | (block << 1)
            to = pl.multiple_of((place_ref[half] ^ index) * LANES, LANES)
            out[:, pl.ds(to, LANES)] = ref[:, pl.ds(at * LANES, LANES)]


def assemble(place, pieces):
    arrays = [piece[0] for piece in pieces]
    rows = arrays[0].shape[0]
    columns = sum(array.shape[1] for array in arrays)
    return pl.pallas_call(
        functools.partial(assemble_kernel, [piece[1:] for piece in pieces]),
        out_shape=jax.ShapeDtypeStruct((rows, columns), jnp.bfloat16),
        in_specs=[pl.BlockSpec(memory_space=pltpu.SMEM)]
        + [pl.BlockSpec(memory_space=pltpu.VMEM)] * len(arrays),
        out_specs=pl.BlockSpec(memory_space=pltpu.VMEM),
        compiler_params=pltpu.CompilerParams(vmem_limit_bytes=LIMIT),
        name="assemble",
    )(place, *arrays)


def blocks(gate_pre, up_pre, down_weight):
    n = lax.axis_size("fsdp")
    me = lax.axis_index("fsdp")
    plane = (me // PLANE) % 4
    z_low, z_high = (me // PAIR) % 2, me // (2 * PAIR)
    at_plane = plane.astype(jnp.int32).reshape(1)
    inputs = [
        pltpu.with_memory_space_constraint(array, pltpu.HBM)
        for array in (gate_pre, up_pre, down_weight)
    ]

    def send(array, perm):
        return lax.ppermute(array, "fsdp", perm=perm)

    def to_mid(array):
        return send(array, along_z(n, [(1, 2), (2, 1)]))

    def to_next(array):
        return send(array, along_z(n, [(1, 0), (3, 1), (0, 2), (2, 3)]))

    def to_core(array):
        return send(array, flip(n, CORE))

    def to_pair(array):
        return send(array, flip(n, PAIR))

    a_0, w_0, packed_1, packed_2 = pack(at_plane, (0, 1, 2), *inputs)
    pair_0, mid_0, next_0 = to_pair(a_0), to_mid(w_0), to_next(w_0)
    got_1 = send(packed_1, flip(n, PLANE))
    got_2 = send(packed_2, flip(n, 2 * PLANE))

    (packed_3,) = pack(at_plane, (3,), *inputs, after=(pair_0,))
    packed_3, got_1, got_2 = lax.optimization_barrier((packed_3, got_1, got_2))
    got_3 = send(packed_3, flip(n, 3 * PLANE))
    a_12, w_12 = unpack_pair(got_1, got_2, after=(pair_0,))
    pair_12, mid_12 = to_pair(a_12), to_mid(w_12)
    pair_0, mid_0, next_0 = lax.optimization_barrier((pair_0, mid_0, next_0))
    core_0, core_pair_0 = to_core(a_0), to_core(pair_0)

    order = jnp.array([[1, 2, 3], [1, 3, 2], [2, 3, 1], [3, 2, 1]], jnp.int32)[plane]
    got_3, core_0, core_pair_0 = lax.optimization_barrier((got_3, core_0, core_pair_0))
    a_3, w_3 = unpack(got_3)
    pair_3 = to_pair(a_3)
    a_12, pair_12, a_3 = lax.optimization_barrier((a_12, pair_12, a_3))
    a_12, pair_12, mid_12, got_3 = lax.optimization_barrier((a_12, pair_12, mid_12, got_3))
    core_12, core_pair_12 = to_core(a_12), to_core(pair_12)
    ordered_1, ordered_2 = reorder(order[:2], got_3, w_12)
    mid_3 = to_mid(w_3)
    ordered_1, ordered_2, pair_3, mid_3, mid_12 = lax.optimization_barrier(
        (ordered_1, ordered_2, pair_3, mid_3, mid_12)
    )
    next_1, next_2 = to_next(ordered_1), to_next(ordered_2)
    core_3, core_pair_3 = to_core(a_3), to_core(pair_3)

    a_0, w_0, a_12, w_12, a_3, w_3 = far([a_0, w_0, a_12, w_12, a_3, w_3])
    mid_0, mid_12, mid_3, core_12, core_pair_12 = far([mid_0, mid_12, mid_3, core_12, core_pair_12])
    a_blocks = [(block, None) for block in (a_0, pair_0, core_0, core_pair_0)]
    for block in (a_12, pair_12, core_12, core_pair_12):
        a_blocks += [(block, 0), (block, 1)]
    a_blocks += [(block, None) for block in (a_3, pair_3, core_3, core_pair_3)]
    places = [(0, 2, 1, 3), (4, 8, 6, 10), (5, 9, 7, 11), (12, 14, 13, 15)]
    w_own = [(w_0, None), (w_12, 0), (w_12, 1), (w_3, None)]
    w_mid = [(mid_0, None), (mid_12, 0), (mid_12, 1), (mid_3, None)]
    mid = (z_low ^ z_high).astype(jnp.int32).reshape(1)

    def totals_of(choice, w_choices, calls, after=()):
        totals = {}
        for groups in calls:
            outs = product(choice, groups, places, rows_stack, w_choices, after)
            totals.update(zip(groups, outs))
            after = (outs[0],)
        return [totals[group] for group in sorted(totals)]

    def across_plane(totals):
        return [send(totals[step], flip(n, step * PLANE)) for step in (1, 2, 3)]

    pieces = []

    def spread(terms, kinds, parts, after=()):
        summed = add(terms, kinds, after)
        for piece in range(4):
            mask = (piece >> 1) * PAIR + (piece & 1) * CORE
            block = send(summed[piece], flip(n, mask)) if mask else summed[piece]
            pieces.append((block, ((piece >> 1) << 4) | (piece & 1), parts))

    rows_stack, *own = stack_product(mid, places, a_blocks, [w_own, w_mid])
    own = totals_of(mid, [w_own, w_mid], ([0],), (own[0],)) + own
    own[1], got_3 = lax.optimization_barrier((own[1], got_3))
    (ordered_3,) = reorder(order[2:], got_3, w_12)
    next_3 = to_next(ordered_3)
    own_sums = across_plane(own)
    first, one, two, three = [(block, None) for block in (next_0, next_1, next_2, next_3)]
    w_low = [[first, one], [one, first], [one, two], [one, two]]
    w_high = [[two, three], [two, three], [first, three], [three, first]]
    low = totals_of(at_plane, w_low, ([3, 1, 2, 0],), (own[0],))
    low[1], low[2], low[3], *own_sums = lax.optimization_barrier((*low[1:], *own_sums))
    low_sums = across_plane(low)
    high = totals_of(at_plane, w_high, ([3, 1, 2], [0]), (low[0],))
    high[1], high[2], high[3], *low_sums = lax.optimization_barrier((*high[1:], *low_sums))
    high_sums = across_plane(high)
    spread(
        [(own[0], *own_sums), (low[0], *low_sums)],
        (True, False),
        [(0, 0), (0, 1), (0, 2), (0, 3), (1, 0), (1, 1)],
        (high[0],),
    )
    spread([(high[0], *high_sums)], (False,), [(1, 2), (1, 3)])
    across = z_low * 16 + z_high * 8 + me % 2
    place = jnp.stack([across + plane * 2, across]).astype(jnp.int32)
    return assemble(place, pieces)


def shards(gate_pre, up_pre, down_weight):
    hidden = silu_product(gate_pre, up_pre)
    terms = jnp.dot(
        hidden,
        lax.all_gather(down_weight, "fsdp", axis=1, tiled=True),
        preferred_element_type=jnp.float32,
    )
    totals = lax.psum(terms, "tp")
    share = totals.shape[1] // lax.axis_size("tp")
    result = lax.dynamic_slice_in_dim(totals, lax.axis_index("tp") * share, share, 1)
    return result.astype(jnp.bfloat16)


def solution(mesh):
    in_blocks = mesh.shape["tp"] == 1 and mesh.shape["fsdp"] == 4 * PAIR
    return jax.shard_map(
        blocks if in_blocks else shards,
        mesh=mesh,
        in_specs=(P("fsdp", "tp"), P("fsdp", "tp"), P("tp", "fsdp")),
        out_specs=P("fsdp", "tp"),
        check_vma=False,
    )
```

```python
import functools

import jax
import jax.numpy as jnp
from jax import lax
from jax.experimental import pallas as pl
from jax.experimental.pallas import tpu as pltpu
from jax.sharding import PartitionSpec as P

CORE, PLANE, PAIR = 1, 2, 8
LIMIT = 10 * 1024 * 1024
LANES = 128


def flip(n, mask):
    return [(source, source ^ mask) for source in range(n)]


def along_z(n, pairs):
    low = PAIR
    return [(a * low + rest, b * low + rest) for a, b in pairs for rest in range(low)]


def silu_product(gate, up):
    return (jax.nn.silu(gate.astype(jnp.float32)) * up.astype(jnp.float32)).astype(jnp.bfloat16)


def pack_kernel(apart, count, plane_ref, *refs):
    outs = refs[len(refs) - count - apart :]
    pairs = [(outs[0], outs[1])] if apart else []
    pairs += [(out.at[0], out.at[1]) for out in outs[2 * apart :]]
    for at, (a, w) in enumerate(pairs):
        gate, up, weight = refs[3 * at : 3 * at + 3]
        hidden = silu_product(gate[...], up[...])
        for tile in range(a.shape[0]):
            a[tile] = hidden[:, tile * LANES : (tile + 1) * LANES]
            w[tile] = weight[pl.ds(tile * LANES, LANES)]


def pack(plane, steps, gate, up, weight, after=()):
    rows, columns = gate.shape[0], weight.shape[1]
    tiles = gate.shape[1] // (4 * LANES)
    grid = 4
    share = tiles // grid
    apart = int(steps[0] == 0)
    single = pltpu.HBM((tiles, rows, LANES), jnp.bfloat16)
    double = jax.ShapeDtypeStruct((2, tiles, rows, LANES), jnp.bfloat16)
    single_spec = pl.BlockSpec((share, rows, LANES), lambda at, plane: (at, 0, 0))
    double_spec = pl.BlockSpec((2, share, rows, LANES), lambda at, plane: (0, at, 0, 0))
    others = len(steps) - apart
    in_specs = []
    for step in steps:

        def across(at, plane, step=step):
            return 0, (plane[0] ^ step) * grid + at

        def down(at, plane, step=step):
            return (plane[0] ^ step) * grid + at, 0

        wide = pl.BlockSpec((rows, share * LANES), across)
        in_specs += [wide, wide, pl.BlockSpec((share * LANES, columns), down)]
    in_specs += [pl.BlockSpec(memory_space=pl.ANY)] * len(after)
    return pl.pallas_call(
        functools.partial(pack_kernel, apart, len(steps)),
        out_shape=[single] * (2 * apart) + [double] * others,
        grid_spec=pltpu.PrefetchScalarGridSpec(
            num_scalar_prefetch=1,
            grid=(grid,),
            in_specs=in_specs,
            out_specs=[single_spec] * (2 * apart) + [double_spec] * others,
        ),
        compiler_params=pltpu.CompilerParams(vmem_limit_bytes=LIMIT),
        cost_estimate=pl.CostEstimate(
            flops=0,
            bytes_accessed=10 * rows * tiles * LANES * len(steps),
            transcendentals=rows * tiles * LANES * len(steps),
        ),
        name="pack",
    )(plane, *[gate, up, weight] * len(steps), *after)


def unpack_pair_kernel(one, two, *refs):
    a, w, held, in_sem, out_sem = refs[-5:]
    ways = [
        (source.at[kind], out.at[at])
        for at, source in enumerate((one, two))
        for kind, out in enumerate((a, w))
    ]
    into = [
        pltpu.make_async_copy(source, held.at[at], in_sem.at[at])
        for at, (source, _) in enumerate(ways)
    ]
    out_of = [
        pltpu.make_async_copy(held.at[at], to, out_sem.at[at]) for at, (_, to) in enumerate(ways)
    ]
    for copy in into:
        copy.start()
    for copy_in, copy_out in zip(into, out_of):
        copy_in.wait()
        copy_out.start()
    for copy in out_of:
        copy.wait()


def unpack_pair(one, two, after):
    return pl.pallas_call(
        unpack_pair_kernel,
        out_shape=[pltpu.HBM(one.shape, one.dtype)] * 2,
        in_specs=[pl.BlockSpec(memory_space=pl.ANY)] * (2 + len(after)),
        out_specs=[pl.BlockSpec(memory_space=pl.ANY)] * 2,
        scratch_shapes=[
            pltpu.VMEM((4,) + one.shape[1:], one.dtype),
            pltpu.SemaphoreType.DMA((4,)),
            pltpu.SemaphoreType.DMA((4,)),
        ],
        compiler_params=pltpu.CompilerParams(vmem_limit_bytes=LIMIT),
        cost_estimate=pl.CostEstimate(flops=0, bytes_accessed=8 * one.size, transcendentals=0),
        name="unpack_pair",
    )(one, two, *after)


def unpack_kernel(packed, a, w, held, in_sem, out_sem):
    into = [pltpu.make_async_copy(packed.at[at], held.at[at], in_sem.at[at]) for at in range(2)]
    out_of = [
        pltpu.make_async_copy(held.at[at], out, out_sem.at[at]) for at, out in enumerate((a, w))
    ]
    for copy in into:
        copy.start()
    for copy_in, copy_out in zip(into, out_of):
        copy_in.wait()
        copy_out.start()
    for copy in out_of:
        copy.wait()


def unpack(packed):
    return pl.pallas_call(
        unpack_kernel,
        out_shape=[pltpu.HBM(packed.shape[1:], packed.dtype)] * 2,
        in_specs=[pl.BlockSpec(memory_space=pl.ANY)],
        out_specs=[pl.BlockSpec(memory_space=pl.ANY)] * 2,
        scratch_shapes=[
            pltpu.VMEM(packed.shape, packed.dtype),
            pltpu.SemaphoreType.DMA((2,)),
            pltpu.SemaphoreType.DMA((2,)),
        ],
        compiler_params=pltpu.CompilerParams(vmem_limit_bytes=LIMIT),
        cost_estimate=pl.CostEstimate(flops=0, bytes_accessed=4 * packed.size, transcendentals=0),
        name="unpack",
    )(packed)


def reorder_kernel(count, order_ref, packed, w_12, *refs):
    out, held, in_sem, out_sem = refs
    into = [
        pltpu.make_async_copy(source, held.at[at], in_sem.at[at])
        for at, source in enumerate((packed.at[0], w_12.at[0], w_12.at[1], packed.at[1]))
    ]
    out_of = [
        pltpu.make_async_copy(
            held.at[order_ref[at]], out if count == 1 else out.at[at], out_sem.at[at]
        )
        for at in range(count)
    ]
    for copy in into:
        copy.start()
    for copy in into:
        copy.wait()
    for copy in out_of:
        copy.start()
    for copy in out_of:
        copy.wait()


def reorder(order, packed, w_12):
    shape, count = packed.shape[1:], order.shape[0]
    return pl.pallas_call(
        functools.partial(reorder_kernel, count),
        out_shape=pltpu.HBM(shape if count == 1 else (count,) + shape, packed.dtype),
        in_specs=[pl.BlockSpec(memory_space=pltpu.SMEM)]
        + [pl.BlockSpec(memory_space=pl.ANY)] * 2,
        out_specs=pl.BlockSpec(memory_space=pl.ANY),
        scratch_shapes=[
            pltpu.VMEM((4,) + shape, packed.dtype),
            pltpu.SemaphoreType.DMA((4,)),
            pltpu.SemaphoreType.DMA((count,)),
        ],
        compiler_params=pltpu.CompilerParams(vmem_limit_bytes=LIMIT),
        cost_estimate=pl.CostEstimate(flops=0, bytes_accessed=8 * packed.size, transcendentals=0),
        name="reorder",
    )(order, packed, *far([w_12]))


def far(arrays):
    return [pltpu.with_memory_space_constraint(array, pltpu.HBM) for array in arrays]


def multiply(a, right, place, out):
    tiles, rows = a.shape[0], a.shape[1] // 16
    for half in range(2):
        left = jnp.concatenate(
            [
                jnp.concatenate([a[tile, pl.ds(block * rows, rows)] for tile in range(tiles)], axis=1)
                for block in place[2 * half : 2 * half + 2]
            ],
            axis=0,
        )
        total = jnp.dot(left, right, preferred_element_type=jnp.float32)
        for at in range(2):
            out[2 * half + at] = total[at * rows : (at + 1) * rows].astype(out.dtype)


def stack_product_kernel(places, a_at, w_at, choice_ref, *refs):
    stack_ref, *outs, w, a_sem, w_sem = refs[-7:]
    tiles, _, columns = w.shape
    columns //= len(w_at[0])
    rows = stack_ref.shape[1] // 16

    def pick(at):
        ref, index = at
        return refs[ref] if index is None else refs[ref].at[index]

    def w_copy(at, choice):
        return pltpu.make_async_copy(
            pick(w_at[choice][at]), w.at[:, :, pl.ds(at * columns, columns)], w_sem.at[at]
        )

    def a_copy(at):
        return pltpu.make_async_copy(
            pick(a_at[at]), stack_ref.at[:, pl.ds(at * rows, rows)], a_sem.at[at]
        )

    for at in range(len(w_at[0])):
        for choice in range(len(w_at)):

            @pl.when(choice_ref[0] == choice)
            def _():
                w_copy(at, choice).start()

    for group in (1, 2, 3, 0):
        for at in places[group]:
            a_copy(at).start()
    for at in range(len(w_at[0])):
        w_copy(at, 0).wait()
    right = w[...].reshape(tiles * LANES, len(w_at[0]) * columns)
    for group in (1, 2, 3):
        for at in places[group]:
            a_copy(at).wait()
        multiply(stack_ref, right, places[group], outs[group - 1])
    for at in places[0]:
        a_copy(at).wait()


def stack_product(choice, places, a_blocks, w_choices):
    arrays = []

    def at(block):
        array, index = block
        for known, other in enumerate(arrays):
            if other is array:
                return known, index
        arrays.append(array)
        return len(arrays) - 1, index

    a_at = [at(block) for block in a_blocks]
    w_at = [[at(block) for block in blocks] for blocks in w_choices]
    tiles, rows, _ = a_blocks[0][0].shape
    wide = len(w_choices[0]) * w_choices[0][0][0].shape[-1]
    return pl.pallas_call(
        functools.partial(stack_product_kernel, places, a_at, w_at),
        out_shape=[pltpu.VMEM((tiles, 16 * rows, LANES), jnp.bfloat16)]
        + [jax.ShapeDtypeStruct((4, rows, wide), jnp.bfloat16)] * 3,
        in_specs=[pl.BlockSpec(memory_space=pltpu.SMEM)]
        + [pl.BlockSpec(memory_space=pl.ANY)] * len(arrays),
        out_specs=[pl.BlockSpec(memory_space=pltpu.VMEM)] * 4,
        scratch_shapes=[
            pltpu.VMEM((tiles, LANES, wide), jnp.bfloat16),
            pltpu.SemaphoreType.DMA((16,)),
            pltpu.SemaphoreType.DMA((len(w_at[0]),)),
        ],
        compiler_params=pltpu.CompilerParams(vmem_limit_bytes=LIMIT),
        cost_estimate=pl.CostEstimate(
            flops=24 * rows * tiles * LANES * wide,
            bytes_accessed=2 * tiles * LANES * (16 * rows + wide),
            transcendentals=0,
        ),
        name="stack_product",
    )(choice, *arrays)


def product_kernel(places, w_at, choice_ref, a, *refs):
    groups, wide = len(places), len(w_at[0])
    outs, (w, w_sem) = refs[-2 - groups : -2], refs[-2:]
    tiles, _, columns = w.shape
    columns //= wide

    def pick(at):
        ref, index = at
        return refs[ref] if index is None else refs[ref].at[index]

    def w_copy(at, choice):
        return pltpu.make_async_copy(
            pick(w_at[choice][at]), w.at[:, :, pl.ds(at * columns, columns)], w_sem.at[at]
        )

    for at in range(wide):
        for choice in range(len(w_at)):

            @pl.when(choice_ref[0] == choice)
            def _():
                w_copy(at, choice).start()

    for at in range(wide):
        w_copy(at, 0).wait()
    right = w[...].reshape(tiles * LANES, wide * columns)
    for place, out in zip(places, outs):
        multiply(a, right, place, out)


def product(choice, groups, places, rows_stack, w_choices, after=()):
    arrays = []

    def at(block):
        array, index = block
        for known, other in enumerate(arrays):
            if other is array:
                return known, index
        arrays.append(array)
        return len(arrays) - 1, index

    w_at = [[at(block) for block in blocks] for blocks in w_choices]
    tiles, rows, _ = rows_stack.shape
    rows //= 16
    columns = w_choices[-1][0][0].shape[-1]
    wide = len(w_choices[0])
    shape = (4, rows, wide * columns)
    count = len(arrays) + len(after)
    return pl.pallas_call(
        functools.partial(product_kernel, [places[group] for group in groups], w_at),
        out_shape=[
            jax.ShapeDtypeStruct(shape, jnp.float32 if group == 0 else jnp.bfloat16)
            for group in groups
        ],
        in_specs=[
            pl.BlockSpec(memory_space=pltpu.SMEM),
            pl.BlockSpec(memory_space=pltpu.VMEM),
        ]
        + [pl.BlockSpec(memory_space=pl.ANY)] * count,
        out_specs=[pl.BlockSpec(memory_space=pltpu.VMEM)] * len(groups),
        scratch_shapes=[
            pltpu.VMEM((tiles, LANES, wide * columns), jnp.bfloat16),
            pltpu.SemaphoreType.DMA((wide,)),
        ],
        compiler_params=pltpu.CompilerParams(vmem_limit_bytes=LIMIT),
        cost_estimate=pl.CostEstimate(
            flops=8 * len(groups) * rows * tiles * LANES * wide * columns,
            bytes_accessed=2 * tiles * LANES * (4 * len(groups) * rows + wide * columns),
            transcendentals=0,
        ),
        name="product",
    )(choice, pltpu.with_memory_space_constraint(rows_stack, pltpu.VMEM), *arrays, *after)


def add_kernel(kinds, *refs):
    outs, first = refs[-4:], 0
    for kind, relative in enumerate(kinds):
        own, *others = refs[4 * kind : 4 * kind + 4]
        blocks_wide = own.shape[2] // LANES
        for piece in range(4):
            for at in range(blocks_wide):
                total = own[piece, :, pl.ds(at * LANES, LANES)]
                for step, ref in zip((1, 2, 3), others):
                    source = at ^ step if relative else at
                    total += ref[piece, :, pl.ds(source * LANES, LANES)].astype(jnp.float32)
                outs[piece][:, pl.ds((first + at) * LANES, LANES)] = total.astype(jnp.bfloat16)
        first += blocks_wide


def add(terms, kinds, after=()):
    rows = terms[0][0].shape[1]
    columns = sum(own.shape[2] for own, *_ in terms)
    arrays = [array for group in terms for array in group]
    return pl.pallas_call(
        functools.partial(add_kernel, kinds),
        out_shape=[jax.ShapeDtypeStruct((rows, columns), jnp.bfloat16)] * 4,
        in_specs=[pl.BlockSpec(memory_space=pltpu.VMEM)] * len(arrays)
        + [pl.BlockSpec(memory_space=pl.ANY)] * len(after),
        out_specs=[pl.BlockSpec(memory_space=pltpu.VMEM)] * 4,
        compiler_params=pltpu.CompilerParams(vmem_limit_bytes=LIMIT),
        cost_estimate=pl.CostEstimate(
            flops=12 * rows * columns, bytes_accessed=48 * rows * columns, transcendentals=0
        ),
        name="add",
    )(*arrays, *after)


def assemble_kernel(groups, place_ref, *refs):
    out = refs[-1]
    for ref, (fixed, parts) in zip(refs, groups):
        for at, (half, block) in enumerate(parts):
            index = fixed | (half << 3) | (block << 1)
            to = pl.multiple_of((place_ref[half] ^ index) * LANES, LANES)
            out[:, pl.ds(to, LANES)] = ref[:, pl.ds(at * LANES, LANES)]


def assemble(place, pieces):
    arrays = [piece[0] for piece in pieces]
    rows = arrays[0].shape[0]
    columns = sum(array.shape[1] for array in arrays)
    return pl.pallas_call(
        functools.partial(assemble_kernel, [piece[1:] for piece in pieces]),
        out_shape=jax.ShapeDtypeStruct((rows, columns), jnp.bfloat16),
        in_specs=[pl.BlockSpec(memory_space=pltpu.SMEM)]
        + [pl.BlockSpec(memory_space=pltpu.VMEM)] * len(arrays),
        out_specs=pl.BlockSpec(memory_space=pltpu.VMEM),
        compiler_params=pltpu.CompilerParams(vmem_limit_bytes=LIMIT),
        name="assemble",
    )(place, *arrays)


def blocks(gate_pre, up_pre, down_weight):
    n = lax.axis_size("fsdp")
    me = lax.axis_index("fsdp")
    plane = (me // PLANE) % 4
    z_low, z_high = (me // PAIR) % 2, me // (2 * PAIR)
    at_plane = plane.astype(jnp.int32).reshape(1)
    inputs = [
        pltpu.with_memory_space_constraint(array, pltpu.HBM)
        for array in (gate_pre, up_pre, down_weight)
    ]

    def send(array, perm):
        return lax.ppermute(array, "fsdp", perm=perm)

    def to_mid(array):
        return send(array, along_z(n, [(1, 2), (2, 1)]))

    def to_next(array):
        return send(array, along_z(n, [(1, 0), (3, 1), (0, 2), (2, 3)]))

    def to_core(array):
        return send(array, flip(n, CORE))

    def to_pair(array):
        return send(array, flip(n, PAIR))

    a_0, w_0, packed_1, packed_2 = pack(at_plane, (0, 1, 2), *inputs)
    pair_0, mid_0, next_0 = to_pair(a_0), to_mid(w_0), to_next(w_0)
    got_1 = send(packed_1, flip(n, PLANE))
    got_2 = send(packed_2, flip(n, 2 * PLANE))

    (packed_3,) = pack(at_plane, (3,), *inputs, after=(pair_0,))
    packed_3, got_1, got_2 = lax.optimization_barrier((packed_3, got_1, got_2))
    got_3 = send(packed_3, flip(n, 3 * PLANE))
    a_12, w_12 = unpack_pair(got_1, got_2, after=(pair_0,))
    pair_12, mid_12 = to_pair(a_12), to_mid(w_12)
    pair_0, mid_0, next_0 = lax.optimization_barrier((pair_0, mid_0, next_0))
    core_0, core_pair_0 = to_core(a_0), to_core(pair_0)

    order = jnp.array([[1, 2, 3], [1, 3, 2], [2, 3, 1], [3, 2, 1]], jnp.int32)[plane]
    got_3, core_0, core_pair_0 = lax.optimization_barrier((got_3, core_0, core_pair_0))
    a_3, w_3 = unpack(got_3)
    pair_3 = to_pair(a_3)
    a_12, pair_12, a_3 = lax.optimization_barrier((a_12, pair_12, a_3))
    a_12, pair_12, mid_12, got_3 = lax.optimization_barrier((a_12, pair_12, mid_12, got_3))
    core_12, core_pair_12 = to_core(a_12), to_core(pair_12)
    ordered_12 = reorder(order[:2], got_3, w_12)
    mid_3 = to_mid(w_3)
    ordered_12, pair_3, mid_3, mid_12 = lax.optimization_barrier(
        (ordered_12, pair_3, mid_3, mid_12)
    )
    next_12 = to_next(ordered_12)
    core_3, core_pair_3 = to_core(a_3), to_core(pair_3)

    a_0, w_0, a_12, w_12, a_3, w_3 = far([a_0, w_0, a_12, w_12, a_3, w_3])
    mid_0, mid_12, mid_3, core_12, core_pair_12 = far([mid_0, mid_12, mid_3, core_12, core_pair_12])
    a_blocks = [(block, None) for block in (a_0, pair_0, core_0, core_pair_0)]
    for block in (a_12, pair_12, core_12, core_pair_12):
        a_blocks += [(block, 0), (block, 1)]
    a_blocks += [(block, None) for block in (a_3, pair_3, core_3, core_pair_3)]
    places = [(0, 2, 1, 3), (4, 8, 6, 10), (5, 9, 7, 11), (12, 14, 13, 15)]
    w_own = [(w_0, None), (w_12, 0), (w_12, 1), (w_3, None)]
    w_mid = [(mid_0, None), (mid_12, 0), (mid_12, 1), (mid_3, None)]
    mid = (z_low ^ z_high).astype(jnp.int32).reshape(1)

    def totals_of(choice, w_choices, calls, after=()):
        totals = {}
        for groups in calls:
            outs = product(choice, groups, places, rows_stack, w_choices, after)
            totals.update(zip(groups, outs))
            after = (outs[0],)
        return [totals[group] for group in sorted(totals)]

    def across_plane(totals):
        return [send(totals[step], flip(n, step * PLANE)) for step in (1, 2, 3)]

    pieces = []

    def spread(terms, kinds, parts, after=()):
        summed = add(terms, kinds, after)
        for piece in range(4):
            mask = (piece >> 1) * PAIR + (piece & 1) * CORE
            block = send(summed[piece], flip(n, mask)) if mask else summed[piece]
            pieces.append((block, ((piece >> 1) << 4) | (piece & 1), parts))

    rows_stack, *own = stack_product(mid, places, a_blocks, [w_own, w_mid])
    own = totals_of(mid, [w_own, w_mid], ([0],), (own[0],)) + own
    own[1], got_3 = lax.optimization_barrier((own[1], got_3))
    ordered_3 = reorder(order[2:], got_3, w_12)
    next_3 = to_next(ordered_3)
    own_sums = across_plane(own)
    first, one, two, three = (next_0, None), (next_12, 0), (next_12, 1), (next_3, None)
    w_low = [[first, one], [one, first], [one, two], [one, two]]
    w_high = [[two, three], [two, three], [first, three], [three, first]]
    low = totals_of(at_plane, w_low, ([3, 1, 2, 0],), (own[0],))
    low[1], low[2], low[3], *own_sums = lax.optimization_barrier((*low[1:], *own_sums))
    low_sums = across_plane(low)
    high = totals_of(at_plane, w_high, ([3, 1, 2], [0]), (low[0],))
    high[1], high[2], high[3], *low_sums = lax.optimization_barrier((*high[1:], *low_sums))
    high_sums = across_plane(high)
    spread(
        [(own[0], *own_sums), (low[0], *low_sums)],
        (True, False),
        [(0, 0), (0, 1), (0, 2), (0, 3), (1, 0), (1, 1)],
        (high[0],),
    )
    spread([(high[0], *high_sums)], (False,), [(1, 2), (1, 3)])
    across = z_low * 16 + z_high * 8 + me % 2
    place = jnp.stack([across + plane * 2, across]).astype(jnp.int32)
    return assemble(place, pieces)


def shards(gate_pre, up_pre, down_weight):
    hidden = silu_product(gate_pre, up_pre)
    terms = jnp.dot(
        hidden,
        lax.all_gather(down_weight, "fsdp", axis=1, tiled=True),
        preferred_element_type=jnp.float32,
    )
    totals = lax.psum(terms, "tp")
    share = totals.shape[1] // lax.axis_size("tp")
    result = lax.dynamic_slice_in_dim(totals, lax.axis_index("tp") * share, share, 1)
    return result.astype(jnp.bfloat16)


def solution(mesh):
    in_blocks = mesh.shape["tp"] == 1 and mesh.shape["fsdp"] == 4 * PAIR
    return jax.shard_map(
        blocks if in_blocks else shards,
        mesh=mesh,
        in_specs=(P("fsdp", "tp"), P("fsdp", "tp"), P("tp", "fsdp")),
        out_specs=P("fsdp", "tp"),
        check_vma=False,
    )
```

```python
import functools

import jax
import jax.numpy as jnp
from jax import lax
from jax.experimental import pallas as pl
from jax.experimental.pallas import tpu as pltpu
from jax.sharding import PartitionSpec as P

CORE, PLANE, PAIR = 1, 2, 8
LIMIT = 10 * 1024 * 1024
LANES = 128


def flip(n, mask):
    return [(source, source ^ mask) for source in range(n)]


def along_z(n, pairs):
    low = PAIR
    return [(a * low + rest, b * low + rest) for a, b in pairs for rest in range(low)]


def silu_product(gate, up):
    return (jax.nn.silu(gate.astype(jnp.float32)) * up.astype(jnp.float32)).astype(jnp.bfloat16)


def pack_kernel(apart, count, plane_ref, *refs):
    outs = refs[len(refs) - count - apart :]
    pairs = [(outs[0], outs[1])] if apart else []
    pairs += [(out.at[0], out.at[1]) for out in outs[2 * apart :]]
    for at, (a, w) in enumerate(pairs):
        gate, up, weight = refs[3 * at : 3 * at + 3]
        hidden = silu_product(gate[...], up[...])
        for tile in range(a.shape[0]):
            a[tile] = hidden[:, tile * LANES : (tile + 1) * LANES]
            w[tile] = weight[pl.ds(tile * LANES, LANES)]


def pack(plane, steps, gate, up, weight, after=()):
    rows, columns = gate.shape[0], weight.shape[1]
    tiles = gate.shape[1] // (4 * LANES)
    grid = 4
    share = tiles // grid
    apart = int(steps[0] == 0)
    single = pltpu.HBM((tiles, rows, LANES), jnp.bfloat16)
    double = jax.ShapeDtypeStruct((2, tiles, rows, LANES), jnp.bfloat16)
    single_spec = pl.BlockSpec((share, rows, LANES), lambda at, plane: (at, 0, 0))
    double_spec = pl.BlockSpec((2, share, rows, LANES), lambda at, plane: (0, at, 0, 0))
    others = len(steps) - apart
    in_specs = []
    for step in steps:

        def across(at, plane, step=step):
            return 0, (plane[0] ^ step) * grid + at

        def down(at, plane, step=step):
            return (plane[0] ^ step) * grid + at, 0

        wide = pl.BlockSpec((rows, share * LANES), across)
        in_specs += [wide, wide, pl.BlockSpec((share * LANES, columns), down)]
    in_specs += [pl.BlockSpec(memory_space=pl.ANY)] * len(after)
    return pl.pallas_call(
        functools.partial(pack_kernel, apart, len(steps)),
        out_shape=[single] * (2 * apart) + [double] * others,
        grid_spec=pltpu.PrefetchScalarGridSpec(
            num_scalar_prefetch=1,
            grid=(grid,),
            in_specs=in_specs,
            out_specs=[single_spec] * (2 * apart) + [double_spec] * others,
        ),
        compiler_params=pltpu.CompilerParams(vmem_limit_bytes=LIMIT),
        cost_estimate=pl.CostEstimate(
            flops=0,
            bytes_accessed=10 * rows * tiles * LANES * len(steps),
            transcendentals=rows * tiles * LANES * len(steps),
        ),
        name="pack",
    )(plane, *[gate, up, weight] * len(steps), *after)


def unpack_pair_kernel(one, two, *refs):
    a, w, held, in_sem, out_sem = refs[-5:]
    ways = [
        (source.at[kind], out.at[at])
        for at, source in enumerate((one, two))
        for kind, out in enumerate((a, w))
    ]
    into = [
        pltpu.make_async_copy(source, held.at[at], in_sem.at[at])
        for at, (source, _) in enumerate(ways)
    ]
    out_of = [
        pltpu.make_async_copy(held.at[at], to, out_sem.at[at]) for at, (_, to) in enumerate(ways)
    ]
    for copy in into:
        copy.start()
    for copy_in, copy_out in zip(into, out_of):
        copy_in.wait()
        copy_out.start()
    for copy in out_of:
        copy.wait()


def unpack_pair(one, two, after):
    return pl.pallas_call(
        unpack_pair_kernel,
        out_shape=[pltpu.HBM(one.shape, one.dtype)] * 2,
        in_specs=[pl.BlockSpec(memory_space=pl.ANY)] * (2 + len(after)),
        out_specs=[pl.BlockSpec(memory_space=pl.ANY)] * 2,
        scratch_shapes=[
            pltpu.VMEM((4,) + one.shape[1:], one.dtype),
            pltpu.SemaphoreType.DMA((4,)),
            pltpu.SemaphoreType.DMA((4,)),
        ],
        compiler_params=pltpu.CompilerParams(vmem_limit_bytes=LIMIT),
        cost_estimate=pl.CostEstimate(flops=0, bytes_accessed=8 * one.size, transcendentals=0),
        name="unpack_pair",
    )(one, two, *after)


def unpack_kernel(packed, a, w, held, in_sem, out_sem):
    into = [pltpu.make_async_copy(packed.at[at], held.at[at], in_sem.at[at]) for at in range(2)]
    out_of = [
        pltpu.make_async_copy(held.at[at], out, out_sem.at[at]) for at, out in enumerate((a, w))
    ]
    for copy in into:
        copy.start()
    for copy_in, copy_out in zip(into, out_of):
        copy_in.wait()
        copy_out.start()
    for copy in out_of:
        copy.wait()


def unpack(packed):
    return pl.pallas_call(
        unpack_kernel,
        out_shape=[pltpu.HBM(packed.shape[1:], packed.dtype)] * 2,
        in_specs=[pl.BlockSpec(memory_space=pl.ANY)],
        out_specs=[pl.BlockSpec(memory_space=pl.ANY)] * 2,
        scratch_shapes=[
            pltpu.VMEM(packed.shape, packed.dtype),
            pltpu.SemaphoreType.DMA((2,)),
            pltpu.SemaphoreType.DMA((2,)),
        ],
        compiler_params=pltpu.CompilerParams(vmem_limit_bytes=LIMIT),
        cost_estimate=pl.CostEstimate(flops=0, bytes_accessed=4 * packed.size, transcendentals=0),
        name="unpack",
    )(packed)


def reorder_kernel(count, order_ref, packed, w_12, *refs):
    out, held, in_sem, out_sem = refs
    into = [
        pltpu.make_async_copy(source, held.at[at], in_sem.at[at])
        for at, source in enumerate((packed.at[0], w_12.at[0], w_12.at[1], packed.at[1]))
    ]
    out_of = [
        pltpu.make_async_copy(
            held.at[order_ref[at]], out if count == 1 else out.at[at], out_sem.at[at]
        )
        for at in range(count)
    ]
    for copy in into:
        copy.start()
    for copy in into:
        copy.wait()
    for copy in out_of:
        copy.start()
    for copy in out_of:
        copy.wait()


def reorder(order, packed, w_12):
    shape, count = packed.shape[1:], order.shape[0]
    return pl.pallas_call(
        functools.partial(reorder_kernel, count),
        out_shape=pltpu.HBM(shape if count == 1 else (count,) + shape, packed.dtype),
        in_specs=[pl.BlockSpec(memory_space=pltpu.SMEM)]
        + [pl.BlockSpec(memory_space=pl.ANY)] * 2,
        out_specs=pl.BlockSpec(memory_space=pl.ANY),
        scratch_shapes=[
            pltpu.VMEM((4,) + shape, packed.dtype),
            pltpu.SemaphoreType.DMA((4,)),
            pltpu.SemaphoreType.DMA((count,)),
        ],
        compiler_params=pltpu.CompilerParams(vmem_limit_bytes=LIMIT),
        cost_estimate=pl.CostEstimate(flops=0, bytes_accessed=8 * packed.size, transcendentals=0),
        name="reorder",
    )(order, packed, *far([w_12]))


def far(arrays):
    return [pltpu.with_memory_space_constraint(array, pltpu.HBM) for array in arrays]


def multiply(a, right, place, out):
    tiles, rows = a.shape[0], a.shape[1] // 16
    for half in range(2):
        left = jnp.concatenate(
            [
                jnp.concatenate([a[tile, pl.ds(block * rows, rows)] for tile in range(tiles)], axis=1)
                for block in place[2 * half : 2 * half + 2]
            ],
            axis=0,
        )
        total = jnp.dot(left, right, preferred_element_type=jnp.float32)
        for at in range(2):
            out[2 * half + at] = total[at * rows : (at + 1) * rows].astype(out.dtype)


def stack_product_kernel(places, a_at, w_at, choice_ref, *refs):
    stack_ref, *outs, w, a_sem, w_sem = refs[-7:]
    tiles, _, columns = w.shape
    columns //= len(w_at[0])
    rows = stack_ref.shape[1] // 16

    def pick(at):
        ref, index = at
        return refs[ref] if index is None else refs[ref].at[index]

    def w_copy(at, choice):
        return pltpu.make_async_copy(
            pick(w_at[choice][at]), w.at[:, :, pl.ds(at * columns, columns)], w_sem.at[at]
        )

    def a_copy(at):
        return pltpu.make_async_copy(
            pick(a_at[at]), stack_ref.at[:, pl.ds(at * rows, rows)], a_sem.at[at]
        )

    for at in range(len(w_at[0])):
        for choice in range(len(w_at)):

            @pl.when(choice_ref[0] == choice)
            def _():
                w_copy(at, choice).start()

    for group in (1, 2, 3, 0):
        for at in places[group]:
            a_copy(at).start()
    for at in range(len(w_at[0])):
        w_copy(at, 0).wait()
    right = w[...].reshape(tiles * LANES, len(w_at[0]) * columns)
    for group in (1, 2, 3):
        for at in places[group]:
            a_copy(at).wait()
        multiply(stack_ref, right, places[group], outs[group - 1])
    for at in places[0]:
        a_copy(at).wait()


def stack_product(choice, places, a_blocks, w_choices):
    arrays = []

    def at(block):
        array, index = block
        for known, other in enumerate(arrays):
            if other is array:
                return known, index
        arrays.append(array)
        return len(arrays) - 1, index

    a_at = [at(block) for block in a_blocks]
    w_at = [[at(block) for block in blocks] for blocks in w_choices]
    tiles, rows, _ = a_blocks[0][0].shape
    wide = len(w_choices[0]) * w_choices[0][0][0].shape[-1]
    return pl.pallas_call(
        functools.partial(stack_product_kernel, places, a_at, w_at),
        out_shape=[pltpu.VMEM((tiles, 16 * rows, LANES), jnp.bfloat16)]
        + [jax.ShapeDtypeStruct((4, rows, wide), jnp.bfloat16)] * 3,
        in_specs=[pl.BlockSpec(memory_space=pltpu.SMEM)]
        + [pl.BlockSpec(memory_space=pl.ANY)] * len(arrays),
        out_specs=[pl.BlockSpec(memory_space=pltpu.VMEM)] * 4,
        scratch_shapes=[
            pltpu.VMEM((tiles, LANES, wide), jnp.bfloat16),
            pltpu.SemaphoreType.DMA((16,)),
            pltpu.SemaphoreType.DMA((len(w_at[0]),)),
        ],
        compiler_params=pltpu.CompilerParams(vmem_limit_bytes=LIMIT),
        cost_estimate=pl.CostEstimate(
            flops=24 * rows * tiles * LANES * wide,
            bytes_accessed=2 * tiles * LANES * (16 * rows + wide),
            transcendentals=0,
        ),
        name="stack_product",
    )(choice, *arrays)


def product_kernel(places, w_at, choice_ref, a, *refs):
    groups, wide = len(places), len(w_at[0])
    outs, (w, w_sem) = refs[-2 - groups : -2], refs[-2:]
    tiles, _, columns = w.shape
    columns //= wide

    def pick(at):
        ref, index = at
        return refs[ref] if index is None else refs[ref].at[index]

    def w_copy(at, choice):
        return pltpu.make_async_copy(
            pick(w_at[choice][at]), w.at[:, :, pl.ds(at * columns, columns)], w_sem.at[at]
        )

    for at in range(wide):
        for choice in range(len(w_at)):

            @pl.when(choice_ref[0] == choice)
            def _():
                w_copy(at, choice).start()

    for at in range(wide):
        w_copy(at, 0).wait()
    right = w[...].reshape(tiles * LANES, wide * columns)
    for place, out in zip(places, outs):
        multiply(a, right, place, out)


def product(choice, groups, places, rows_stack, w_choices, after=()):
    arrays = []

    def at(block):
        array, index = block
        for known, other in enumerate(arrays):
            if other is array:
                return known, index
        arrays.append(array)
        return len(arrays) - 1, index

    w_at = [[at(block) for block in blocks] for blocks in w_choices]
    tiles, rows, _ = rows_stack.shape
    rows //= 16
    columns = w_choices[-1][0][0].shape[-1]
    wide = len(w_choices[0])
    shape = (4, rows, wide * columns)
    count = len(arrays) + len(after)
    return pl.pallas_call(
        functools.partial(product_kernel, [places[group] for group in groups], w_at),
        out_shape=[
            jax.ShapeDtypeStruct(shape, jnp.float32 if group == 0 else jnp.bfloat16)
            for group in groups
        ],
        in_specs=[
            pl.BlockSpec(memory_space=pltpu.SMEM),
            pl.BlockSpec(memory_space=pltpu.VMEM),
        ]
        + [pl.BlockSpec(memory_space=pl.ANY)] * count,
        out_specs=[pl.BlockSpec(memory_space=pltpu.VMEM)] * len(groups),
        scratch_shapes=[
            pltpu.VMEM((tiles, LANES, wide * columns), jnp.bfloat16),
            pltpu.SemaphoreType.DMA((wide,)),
        ],
        compiler_params=pltpu.CompilerParams(vmem_limit_bytes=LIMIT),
        cost_estimate=pl.CostEstimate(
            flops=8 * len(groups) * rows * tiles * LANES * wide * columns,
            bytes_accessed=2 * tiles * LANES * (4 * len(groups) * rows + wide * columns),
            transcendentals=0,
        ),
        name="product",
    )(choice, pltpu.with_memory_space_constraint(rows_stack, pltpu.VMEM), *arrays, *after)


def add_kernel(kinds, *refs):
    outs, first = refs[-4:], 0
    for kind, relative in enumerate(kinds):
        own, *others = refs[4 * kind : 4 * kind + 4]
        blocks_wide = own.shape[2] // LANES
        for piece in range(4):
            for at in range(blocks_wide):
                total = own[piece, :, pl.ds(at * LANES, LANES)]
                for step, ref in zip((1, 2, 3), others):
                    source = at ^ step if relative else at
                    total += ref[piece, :, pl.ds(source * LANES, LANES)].astype(jnp.float32)
                outs[piece][:, pl.ds((first + at) * LANES, LANES)] = total.astype(jnp.bfloat16)
        first += blocks_wide


def add(terms, kinds, after=()):
    rows = terms[0][0].shape[1]
    columns = sum(own.shape[2] for own, *_ in terms)
    arrays = [array for group in terms for array in group]
    return pl.pallas_call(
        functools.partial(add_kernel, kinds),
        out_shape=[jax.ShapeDtypeStruct((rows, columns), jnp.bfloat16)] * 4,
        in_specs=[pl.BlockSpec(memory_space=pltpu.VMEM)] * len(arrays)
        + [pl.BlockSpec(memory_space=pl.ANY)] * len(after),
        out_specs=[pl.BlockSpec(memory_space=pltpu.VMEM)] * 4,
        compiler_params=pltpu.CompilerParams(vmem_limit_bytes=LIMIT),
        cost_estimate=pl.CostEstimate(
            flops=12 * rows * columns, bytes_accessed=48 * rows * columns, transcendentals=0
        ),
        name="add",
    )(*arrays, *after)


def assemble_kernel(groups, place_ref, *refs):
    out = refs[-1]
    for ref, (fixed, parts) in zip(refs, groups):
        for at, (half, block) in enumerate(parts):
            index = fixed | (half << 3) | (block << 1)
            to = pl.multiple_of((place_ref[half] ^ index) * LANES, LANES)
            out[:, pl.ds(to, LANES)] = ref[:, pl.ds(at * LANES, LANES)]


def assemble(place, pieces):
    arrays = [piece[0] for piece in pieces]
    rows = arrays[0].shape[0]
    columns = sum(array.shape[1] for array in arrays)
    return pl.pallas_call(
        functools.partial(assemble_kernel, [piece[1:] for piece in pieces]),
        out_shape=jax.ShapeDtypeStruct((rows, columns), jnp.bfloat16),
        in_specs=[pl.BlockSpec(memory_space=pltpu.SMEM)]
        + [pl.BlockSpec(memory_space=pltpu.VMEM)] * len(arrays),
        out_specs=pl.BlockSpec(memory_space=pltpu.VMEM),
        compiler_params=pltpu.CompilerParams(vmem_limit_bytes=LIMIT),
        name="assemble",
    )(place, *arrays)


def blocks(gate_pre, up_pre, down_weight):
    n = lax.axis_size("fsdp")
    me = lax.axis_index("fsdp")
    plane = (me // PLANE) % 4
    z_low, z_high = (me // PAIR) % 2, me // (2 * PAIR)
    at_plane = plane.astype(jnp.int32).reshape(1)
    inputs = [
        pltpu.with_memory_space_constraint(array, pltpu.HBM)
        for array in (gate_pre, up_pre, down_weight)
    ]

    def send(array, perm):
        return lax.ppermute(array, "fsdp", perm=perm)

    def to_mid(array):
        return send(array, along_z(n, [(1, 2), (2, 1)]))

    def to_next(array):
        return send(array, along_z(n, [(1, 0), (3, 1), (0, 2), (2, 3)]))

    def to_core(array):
        return send(array, flip(n, CORE))

    def to_pair(array):
        return send(array, flip(n, PAIR))

    packed_1, packed_2 = pack(at_plane, (1, 2), *inputs)
    a_0, w_0 = pack(at_plane, (0,), *inputs, after=(packed_1,))
    pair_0, mid_0, next_0 = to_pair(a_0), to_mid(w_0), to_next(w_0)
    got_1 = send(packed_1, flip(n, PLANE))
    got_2 = send(packed_2, flip(n, 2 * PLANE))

    (packed_3,) = pack(at_plane, (3,), *inputs, after=(pair_0,))
    packed_3, got_1, got_2 = lax.optimization_barrier((packed_3, got_1, got_2))
    got_3 = send(packed_3, flip(n, 3 * PLANE))
    a_12, w_12 = unpack_pair(got_1, got_2, after=(pair_0,))
    pair_12, mid_12 = to_pair(a_12), to_mid(w_12)
    pair_0, mid_0, next_0 = lax.optimization_barrier((pair_0, mid_0, next_0))
    core_0, core_pair_0 = to_core(a_0), to_core(pair_0)

    order = jnp.array([[1, 2, 3], [1, 3, 2], [2, 3, 1], [3, 2, 1]], jnp.int32)[plane]
    got_3, core_0, core_pair_0 = lax.optimization_barrier((got_3, core_0, core_pair_0))
    a_3, w_3 = unpack(got_3)
    pair_3 = to_pair(a_3)
    a_12, pair_12, a_3 = lax.optimization_barrier((a_12, pair_12, a_3))
    a_12, pair_12, mid_12, got_3 = lax.optimization_barrier((a_12, pair_12, mid_12, got_3))
    core_12, core_pair_12 = to_core(a_12), to_core(pair_12)
    ordered_12 = reorder(order[:2], got_3, w_12)
    mid_3 = to_mid(w_3)
    ordered_12, pair_3, mid_3, mid_12 = lax.optimization_barrier(
        (ordered_12, pair_3, mid_3, mid_12)
    )
    next_12 = to_next(ordered_12)
    core_3, core_pair_3 = to_core(a_3), to_core(pair_3)

    a_0, w_0, a_12, w_12, a_3, w_3 = far([a_0, w_0, a_12, w_12, a_3, w_3])
    mid_0, mid_12, mid_3, core_12, core_pair_12 = far([mid_0, mid_12, mid_3, core_12, core_pair_12])
    a_blocks = [(block, None) for block in (a_0, pair_0, core_0, core_pair_0)]
    for block in (a_12, pair_12, core_12, core_pair_12):
        a_blocks += [(block, 0), (block, 1)]
    a_blocks += [(block, None) for block in (a_3, pair_3, core_3, core_pair_3)]
    places = [(0, 2, 1, 3), (4, 8, 6, 10), (5, 9, 7, 11), (12, 14, 13, 15)]
    w_own = [(w_0, None), (w_12, 0), (w_12, 1), (w_3, None)]
    w_mid = [(mid_0, None), (mid_12, 0), (mid_12, 1), (mid_3, None)]
    mid = (z_low ^ z_high).astype(jnp.int32).reshape(1)

    def totals_of(choice, w_choices, calls, after=()):
        totals = {}
        for groups in calls:
            outs = product(choice, groups, places, rows_stack, w_choices, after)
            totals.update(zip(groups, outs))
            after = (outs[0],)
        return [totals[group] for group in sorted(totals)]

    def across_plane(totals):
        return [send(totals[step], flip(n, step * PLANE)) for step in (1, 2, 3)]

    pieces = []

    def spread(terms, kinds, parts, after=()):
        summed = add(terms, kinds, after)
        for piece in range(4):
            mask = (piece >> 1) * PAIR + (piece & 1) * CORE
            block = send(summed[piece], flip(n, mask)) if mask else summed[piece]
            pieces.append((block, ((piece >> 1) << 4) | (piece & 1), parts))

    rows_stack, *own = stack_product(mid, places, a_blocks, [w_own, w_mid])
    own = totals_of(mid, [w_own, w_mid], ([0],), (own[0],)) + own
    own[1], got_3 = lax.optimization_barrier((own[1], got_3))
    ordered_3 = reorder(order[2:], got_3, w_12)
    next_3 = to_next(ordered_3)
    own_sums = across_plane(own)
    first, one, two, three = (next_0, None), (next_12, 0), (next_12, 1), (next_3, None)
    w_low = [[first, one], [one, first], [one, two], [one, two]]
    w_high = [[two, three], [two, three], [first, three], [three, first]]
    low = totals_of(at_plane, w_low, ([3, 1, 2, 0],), (own[0],))
    low[1], low[2], low[3], *own_sums = lax.optimization_barrier((*low[1:], *own_sums))
    low_sums = across_plane(low)
    high = totals_of(at_plane, w_high, ([3, 1, 2], [0]), (low[0],))
    high[1], high[2], high[3], *low_sums = lax.optimization_barrier((*high[1:], *low_sums))
    high_sums = across_plane(high)
    spread(
        [(own[0], *own_sums), (low[0], *low_sums)],
        (True, False),
        [(0, 0), (0, 1), (0, 2), (0, 3), (1, 0), (1, 1)],
        (high[0],),
    )
    spread([(high[0], *high_sums)], (False,), [(1, 2), (1, 3)])
    across = z_low * 16 + z_high * 8 + me % 2
    place = jnp.stack([across + plane * 2, across]).astype(jnp.int32)
    return assemble(place, pieces)


def shards(gate_pre, up_pre, down_weight):
    hidden = silu_product(gate_pre, up_pre)
    terms = jnp.dot(
        hidden,
        lax.all_gather(down_weight, "fsdp", axis=1, tiled=True),
        preferred_element_type=jnp.float32,
    )
    totals = lax.psum(terms, "tp")
    share = totals.shape[1] // lax.axis_size("tp")
    result = lax.dynamic_slice_in_dim(totals, lax.axis_index("tp") * share, share, 1)
    return result.astype(jnp.bfloat16)


def solution(mesh):
    in_blocks = mesh.shape["tp"] == 1 and mesh.shape["fsdp"] == 4 * PAIR
    return jax.shard_map(
        blocks if in_blocks else shards,
        mesh=mesh,
        in_specs=(P("fsdp", "tp"), P("fsdp", "tp"), P("tp", "fsdp")),
        out_specs=P("fsdp", "tp"),
        check_vma=False,
    )
```

```python
import functools

import jax
import jax.numpy as jnp
from jax import lax
from jax.experimental import pallas as pl
from jax.experimental.pallas import tpu as pltpu
from jax.sharding import PartitionSpec as P

CORE, PLANE, PAIR = 1, 2, 8
LIMIT = 10 * 1024 * 1024
LANES = 128


def flip(n, mask):
    return [(source, source ^ mask) for source in range(n)]


def along_z(n, pairs):
    low = PAIR
    return [(a * low + rest, b * low + rest) for a, b in pairs for rest in range(low)]


def silu_product(gate, up):
    return (jax.nn.silu(gate.astype(jnp.float32)) * up.astype(jnp.float32)).astype(jnp.bfloat16)


def pack_kernel(apart, count, plane_ref, *refs):
    outs = refs[len(refs) - count - apart :]
    pairs = [(outs[0], outs[1])] if apart else []
    pairs += [(out.at[0], out.at[1]) for out in outs[2 * apart :]]
    for at, (a, w) in enumerate(pairs):
        gate, up, weight = refs[3 * at : 3 * at + 3]
        hidden = silu_product(gate[...], up[...])
        for tile in range(a.shape[0]):
            a[tile] = hidden[:, tile * LANES : (tile + 1) * LANES]
            w[tile] = weight[pl.ds(tile * LANES, LANES)]


def pack(plane, steps, gate, up, weight, after=()):
    rows, columns = gate.shape[0], weight.shape[1]
    tiles = gate.shape[1] // (4 * LANES)
    grid = 4
    share = tiles // grid
    apart = int(steps[0] == 0)
    single = pltpu.HBM((tiles, rows, LANES), jnp.bfloat16)
    double = jax.ShapeDtypeStruct((2, tiles, rows, LANES), jnp.bfloat16)
    single_spec = pl.BlockSpec((share, rows, LANES), lambda at, plane: (at, 0, 0))
    double_spec = pl.BlockSpec((2, share, rows, LANES), lambda at, plane: (0, at, 0, 0))
    others = len(steps) - apart
    in_specs = []
    for step in steps:

        def across(at, plane, step=step):
            return 0, (plane[0] ^ step) * grid + at

        def down(at, plane, step=step):
            return (plane[0] ^ step) * grid + at, 0

        wide = pl.BlockSpec((rows, share * LANES), across)
        in_specs += [wide, wide, pl.BlockSpec((share * LANES, columns), down)]
    in_specs += [pl.BlockSpec(memory_space=pl.ANY)] * len(after)
    return pl.pallas_call(
        functools.partial(pack_kernel, apart, len(steps)),
        out_shape=[single] * (2 * apart) + [double] * others,
        grid_spec=pltpu.PrefetchScalarGridSpec(
            num_scalar_prefetch=1,
            grid=(grid,),
            in_specs=in_specs,
            out_specs=[single_spec] * (2 * apart) + [double_spec] * others,
        ),
        compiler_params=pltpu.CompilerParams(vmem_limit_bytes=LIMIT),
        cost_estimate=pl.CostEstimate(
            flops=0,
            bytes_accessed=10 * rows * tiles * LANES * len(steps),
            transcendentals=rows * tiles * LANES * len(steps),
        ),
        name="pack",
    )(plane, *[gate, up, weight] * len(steps), *after)


def unpack_pair_kernel(one, two, *refs):
    a, w, held, in_sem, out_sem = refs[-5:]
    ways = [
        (source.at[kind], out.at[at])
        for at, source in enumerate((one, two))
        for kind, out in enumerate((a, w))
    ]
    into = [
        pltpu.make_async_copy(source, held.at[at], in_sem.at[at])
        for at, (source, _) in enumerate(ways)
    ]
    out_of = [
        pltpu.make_async_copy(held.at[at], to, out_sem.at[at]) for at, (_, to) in enumerate(ways)
    ]
    for copy in into:
        copy.start()
    for copy_in, copy_out in zip(into, out_of):
        copy_in.wait()
        copy_out.start()
    for copy in out_of:
        copy.wait()


def unpack_pair(one, two, after):
    return pl.pallas_call(
        unpack_pair_kernel,
        out_shape=[pltpu.HBM(one.shape, one.dtype)] * 2,
        in_specs=[pl.BlockSpec(memory_space=pl.ANY)] * (2 + len(after)),
        out_specs=[pl.BlockSpec(memory_space=pl.ANY)] * 2,
        scratch_shapes=[
            pltpu.VMEM((4,) + one.shape[1:], one.dtype),
            pltpu.SemaphoreType.DMA((4,)),
            pltpu.SemaphoreType.DMA((4,)),
        ],
        compiler_params=pltpu.CompilerParams(vmem_limit_bytes=LIMIT),
        cost_estimate=pl.CostEstimate(flops=0, bytes_accessed=8 * one.size, transcendentals=0),
        name="unpack_pair",
    )(one, two, *after)


def unpack_kernel(packed, a, w, held, in_sem, out_sem):
    into = [pltpu.make_async_copy(packed.at[at], held.at[at], in_sem.at[at]) for at in range(2)]
    out_of = [
        pltpu.make_async_copy(held.at[at], out, out_sem.at[at]) for at, out in enumerate((a, w))
    ]
    for copy in into:
        copy.start()
    for copy_in, copy_out in zip(into, out_of):
        copy_in.wait()
        copy_out.start()
    for copy in out_of:
        copy.wait()


def unpack(packed):
    return pl.pallas_call(
        unpack_kernel,
        out_shape=[pltpu.HBM(packed.shape[1:], packed.dtype)] * 2,
        in_specs=[pl.BlockSpec(memory_space=pl.ANY)],
        out_specs=[pl.BlockSpec(memory_space=pl.ANY)] * 2,
        scratch_shapes=[
            pltpu.VMEM(packed.shape, packed.dtype),
            pltpu.SemaphoreType.DMA((2,)),
            pltpu.SemaphoreType.DMA((2,)),
        ],
        compiler_params=pltpu.CompilerParams(vmem_limit_bytes=LIMIT),
        cost_estimate=pl.CostEstimate(flops=0, bytes_accessed=4 * packed.size, transcendentals=0),
        name="unpack",
    )(packed)


def reorder_kernel(count, order_ref, packed, w_12, *refs):
    out, held, in_sem, out_sem = refs
    into = [
        pltpu.make_async_copy(source, held.at[at], in_sem.at[at])
        for at, source in enumerate((packed.at[0], w_12.at[0], w_12.at[1], packed.at[1]))
    ]
    out_of = [
        pltpu.make_async_copy(
            held.at[order_ref[at]], out if count == 1 else out.at[at], out_sem.at[at]
        )
        for at in range(count)
    ]
    for copy in into:
        copy.start()
    for copy in into:
        copy.wait()
    for copy in out_of:
        copy.start()
    for copy in out_of:
        copy.wait()


def reorder(order, packed, w_12):
    shape, count = packed.shape[1:], order.shape[0]
    return pl.pallas_call(
        functools.partial(reorder_kernel, count),
        out_shape=pltpu.HBM(shape if count == 1 else (count,) + shape, packed.dtype),
        in_specs=[pl.BlockSpec(memory_space=pltpu.SMEM)]
        + [pl.BlockSpec(memory_space=pl.ANY)] * 2,
        out_specs=pl.BlockSpec(memory_space=pl.ANY),
        scratch_shapes=[
            pltpu.VMEM((4,) + shape, packed.dtype),
            pltpu.SemaphoreType.DMA((4,)),
            pltpu.SemaphoreType.DMA((count,)),
        ],
        compiler_params=pltpu.CompilerParams(vmem_limit_bytes=LIMIT),
        cost_estimate=pl.CostEstimate(flops=0, bytes_accessed=8 * packed.size, transcendentals=0),
        name="reorder",
    )(order, packed, *far([w_12]))


def far(arrays):
    return [pltpu.with_memory_space_constraint(array, pltpu.HBM) for array in arrays]


def multiply(a, right, place, out):
    tiles, rows = a.shape[0], a.shape[1] // 16
    for half in range(2):
        left = jnp.concatenate(
            [
                jnp.concatenate([a[tile, pl.ds(block * rows, rows)] for tile in range(tiles)], axis=1)
                for block in place[2 * half : 2 * half + 2]
            ],
            axis=0,
        )
        total = jnp.dot(left, right, preferred_element_type=jnp.float32)
        for at in range(2):
            out[2 * half + at] = total[at * rows : (at + 1) * rows].astype(out.dtype)


def stack_product_kernel(places, a_at, w_at, choice_ref, *refs):
    stack_ref, *outs, w, a_sem, w_sem = refs[-7:]
    tiles, _, columns = w.shape
    columns //= len(w_at[0])
    rows = stack_ref.shape[1] // 16

    def pick(at):
        ref, index = at
        return refs[ref] if index is None else refs[ref].at[index]

    def w_copy(at, choice):
        return pltpu.make_async_copy(
            pick(w_at[choice][at]), w.at[:, :, pl.ds(at * columns, columns)], w_sem.at[at]
        )

    def a_copy(at):
        return pltpu.make_async_copy(
            pick(a_at[at]), stack_ref.at[:, pl.ds(at * rows, rows)], a_sem.at[at]
        )

    for at in range(len(w_at[0])):
        for choice in range(len(w_at)):

            @pl.when(choice_ref[0] == choice)
            def _():
                w_copy(at, choice).start()

    for group in (1, 2, 3, 0):
        for at in places[group]:
            a_copy(at).start()
    for at in range(len(w_at[0])):
        w_copy(at, 0).wait()
    right = w[...].reshape(tiles * LANES, len(w_at[0]) * columns)
    for group in (1, 2, 3):
        for at in places[group]:
            a_copy(at).wait()
        multiply(stack_ref, right, places[group], outs[group - 1])
    for at in places[0]:
        a_copy(at).wait()


def stack_product(choice, places, a_blocks, w_choices):
    arrays = []

    def at(block):
        array, index = block
        for known, other in enumerate(arrays):
            if other is array:
                return known, index
        arrays.append(array)
        return len(arrays) - 1, index

    a_at = [at(block) for block in a_blocks]
    w_at = [[at(block) for block in blocks] for blocks in w_choices]
    tiles, rows, _ = a_blocks[0][0].shape
    wide = len(w_choices[0]) * w_choices[0][0][0].shape[-1]
    return pl.pallas_call(
        functools.partial(stack_product_kernel, places, a_at, w_at),
        out_shape=[pltpu.VMEM((tiles, 16 * rows, LANES), jnp.bfloat16)]
        + [jax.ShapeDtypeStruct((4, rows, wide), jnp.bfloat16)] * 3,
        in_specs=[pl.BlockSpec(memory_space=pltpu.SMEM)]
        + [pl.BlockSpec(memory_space=pl.ANY)] * len(arrays),
        out_specs=[pl.BlockSpec(memory_space=pltpu.VMEM)] * 4,
        scratch_shapes=[
            pltpu.VMEM((tiles, LANES, wide), jnp.bfloat16),
            pltpu.SemaphoreType.DMA((16,)),
            pltpu.SemaphoreType.DMA((len(w_at[0]),)),
        ],
        compiler_params=pltpu.CompilerParams(vmem_limit_bytes=LIMIT),
        cost_estimate=pl.CostEstimate(
            flops=24 * rows * tiles * LANES * wide,
            bytes_accessed=2 * tiles * LANES * (16 * rows + wide),
            transcendentals=0,
        ),
        name="stack_product",
    )(choice, *arrays)


def product_kernel(places, w_at, choice_ref, a, *refs):
    groups, wide = len(places), len(w_at[0])
    outs, (w, w_sem) = refs[-2 - groups : -2], refs[-2:]
    tiles, _, columns = w.shape
    columns //= wide

    def pick(at):
        ref, index = at
        return refs[ref] if index is None else refs[ref].at[index]

    def w_copy(at, choice):
        return pltpu.make_async_copy(
            pick(w_at[choice][at]), w.at[:, :, pl.ds(at * columns, columns)], w_sem.at[at]
        )

    for at in range(wide):
        for choice in range(len(w_at)):

            @pl.when(choice_ref[0] == choice)
            def _():
                w_copy(at, choice).start()

    for at in range(wide):
        w_copy(at, 0).wait()
    right = w[...].reshape(tiles * LANES, wide * columns)
    for place, out in zip(places, outs):
        multiply(a, right, place, out)


def product(choice, groups, places, rows_stack, w_choices, after=()):
    arrays = []

    def at(block):
        array, index = block
        for known, other in enumerate(arrays):
            if other is array:
                return known, index
        arrays.append(array)
        return len(arrays) - 1, index

    w_at = [[at(block) for block in blocks] for blocks in w_choices]
    tiles, rows, _ = rows_stack.shape
    rows //= 16
    columns = w_choices[-1][0][0].shape[-1]
    wide = len(w_choices[0])
    shape = (4, rows, wide * columns)
    count = len(arrays) + len(after)
    return pl.pallas_call(
        functools.partial(product_kernel, [places[group] for group in groups], w_at),
        out_shape=[
            jax.ShapeDtypeStruct(shape, jnp.float32 if group == 0 else jnp.bfloat16)
            for group in groups
        ],
        in_specs=[
            pl.BlockSpec(memory_space=pltpu.SMEM),
            pl.BlockSpec(memory_space=pltpu.VMEM),
        ]
        + [pl.BlockSpec(memory_space=pl.ANY)] * count,
        out_specs=[pl.BlockSpec(memory_space=pltpu.VMEM)] * len(groups),
        scratch_shapes=[
            pltpu.VMEM((tiles, LANES, wide * columns), jnp.bfloat16),
            pltpu.SemaphoreType.DMA((wide,)),
        ],
        compiler_params=pltpu.CompilerParams(vmem_limit_bytes=LIMIT),
        cost_estimate=pl.CostEstimate(
            flops=8 * len(groups) * rows * tiles * LANES * wide * columns,
            bytes_accessed=2 * tiles * LANES * (4 * len(groups) * rows + wide * columns),
            transcendentals=0,
        ),
        name="product",
    )(choice, pltpu.with_memory_space_constraint(rows_stack, pltpu.VMEM), *arrays, *after)


def add_kernel(kinds, *refs):
    outs, first = refs[-4:], 0
    for kind, relative in enumerate(kinds):
        own, *others = refs[4 * kind : 4 * kind + 4]
        blocks_wide = own.shape[2] // LANES
        for piece in range(4):
            for at in range(blocks_wide):
                total = own[piece, :, pl.ds(at * LANES, LANES)]
                for step, ref in zip((3, 1, 2), others):
                    source = at ^ step if relative else at
                    total += ref[piece, :, pl.ds(source * LANES, LANES)].astype(jnp.float32)
                outs[piece][:, pl.ds((first + at) * LANES, LANES)] = total.astype(jnp.bfloat16)
        first += blocks_wide


def add(terms, kinds, after=()):
    rows = terms[0][0].shape[1]
    columns = sum(own.shape[2] for own, *_ in terms)
    arrays = [array for group in terms for array in group]
    return pl.pallas_call(
        functools.partial(add_kernel, kinds),
        out_shape=[jax.ShapeDtypeStruct((rows, columns), jnp.bfloat16)] * 4,
        in_specs=[pl.BlockSpec(memory_space=pltpu.VMEM)] * len(arrays)
        + [pl.BlockSpec(memory_space=pl.ANY)] * len(after),
        out_specs=[pl.BlockSpec(memory_space=pltpu.VMEM)] * 4,
        compiler_params=pltpu.CompilerParams(vmem_limit_bytes=LIMIT),
        cost_estimate=pl.CostEstimate(
            flops=12 * rows * columns, bytes_accessed=48 * rows * columns, transcendentals=0
        ),
        name="add",
    )(*arrays, *after)


def assemble_kernel(groups, place_ref, *refs):
    out = refs[-1]
    for ref, (fixed, parts) in zip(refs, groups):
        for at, (half, block) in enumerate(parts):
            index = fixed | (half << 3) | (block << 1)
            to = pl.multiple_of((place_ref[half] ^ index) * LANES, LANES)
            out[:, pl.ds(to, LANES)] = ref[:, pl.ds(at * LANES, LANES)]


def assemble(place, pieces):
    arrays = [piece[0] for piece in pieces]
    rows = arrays[0].shape[0]
    columns = sum(array.shape[1] for array in arrays)
    return pl.pallas_call(
        functools.partial(assemble_kernel, [piece[1:] for piece in pieces]),
        out_shape=jax.ShapeDtypeStruct((rows, columns), jnp.bfloat16),
        in_specs=[pl.BlockSpec(memory_space=pltpu.SMEM)]
        + [pl.BlockSpec(memory_space=pltpu.VMEM)] * len(arrays),
        out_specs=pl.BlockSpec(memory_space=pltpu.VMEM),
        compiler_params=pltpu.CompilerParams(vmem_limit_bytes=LIMIT),
        name="assemble",
    )(place, *arrays)


def blocks(gate_pre, up_pre, down_weight):
    n = lax.axis_size("fsdp")
    me = lax.axis_index("fsdp")
    plane = (me // PLANE) % 4
    z_low, z_high = (me // PAIR) % 2, me // (2 * PAIR)
    at_plane = plane.astype(jnp.int32).reshape(1)
    inputs = [
        pltpu.with_memory_space_constraint(array, pltpu.HBM)
        for array in (gate_pre, up_pre, down_weight)
    ]

    def send(array, perm):
        return lax.ppermute(array, "fsdp", perm=perm)

    def to_mid(array):
        return send(array, along_z(n, [(1, 2), (2, 1)]))

    def to_next(array):
        return send(array, along_z(n, [(1, 0), (3, 1), (0, 2), (2, 3)]))

    def to_core(array):
        return send(array, flip(n, CORE))

    def to_pair(array):
        return send(array, flip(n, PAIR))

    packed_1, packed_2 = pack(at_plane, (1, 2), *inputs)
    a_0, w_0 = pack(at_plane, (0,), *inputs, after=(packed_1,))
    pair_0, mid_0, next_0 = to_pair(a_0), to_mid(w_0), to_next(w_0)
    got_1 = send(packed_1, flip(n, PLANE))
    got_2 = send(packed_2, flip(n, 2 * PLANE))

    (packed_3,) = pack(at_plane, (3,), *inputs, after=(pair_0,))
    packed_3, got_1, got_2 = lax.optimization_barrier((packed_3, got_1, got_2))
    got_3 = send(packed_3, flip(n, 3 * PLANE))
    a_12, w_12 = unpack_pair(got_1, got_2, after=(pair_0,))
    pair_12, mid_12 = to_pair(a_12), to_mid(w_12)
    pair_0, mid_0, next_0 = lax.optimization_barrier((pair_0, mid_0, next_0))
    core_0, core_pair_0 = to_core(a_0), to_core(pair_0)

    order = jnp.array([[1, 2, 3], [1, 3, 2], [2, 3, 1], [3, 2, 1]], jnp.int32)[plane]
    got_3, core_0, core_pair_0 = lax.optimization_barrier((got_3, core_0, core_pair_0))
    a_3, w_3 = unpack(got_3)
    pair_3 = to_pair(a_3)
    a_12, pair_12, a_3 = lax.optimization_barrier((a_12, pair_12, a_3))
    a_12, pair_12, mid_12, got_3 = lax.optimization_barrier((a_12, pair_12, mid_12, got_3))
    core_12, core_pair_12 = to_core(a_12), to_core(pair_12)
    ordered_12 = reorder(order[:2], got_3, w_12)
    mid_3 = to_mid(w_3)
    ordered_12, pair_3, mid_3, mid_12 = lax.optimization_barrier(
        (ordered_12, pair_3, mid_3, mid_12)
    )
    next_12 = to_next(ordered_12)
    core_3, core_pair_3 = to_core(a_3), to_core(pair_3)

    a_0, w_0, a_12, w_12, a_3, w_3 = far([a_0, w_0, a_12, w_12, a_3, w_3])
    mid_0, mid_12, mid_3, core_12, core_pair_12 = far([mid_0, mid_12, mid_3, core_12, core_pair_12])
    a_blocks = [(block, None) for block in (a_0, pair_0, core_0, core_pair_0)]
    for block in (a_12, pair_12, core_12, core_pair_12):
        a_blocks += [(block, 0), (block, 1)]
    a_blocks += [(block, None) for block in (a_3, pair_3, core_3, core_pair_3)]
    places = [(0, 2, 1, 3), (4, 8, 6, 10), (5, 9, 7, 11), (12, 14, 13, 15)]
    w_own = [(w_0, None), (w_12, 0), (w_12, 1), (w_3, None)]
    w_mid = [(mid_0, None), (mid_12, 0), (mid_12, 1), (mid_3, None)]
    mid = (z_low ^ z_high).astype(jnp.int32).reshape(1)

    def totals_of(choice, w_choices, calls, after=()):
        totals = {}
        for groups in calls:
            outs = product(choice, groups, places, rows_stack, w_choices, after)
            totals.update(zip(groups, outs))
            after = (outs[0],)
        return [totals[group] for group in sorted(totals)]

    def across_plane(totals):
        return [send(totals[step], flip(n, step * PLANE)) for step in (3, 1, 2)]

    pieces = []

    def spread(terms, kinds, parts, after=()):
        summed = add(terms, kinds, after)
        for piece in range(4):
            mask = (piece >> 1) * PAIR + (piece & 1) * CORE
            block = send(summed[piece], flip(n, mask)) if mask else summed[piece]
            pieces.append((block, ((piece >> 1) << 4) | (piece & 1), parts))

    rows_stack, *own = stack_product(mid, places, a_blocks, [w_own, w_mid])
    own = totals_of(mid, [w_own, w_mid], ([0],), (own[0],)) + own
    own[1], got_3 = lax.optimization_barrier((own[1], got_3))
    ordered_3 = reorder(order[2:], got_3, w_12)
    next_3 = to_next(ordered_3)
    own_sums = across_plane(own)
    first, one, two, three = (next_0, None), (next_12, 0), (next_12, 1), (next_3, None)
    w_low = [[first, one], [one, first], [one, two], [one, two]]
    w_high = [[two, three], [two, three], [first, three], [three, first]]
    low = totals_of(at_plane, w_low, ([3, 1, 2, 0],), (own[0],))
    low[1], low[2], low[3], *own_sums = lax.optimization_barrier((*low[1:], *own_sums))
    low_sums = across_plane(low)
    high = totals_of(at_plane, w_high, ([3, 1, 2], [0]), (low[0],))
    high[1], high[2], high[3], *low_sums = lax.optimization_barrier((*high[1:], *low_sums))
    high_sums = across_plane(high)
    spread(
        [(own[0], *own_sums), (low[0], *low_sums)],
        (True, False),
        [(0, 0), (0, 1), (0, 2), (0, 3), (1, 0), (1, 1)],
        (high[0],),
    )
    spread([(high[0], *high_sums)], (False,), [(1, 2), (1, 3)])
    across = z_low * 16 + z_high * 8 + me % 2
    place = jnp.stack([across + plane * 2, across]).astype(jnp.int32)
    return assemble(place, pieces)


def shards(gate_pre, up_pre, down_weight):
    hidden = silu_product(gate_pre, up_pre)
    terms = jnp.dot(
        hidden,
        lax.all_gather(down_weight, "fsdp", axis=1, tiled=True),
        preferred_element_type=jnp.float32,
    )
    totals = lax.psum(terms, "tp")
    share = totals.shape[1] // lax.axis_size("tp")
    result = lax.dynamic_slice_in_dim(totals, lax.axis_index("tp") * share, share, 1)
    return result.astype(jnp.bfloat16)


def solution(mesh):
    in_blocks = mesh.shape["tp"] == 1 and mesh.shape["fsdp"] == 4 * PAIR
    return jax.shard_map(
        blocks if in_blocks else shards,
        mesh=mesh,
        in_specs=(P("fsdp", "tp"), P("fsdp", "tp"), P("tp", "fsdp")),
        out_specs=P("fsdp", "tp"),
        check_vma=False,
    )
```
